32 devices in a mesh: dp: 16 (over z, y, x), mp: 2 (over core).
Axes of the slice: x: 2, y: 2, z: 4, core: 2. Of those that a mesh axis runs over, the one named last changes fastest.
Arguments:
- media_feats: bfloat16 [2, 8192, 1536], P(None, ('dp', 'mp')), may hold values from -6 to 6
- latents: bfloat16 [2, 8192, 1536], P(None, ('dp', 'mp')), may hold values from -6 to 6
- patch_counts: int32 [2, 128], P(None, ('dp', 'mp')), may hold values from 1 to 253, as said below
- cotangent: bfloat16 [2, 8192, 1536], P(None, ('dp', 'mp')), may hold values from -6 to 6
- query_weight: bfloat16 [1536, 1536], replicated, may hold values from -0.15625 to 0.15625
- key_weight: bfloat16 [1536, 1536], replicated, may hold values from -0.15625 to 0.15625
- value_weight: bfloat16 [1536, 1536], replicated, may hold values from -0.15625 to 0.15625
- out_weight: bfloat16 [1536, 1536], replicated, may hold values from -0.625 to 0.625
- up_weight: bfloat16 [1536, 6144], P(None, 'mp'), may hold values from -0.15625 to 0.15625
- down_weight: bfloat16 [6144, 1536], P('mp'), may hold values from -0.078125 to 0.078125
- media_gain: float32 [1536], replicated, may hold values from 0.5 to 1.5
- media_shift: float32 [1536], replicated, may hold values from -3 to 3
- latent_gain: float32 [1536], replicated, may hold values from 0.5 to 1.5
- latent_shift: float32 [1536], replicated, may hold values from -3 to 3
- feed_gain: float32 [1536], replicated, may hold values from 0.5 to 1.5
- feed_shift: float32 [1536], replicated, may hold values from -3 to 3
Outputs:
- latents_out: bfloat16 [2, 8192, 1536], P(None, ('dp', 'mp'))
- grad_latents: float32 [2, 8192, 1536], P(None, ('dp', 'mp'))
- grad_media: float32 [2, 8192, 1536], P(None, ('dp', 'mp'))
- grad_query_weight: float32 [1536, 1536], P(('dp', 'mp'))
- grad_key_weight: float32 [1536, 1536], P(('dp', 'mp'))
- grad_value_weight: float32 [1536, 1536], P(('dp', 'mp'))
- grad_out_weight: float32 [1536, 1536], P(None, ('dp', 'mp'))
- grad_up_weight: float32 [1536, 6144], P('dp', 'mp')
- grad_down_weight: float32 [6144, 1536], P('mp', 'dp')
- grad_media_gain: float32 [1536], P(('dp', 'mp'))
- grad_media_shift: float32 [1536], P(('dp', 'mp'))
- grad_latent_gain: float32 [1536], P(('dp', 'mp'))
- grad_latent_shift: float32 [1536], P(('dp', 'mp'))
- grad_feed_gain: float32 [1536], P(('dp', 'mp'))
- grad_feed_shift: float32 [1536], P(('dp', 'mp'))
The draws below stay inside these ranges and needn't reach their ends.
Inputs may be any that keep to these rules, and one draw needn't show every extreme that they name: `patch_counts`: entries 4 * k to 4 * k + 3 of a micro-batch are the images of one block of 256 patch rows; their counts sum to at most 256, exactly 256 in some block, and their patches fill the block's rows in order from its start. Some image has 253 patch rows.
All inputs are finite; a program needn't handle non-finite values.
Results may differ from the reference program's by a relative error of at most 0.014.
Values may be sent and summed in bfloat16 or wider, within the bound.
No kernel may reach another device: no remote copies, remote signals or barrier semaphores. Data moves between devices by JAX's collectives and lax.ppermute only.
A program may use at most 256 MiB of HBM per device.

```python
from functools import partial
import jax
import jax.numpy as jnp
from jax import lax

D = 1536
HEADS = 16
FF = 6144
LAT_IMG = 64
HEAD_DIM = 96
IMG_MB = 4
PATCH_MB = 256
MICRO = 2
IMAGES = 128
LATS = 8192
PATCHES = 8192


def draw_patch_counts(key, part):
    blocks = MICRO * IMAGES // IMG_MB
    level_key, load_key = jax.random.split(jax.random.fold_in(key, 17), 2)
    levels = jax.random.randint(level_key, (blocks, IMG_MB), 0, 4)
    weight_table = jnp.array([1, 2, 4, 8], dtype=jnp.int32)
    weights = weight_table[levels]
    loads = jax.random.randint(load_key, (blocks,), 1, 5)
    loads = loads.at[0].set(4)
    totals = PATCH_MB * loads // 4
    weight_sum = jnp.sum(weights, -1)
    shares = jnp.maximum(totals[:, None] * weights // weight_sum[:, None], 1)
    leading = shares[:, :-1]
    closing = totals - jnp.sum(leading, -1)
    counts = jnp.concatenate([leading, closing[:, None]], -1)
    slots = jnp.arange(IMG_MB, dtype=jnp.int32)
    first_block = jnp.where(slots == IMG_MB - 1, PATCH_MB - IMG_MB + 1, 1).astype(jnp.int32)
    counts = counts.at[0].set(first_block)
    return counts.reshape(MICRO, IMAGES).astype(jnp.int32)


def raised(values, key, source, target, parts, factor):
    def block_of(axis_at):
        return (jnp.arange(values.shape[axis_at]) // (values.shape[axis_at] // parts)).reshape((-1,) + (1,) * (values.ndim - 1 - axis_at))

    one_side = jax.random.permutation(key, parts)[block_of(target)]
    other_side = (block_of(target) + parts // 2) % parts
    return jnp.where((block_of(source) == one_side) | (block_of(source) == other_side), factor * values, values)


def steps_of(stream_key, extent, cuts, low, top_value):
    def one(dim, shards_of):
        steps = jax.random.uniform(jax.random.fold_in(jax.random.fold_in(stream_key, 6), dim), (shards_of,), jnp.float32, low / len(cuts), top_value / len(cuts))
        return jnp.repeat(jnp.exp(steps), extent[dim] // shards_of).reshape((-1,) + (1,) * (len(extent) - dim - 1))

    factor_of = one(*cuts[0])
    for cut in cuts[1:]:
        factor_of = factor_of * one(*cut)
    return factor_of


def normal_values(rng, extent, width, most, shards=(), kind=jnp.bfloat16):
    values = jax.random.normal(rng, extent, jnp.float32) * width
    if len(shards) > 0:
        values = steps_of(rng, extent, shards, -0.22, 0.18) * values
    return jnp.clip(values, min=-most, max=most).astype(kind)


def gaussian_with(key, shape, spread, bound, pieces, heavy, kind=jnp.bfloat16):
    values = spread * jax.random.normal(key, shape, jnp.float32)
    if pieces:
        values = values * steps_of(key, shape, pieces, -0.22, 0.18)
    return jnp.clip(raised(values, jax.random.fold_in(key, 3), *heavy), -bound, bound).astype(kind)


def setup_inputs(seed: int = 0) -> dict:
    keys = jax.random.split(jax.random.key(seed), 17)
    media_feats = normal_values(keys[0], (MICRO, PATCHES, D), 1.0, 6.0, ((1, 32),))
    latents = normal_values(keys[1], (MICRO, LATS, D), 1.0, 6.0, ((1, 32),))
    patch_counts = draw_patch_counts(jax.random.fold_in(keys[16], 71), 0)
    cotangent = gaussian_with(keys[3], (MICRO, LATS, D), 1.0, 6.0, ((1, 32),), (1, 2, 32, 2.75))
    query_weight = normal_values(keys[4], (D, D), D ** -0.5, 0.15625)
    key_weight = normal_values(keys[5], (D, D), D ** -0.5, 0.15625)
    value_weight = normal_values(keys[6], (D, D), D ** -0.5, 0.15625)
    out_weight = normal_values(keys[7], (D, D), (D // 16) ** -0.5, 0.625)
    up_weight = normal_values(keys[8], (D, FF), D ** -0.5, 0.15625, ((1, 2),))
    down_weight = normal_values(keys[9], (FF, D), FF ** -0.5, 0.078125, ((0, 2),))
    media_gain = jnp.clip(1.0 + 0.1 * jax.random.normal(keys[10], (D,), jnp.float32), 0.5, 1.5)
    media_shift = normal_values(keys[11], (D,), 0.5, 3.0, (), jnp.float32)
    latent_gain = jnp.clip(1.0 + 0.1 * jax.random.normal(keys[12], (D,), jnp.float32), 0.5, 1.5)
    latent_shift = normal_values(keys[13], (D,), 0.5, 3.0, (), jnp.float32)
    feed_gain = jnp.clip(1.0 + 0.1 * jax.random.normal(keys[14], (D,), jnp.float32), 0.5, 1.5)
    feed_shift = normal_values(keys[15], (D,), 0.5, 3.0, (), jnp.float32)
    return {"media_feats": media_feats, "latents": latents, "patch_counts": patch_counts, "cotangent": cotangent, "query_weight": query_weight, "key_weight": key_weight, "value_weight": value_weight, "out_weight": out_weight, "up_weight": up_weight, "down_weight": down_weight, "media_gain": media_gain, "media_shift": media_shift, "latent_gain": latent_gain, "latent_shift": latent_shift, "feed_gain": feed_gain, "feed_shift": feed_shift}


@jax.custom_vjp
def low(v):
    return lax.optimization_barrier(v.astype(jnp.bfloat16)).astype(jnp.float32)

@jax.custom_vjp
def low_back(v):
    return v

def low_keep(v):
    return (low(v), None)

def low_pass(kept, grad):
    return (grad,)

def back_keep(v):
    return (v, None)

def back_low(kept, grad):
    return (low(grad),)
low.defvjp(low_keep, low_pass)
low_back.defvjp(back_keep, back_low)
EPSILON = 1e-05
MASKED_SCORE = -1e+30

def product(left_side, right_side):
    return jnp.dot(left_side, right_side, precision=lax.Precision.HIGHEST)

def normalize(values, gain_vec, shift_vec):
    row_mean = lax.optimization_barrier(jnp.mean(values, -1, keepdims=True))
    centred = values - row_mean
    variance = lax.optimization_barrier(jnp.mean(centred * centred, -1, keepdims=True))
    return centred * lax.rsqrt(variance + EPSILON) * gain_vec + shift_vec

def image_mask(block_counts, query_rows, patch_rows):
    image_ends = jnp.cumsum(block_counts).astype(jnp.int32)
    positions = jnp.arange(patch_rows, dtype=jnp.int32)
    media_image = lax.optimization_barrier(jnp.sum((positions[:, None] >= image_ends[None, :]).astype(jnp.int32), 1))
    latent_image = jnp.arange(query_rows, dtype=jnp.int32) // LAT_IMG
    key_image = jnp.concatenate([media_image, latent_image])
    return latent_image[:, None] == key_image[None, :]

def attend_block(inputs):
    queries, key_media, value_media, key_latent, value_latent, block_counts = inputs
    query_rows = queries.shape[0]
    patch_rows = key_media.shape[0]
    mask_table = image_mask(block_counts, query_rows, patch_rows)
    key_rows = jnp.concatenate([key_media, key_latent]).reshape(-1, HEADS, HEAD_DIM)
    value_rows = jnp.concatenate([value_media, value_latent]).reshape(-1, HEADS, HEAD_DIM)
    query_heads = queries.reshape(query_rows, HEADS, HEAD_DIM)
    scores = jnp.einsum('qhd,khd->hqk', query_heads, key_rows, precision=lax.Precision.HIGHEST) * HEAD_DIM ** (-0.5)
    scores = low_back(scores)
    attn_probs = low(jax.nn.softmax(jnp.where(mask_table[None], scores, MASKED_SCORE), axis=-1))
    mixed_out = jnp.einsum('hqk,khd->qhd', attn_probs, value_rows, precision=lax.Precision.HIGHEST)
    return mixed_out.reshape(query_rows, D)

def layer(block_counts_all, media_feats, latents, query_weight, key_weight, value_weight, out_weight, up_weight, down_weight, media_gain, media_shift, latent_gain, latent_shift, feed_gain, feed_shift):
    media_n = low(normalize(media_feats, media_gain, media_shift))
    latent_n = low(normalize(latents, latent_gain, latent_shift))
    queries = low_back(low(product(latent_n, query_weight)))
    key_media = low_back(low(product(media_n, key_weight)))
    value_media = low_back(low(product(media_n, value_weight)))
    key_latent = low_back(low(product(latent_n, key_weight)))
    value_latent = low_back(low(product(latent_n, value_weight)))
    blocks = media_feats.shape[0] // PATCH_MB
    query_rows = LAT_IMG * IMG_MB
    mixed_out = lax.map(jax.checkpoint(attend_block), (queries.reshape(blocks, query_rows, D), key_media.reshape(blocks, PATCH_MB, D), value_media.reshape(blocks, PATCH_MB, D), key_latent.reshape(blocks, query_rows, D), value_latent.reshape(blocks, query_rows, D), block_counts_all.reshape(blocks, IMG_MB)))
    mixed_out = low_back(low(mixed_out.reshape(-1, D)))
    residual = latents + low_back(product(mixed_out, out_weight))
    feed_in = low(normalize(residual, feed_gain, feed_shift))
    up_proj = low_back(product(feed_in, up_weight))
    hidden = low(jax.nn.gelu(up_proj, approximate=False))
    return residual + product(hidden, down_weight)

def reference(media_feats, latents, patch_counts, cotangent, query_weight, key_weight, value_weight, out_weight, up_weight, down_weight, media_gain, media_shift, latent_gain, latent_shift, feed_gain, feed_shift):
    params = tuple((argument.astype(jnp.float32) for argument in (query_weight, key_weight, value_weight, out_weight, up_weight, down_weight, media_gain, media_shift, latent_gain, latent_shift, feed_gain, feed_shift)))
    outputs = []
    latent_grads = []
    media_grads = []
    totals = None
    for micro_step in range(MICRO):
        forward = partial(layer, patch_counts[micro_step])
        result, pullback = jax.vjp(forward, media_feats[micro_step].astype(jnp.float32), latents[micro_step].astype(jnp.float32), *params)
        gradients = pullback(cotangent[micro_step].astype(jnp.float32))
        outputs.append(result.astype(jnp.bfloat16))
        media_grads.append(gradients[0])
        latent_grads.append(gradients[1])
        weight_grads = tuple(gradients[2:])
        if totals is None:
            totals = weight_grads
        else:
            totals = tuple((left_term + right_term for left_term, right_term in zip(totals, weight_grads)))
    return (jnp.stack(outputs), jnp.stack(latent_grads), jnp.stack(media_grads), totals[0], totals[1], totals[2], totals[3], totals[4], totals[5], totals[6], totals[7], totals[8], totals[9], totals[10], totals[11])
```

```python
import jax
import jax.numpy as jnp
from jax import lax
from jax.sharding import PartitionSpec as P

HEADS = 16
LAT_IMG = 64
EPSILON = 1e-05
MASKED_SCORE = -1e30
ROOT_HALF = 0.7071067811865476
DENSITY_SCALE = 0.3989422804014327
F32 = jnp.float32
BF16 = jnp.bfloat16


def normalize(values, gain_vec, shift_vec):
    row_mean = jnp.mean(values, -1, keepdims=True)
    centred = values - row_mean
    inv_scale = lax.rsqrt(jnp.mean(centred * centred, -1, keepdims=True) + EPSILON)
    scaled = centred * inv_scale
    return (scaled * gain_vec + shift_vec, scaled, inv_scale)


def normalize_back(upstream, gain_vec, scaled, inv_scale):
    weighted = upstream * gain_vec
    first_mean = jnp.mean(weighted, -1, keepdims=True)
    second_mean = jnp.mean(weighted * scaled, -1, keepdims=True)
    grad_input = inv_scale * (weighted - first_mean - scaled * second_mean)
    return (grad_input, jnp.sum(upstream * scaled, 0), jnp.sum(upstream, 0))


def dot(left, right):
    return jnp.dot(left, right, preferred_element_type=F32)


def dot_t(left, right):
    return jnp.einsum("rd,ed->re", left, right, preferred_element_type=F32)


def masked_scores(query_heads, key_heads, mask_table, scale):
    scores = jnp.einsum("qhd,khd->hqk", query_heads, key_heads, preferred_element_type=F32) * scale
    return jnp.where(mask_table[None], scores, MASKED_SCORE)


def mask_of(patch_counts, patches, latent_rows):
    images = patch_counts.shape[0]
    upto = lax.iota(jnp.int32, images)[:, None] >= lax.iota(jnp.int32, images)[None, :]
    image_ends = jnp.sum(jnp.where(upto, patch_counts[None, :], 0), 1)
    positions = lax.iota(jnp.int32, patches)
    media_image = jnp.sum((positions[:, None] >= image_ends[None, :]).astype(jnp.int32), 1)
    latent_image = lax.iota(jnp.int32, latent_rows) // LAT_IMG
    key_image = jnp.concatenate([media_image, latent_image])
    return latent_image[:, None] == key_image[None, :]


def attend(queries, keys, values, mask_table, scale):
    rows, width = queries.shape
    query_heads = queries.reshape(rows, HEADS, -1)
    key_heads = keys.reshape(keys.shape[0], HEADS, -1)
    value_heads = values.reshape(keys.shape[0], HEADS, -1)
    scores = masked_scores(query_heads, key_heads, mask_table, scale)
    row_max = jnp.max(scores, -1, keepdims=True)
    exp_scores = jnp.exp(scores - row_max)
    row_sum = jnp.sum(exp_scores, -1, keepdims=True)
    log_norm = row_max + jnp.log(row_sum)
    probs_low = (exp_scores / row_sum).astype(BF16)
    mixed = jnp.einsum("hqk,khd->qhd", probs_low, value_heads, preferred_element_type=F32)
    return mixed.reshape(rows, width).astype(BF16), log_norm


def attend_back(queries, keys, values, mask_table, scale, log_norm, grad_mixed):
    rows, width = queries.shape
    query_heads = queries.reshape(rows, HEADS, -1)
    key_heads = keys.reshape(keys.shape[0], HEADS, -1)
    value_heads = values.reshape(keys.shape[0], HEADS, -1)
    grad_heads = grad_mixed.reshape(rows, HEADS, -1)
    again = masked_scores(query_heads, key_heads, mask_table, scale)
    probs = jnp.where(mask_table[None], jnp.exp(again - log_norm), 0.0)
    probs_low = probs.astype(BF16)
    grad_values = jnp.einsum("hqk,qhd->khd", probs_low, grad_heads, preferred_element_type=F32)
    grad_probs = jnp.einsum("qhd,khd->hqk", grad_heads, value_heads, preferred_element_type=F32)
    grad_scores = probs * (grad_probs - jnp.sum(grad_probs * probs, -1, keepdims=True))
    grad_low = grad_scores.astype(BF16)
    grad_queries = jnp.einsum("hqk,khd->qhd", grad_low, key_heads, preferred_element_type=F32)
    grad_keys = jnp.einsum("hqk,qhd->khd", grad_low, query_heads, preferred_element_type=F32)
    return (
        (grad_queries * scale).reshape(rows, width).astype(BF16),
        (grad_keys * scale).reshape(-1, width).astype(BF16),
        grad_values.reshape(-1, width).astype(BF16),
    )


def bit_orders(count):
    bits = count.bit_length() - 1
    if bits == 4:
        return [(0, 1, 2, 3), (1, 0, 2, 3), (2, 3, 0, 1)]
    plain = tuple(range(bits))
    third = bits // 3
    return [plain[s:] + plain[:s] for s in (0, third, 2 * third)]


def sided(value, bit, bits, side):
    place = bits.index(bit)
    shape = value.shape
    outer = 1 << place
    parts = value.reshape((outer, 2, shape[0] // (2 * outer)) + shape[1:])
    return lax.dynamic_index_in_dim(parts, side, 1, keepdims=False).reshape((shape[0] // 2,) + shape[1:])


def swap_mp(value, size):
    return lax.ppermute(value, "mp", [(i, i ^ 1) for i in range(size)])


def steps_of(order, with_mp):
    if with_mp:
        return [("mp", 0)] + [("dp", bit + 1) for bit in order]
    return [("dp", bit) for bit in order]


def exchange(value, axis, bit, shifted, sizes):
    flip = 1 if axis == "mp" else 1 << (bit - shifted)
    return lax.ppermute(value, axis, [(i, i ^ flip) for i in range(sizes[axis])])


def halving(terms, bits, steps, block_index, shifted, sizes):
    for axis, bit in steps:
        mine = (block_index >> bit) & 1
        rear = [sided(t, bit, bits, 1 - mine) for t in terms]
        sent = rear[0] if len(rear) == 1 else sum(t.astype(F32) for t in rear).astype(rear[0].dtype)
        got = exchange(sent, axis, bit, shifted, sizes)
        terms = [sided(t, bit, bits, mine) for t in terms] + [got]
        bits = [b for b in bits if b != bit]
    return sum(t[0].astype(F32) for t in terms)


def scatter_product(left_t, right, cuts, orders, block_index, with_mp, sizes):
    blocks = sizes["dp"] * (sizes["mp"] if with_mp else 1)
    width = left_t.shape[0]
    shifted = 1 if with_mp else 0
    all_bits = list(range(blocks.bit_length() - 1))[::-1]
    parted = left_t.reshape(blocks, width // blocks, -1)
    pieces = []
    start = 0
    for cut, order in zip(cuts, orders):
        part = right[:, start : start + cut]
        steps = steps_of(order, with_mp)
        axis, bit = steps[0]
        mine = (block_index >> bit) & 1

        def half(side):
            rows = sided(parted, bit, all_bits, side).reshape(width // 2, -1)
            return dot(rows, part).astype(BF16).reshape(blocks // 2, width // blocks, cut)

        got = exchange(half(1 - mine), axis, bit, shifted, sizes)
        left_bits = [b for b in all_bits if b != bit]
        pieces.append(halving([half(mine), got], left_bits, steps[1:], block_index, shifted, sizes))
        start += cut
    return jnp.concatenate(pieces, 1)


def small_sums(vectors, block_index, order, sizes):
    blocks = sizes["dp"] * sizes["mp"]
    count = len(vectors)
    stacked = jnp.stack(vectors).reshape(count, blocks, -1).transpose(1, 0, 2)
    all_bits = list(range(blocks.bit_length() - 1))[::-1]
    share = halving([stacked], all_bits, steps_of(order, True), block_index, 1, sizes)
    return [share[i] for i in range(count)]


def cut_widths(width, shares):
    unit = 128
    total = width // unit
    whole = sum(shares)
    first = total * shares[0] // whole
    second = total * (shares[0] + shares[1]) // whole - first
    return [first * unit, second * unit, (total - first - second) * unit]


def build(dp_size, mp_size):
    orders = bit_orders(dp_size)
    sizes = {"dp": dp_size, "mp": mp_size}

    def local(
        media_feats,
        latents,
        patch_counts,
        cotangent,
        query_weight,
        key_weight,
        value_weight,
        out_weight,
        up_weight,
        down_weight,
        media_gain,
        media_shift,
        latent_gain,
        latent_shift,
        feed_gain,
        feed_shift,
    ):
        micro, patches, width = media_feats.shape
        latent_rows = latents.shape[1]
        scale = (width // HEADS) ** (-0.5)
        dp_index = lax.axis_index("dp").astype(jnp.int32)
        flat_index = dp_index * mp_size + lax.axis_index("mp").astype(jnp.int32)
        ff_cuts = cut_widths(up_weight.shape[1], (9, 9, 6))
        at_cuts = [cut_widths(width, (5, 4, 3)), cut_widths(width, (4, 5, 3))]

        grad_own = cotangent.reshape(-1, width)
        grad_other = swap_mp(grad_own, mp_size)
        media_full = media_feats.reshape(-1, width).astype(F32)
        latents_full = latents.reshape(-1, width).astype(F32)
        media_n, media_hat, media_inv = normalize(media_full, media_gain, media_shift)
        latent_n, latent_hat, latent_inv = normalize(latents_full, latent_gain, latent_shift)
        media_low = media_n.astype(BF16)
        latent_low = latent_n.astype(BF16)
        both_low = jnp.concatenate([media_low, latent_low])
        queries = dot(latent_low, query_weight).astype(BF16)
        key_both = dot(both_low, key_weight).astype(BF16)
        value_both = dot(both_low, value_weight).astype(BF16)
        media_rows = micro * patches

        def keys_of(both, m):
            return jnp.concatenate(
                [
                    both[m * patches : (m + 1) * patches],
                    both[media_rows + m * latent_rows : media_rows + (m + 1) * latent_rows],
                ]
            )

        masks, mixes, norms = [], [], []
        for m in range(micro):
            mask = mask_of(patch_counts[m], patches, latent_rows)
            mixed, log_norm = attend(
                queries[m * latent_rows : (m + 1) * latent_rows],
                keys_of(key_both, m),
                keys_of(value_both, m),
                mask,
                scale,
            )
            masks.append(mask)
            mixes.append(mixed)
            norms.append(log_norm)
        mixed_low = jnp.concatenate(mixes)
        residual = latents_full + dot(mixed_low, out_weight)
        feed_in, feed_hat, feed_inv = normalize(residual, feed_gain, feed_shift)
        feed_own = feed_in.astype(BF16)
        feed_other = swap_mp(feed_own, mp_size)

        feed_all = jnp.concatenate([feed_own, feed_other])
        grad_all = jnp.concatenate([grad_own, grad_other])
        own = feed_own.shape[0]
        up_proj = dot(feed_all, up_weight)
        normal_cdf = 0.5 * (1.0 + lax.erf(up_proj * ROOT_HALF))
        normal_pdf = jnp.exp(-0.5 * up_proj * up_proj) * DENSITY_SCALE
        hidden = (up_proj * normal_cdf).astype(BF16)
        slope = (normal_cdf + up_proj * normal_pdf).astype(BF16)

        grad_down_t = scatter_product(grad_all.T, hidden, ff_cuts, orders, dp_index, False, sizes)

        grad_up = (dot_t(grad_all, down_weight) * slope.astype(F32)).astype(BF16)
        grad_up_w = scatter_product(feed_all.T, grad_up, ff_cuts, orders, dp_index, False, sizes)

        feed_back = dot_t(grad_up, up_weight)
        grad_feed_in = feed_back[:own] + swap_mp(feed_back[own:].astype(BF16), mp_size).astype(F32)
        branch = dot(hidden, down_weight)
        branch_sum = branch[:own] + swap_mp(branch[own:].astype(BF16), mp_size).astype(F32)
        result = (residual + branch_sum).astype(BF16)

        grad_feed_part, grad_feed_gain, grad_feed_shift = normalize_back(
            grad_feed_in, feed_gain, feed_hat, feed_inv
        )
        grad_residual = grad_own.astype(F32) + grad_feed_part
        grad_residual_low = grad_residual.astype(BF16)
        grad_out_t = scatter_product(grad_residual_low.T, mixed_low, at_cuts[0], orders, flat_index, True, sizes)
        grad_mixed = dot_t(grad_residual_low, out_weight).astype(BF16)

        back = [
            attend_back(
                queries[m * latent_rows : (m + 1) * latent_rows],
                keys_of(key_both, m),
                keys_of(value_both, m),
                masks[m],
                scale,
                norms[m],
                grad_mixed[m * latent_rows : (m + 1) * latent_rows],
            )
            for m in range(micro)
        ]
        grad_queries = jnp.concatenate([b[0] for b in back])
        grad_keys = jnp.concatenate([b[1][:patches] for b in back] + [b[1][patches:] for b in back])
        grad_values = jnp.concatenate([b[2][:patches] for b in back] + [b[2][patches:] for b in back])

        both_t = both_low.T
        latent_t = both_t[:, media_rows:]
        grad_key_w = scatter_product(both_t, grad_keys, at_cuts[0], orders, flat_index, True, sizes)
        grad_value_w = scatter_product(both_t, grad_values, at_cuts[1], orders, flat_index, True, sizes)
        grad_query_w = scatter_product(latent_t, grad_queries, at_cuts[1], orders, flat_index, True, sizes)

        grad_both = dot_t(grad_keys, key_weight) + dot_t(grad_values, value_weight)
        grad_latent_n = grad_both[media_rows:] + dot_t(grad_queries, query_weight)
        grad_latent_part, grad_latent_gain, grad_latent_shift = normalize_back(
            grad_latent_n, latent_gain, latent_hat, latent_inv
        )
        grad_media, grad_media_gain, grad_media_shift = normalize_back(
            grad_both[:media_rows], media_gain, media_hat, media_inv
        )
        grad_latents = grad_residual + grad_latent_part
        sums = small_sums(
            [
                grad_media_gain,
                grad_media_shift,
                grad_latent_gain,
                grad_latent_shift,
                grad_feed_gain,
                grad_feed_shift,
            ],
            flat_index,
            orders[0],
            sizes,
        )
        return (
            result.reshape(latents.shape),
            grad_latents.reshape(latents.shape),
            grad_media.reshape(media_feats.shape),
            grad_query_w,
            grad_key_w,
            grad_value_w,
            grad_out_t.T,
            grad_up_w,
            grad_down_t.T,
            *sums,
        )

    return local


def solution(mesh):
    rows = P(None, ("dp", "mp"), None)
    in_specs = (rows, rows, P(None, ("dp", "mp")), rows, P(), P(), P(), P(), P(None, "mp"), P("mp", None)) + (P(),) * 6
    first = P(("dp", "mp"), None)
    out_specs = (rows, rows, rows, first, first, first, P(None, ("dp", "mp")), P("dp", "mp"), P("mp", "dp")) + (
        P(("dp", "mp")),
    ) * 6
    local = build(mesh.shape["dp"], mesh.shape["mp"])
    return jax.shard_map(local, mesh=mesh, in_specs=in_specs, out_specs=out_specs, check_vma=False)
```

```python
import functools

import jax
import jax.numpy as jnp
from jax import lax
from jax.experimental import pallas as pl
from jax.experimental.pallas import tpu as pltpu
from jax.sharding import PartitionSpec as P

HEADS = 16
LAT_IMG = 64
EPSILON = 1e-05
MASKED_SCORE = -1e30
ROOT_HALF = 0.7071067811865476
DENSITY_SCALE = 0.3989422804014327
F32 = jnp.float32
BF16 = jnp.bfloat16
NN = (((1,), (0,)), ((), ()))
NT = (((1,), (1,)), ((), ()))
TN = (((0,), (0,)), ((), ()))
MIB = 1024 * 1024


def mm(left, right, dims=NN):
    return lax.dot_general(left, right, dims, preferred_element_type=F32)


def low_mm(left, right):
    return mm(left, right).astype(BF16)


def normalize(values, gain_vec, shift_vec):
    row_mean = jnp.mean(values, -1, keepdims=True)
    centred = values - row_mean
    inv_scale = lax.rsqrt(jnp.mean(centred * centred, -1, keepdims=True) + EPSILON)
    scaled = centred * inv_scale
    return (scaled * gain_vec + shift_vec, scaled, inv_scale)


def normalize_back(upstream, gain_vec, scaled, inv_scale):
    weighted = upstream * gain_vec
    first_mean = jnp.mean(weighted, -1, keepdims=True)
    second_mean = jnp.mean(weighted * scaled, -1, keepdims=True)
    grad_input = inv_scale * (weighted - first_mean - scaled * second_mean)
    return (grad_input, jnp.sum(upstream * scaled, 0), jnp.sum(upstream, 0))


def mask_biases(counts, step, keys, lats, pair):
    lane = lax.broadcasted_iota(jnp.int32, (1, lats), 1) // LAT_IMG
    first = jnp.zeros((1, lats), jnp.int32)
    past = jnp.zeros((1, lats), jnp.int32)
    total = jnp.int32(0)
    for i in range(counts.shape[1]):
        after = total + counts[step, i]
        first = jnp.where(lane == i, total, first)
        past = jnp.where(lane == i, after, past)
        total = after
    place = lax.broadcasted_iota(jnp.int32, (keys, lats), 0)
    media = jnp.where((place >= first) & (place < past), 0.0, MASKED_SCORE)
    key_image = lax.broadcasted_iota(jnp.int32, (pair, pair), 0) // LAT_IMG
    latent_image = lax.broadcasted_iota(jnp.int32, (pair, pair), 1) // LAT_IMG
    return media, jnp.where(key_image == latent_image, 0.0, MASKED_SCORE)


def spans(total, size):
    return [slice(start, start + size) for start in range(0, total, size)]


def attend_kernel(counts, q, k, v, mixed, norm, *, heads, dim, pair):
    scale = dim**-0.5
    lats = q.shape[0]
    bias_m, bias_l = mask_biases(counts, pl.program_id(0), k.shape[1], lats, pair)
    pairs = spans(lats, pair)
    for j in range(heads):
        c = slice(dim * j, dim * j + dim)
        qh = q[:, c]
        kl = k[1, :, c]
        vl = v[1, :, c]
        s_m = mm(k[0, :, c], qh, NT) * scale + bias_m
        s_l = jnp.concatenate([mm(kl[p], qh[p], NT) * scale + bias_l for p in pairs], 1)
        top = jnp.maximum(jnp.max(s_m, 0, keepdims=True), jnp.max(s_l, 0, keepdims=True))
        e_m = jnp.exp(s_m - top)
        e_l = jnp.exp(s_l - top)
        total = jnp.sum(e_m, 0, keepdims=True) + jnp.sum(e_l, 0, keepdims=True)
        inverse = 1.0 / total
        p_m = (e_m * inverse).astype(BF16)
        p_l = (e_l * inverse).astype(BF16)
        latent_part = jnp.concatenate([mm(p_l[:, p], vl[p], TN) for p in pairs], 0)
        mixed[:, c] = (mm(p_m, v[0, :, c], TN) + latent_part).astype(BF16)
        norm[0, 0, j : j + 1, :] = top + jnp.log(total)


def attend_back_kernel(counts, q, k, v, grad_mixed, norm, grad_q, grad_k, grad_v, *, heads, dim, pair):
    scale = dim**-0.5
    lats = q.shape[0]
    bias_m, bias_l = mask_biases(counts, pl.program_id(0), k.shape[1], lats, pair)
    pairs = spans(lats, pair)
    for j in range(heads):
        c = slice(dim * j, dim * j + dim)
        qh = q[:, c]
        km = k[0, :, c]
        kl = k[1, :, c]
        vl = v[1, :, c]
        gh = grad_mixed[:, c]
        log_norm = norm[0, 0, j : j + 1, :]
        p_m = jnp.exp(mm(km, qh, NT) * scale + bias_m - log_norm)
        s_l = jnp.concatenate([mm(kl[p], qh[p], NT) * scale + bias_l for p in pairs], 1)
        p_l = jnp.exp(s_l - log_norm)
        d_m = mm(v[0, :, c], gh, NT)
        d_l = jnp.concatenate([mm(vl[p], gh[p], NT) for p in pairs], 1)
        row_mean = jnp.sum(d_m * p_m, 0, keepdims=True) + jnp.sum(d_l * p_l, 0, keepdims=True)
        g_m = (p_m * (d_m - row_mean)).astype(BF16)
        g_l = (p_l * (d_l - row_mean)).astype(BF16)
        p_m = p_m.astype(BF16)
        p_l = p_l.astype(BF16)
        grad_v[0, :, c] = mm(p_m, gh).astype(BF16)
        grad_k[0, :, c] = (mm(g_m, qh) * scale).astype(BF16)
        for p in pairs:
            grad_v[1, p, c] = mm(p_l[:, p], gh[p]).astype(BF16)
            grad_k[1, p, c] = (mm(g_l[:, p], qh[p]) * scale).astype(BF16)
        latent_part = jnp.concatenate([mm(g_l[:, p], kl[p], TN) for p in pairs], 0)
        grad_q[:, c] = ((mm(g_m, km, TN) + latent_part) * scale).astype(BF16)


def attention_call(kernel, counts, queries, keys, values, more, outs, flops):
    micro = counts.shape[0]
    rows = queries.shape[0] // micro
    width = queries.shape[1]
    groups = 2
    heads = HEADS // groups
    group = width // groups
    one = pl.BlockSpec((rows, group), lambda m, g: (m, g))
    two = pl.BlockSpec((2, rows, group), lambda m, g: (0, m, g))
    norm = pl.BlockSpec((1, 1, heads, rows), lambda m, g: (m, g, 0, 0))
    kinds = {
        "one": (one, jax.ShapeDtypeStruct(queries.shape, BF16)),
        "two": (two, jax.ShapeDtypeStruct(keys.shape, BF16)),
        "norm": (norm, jax.ShapeDtypeStruct((micro, groups, heads, rows), F32)),
    }
    return pl.pallas_call(
        functools.partial(kernel, heads=heads, dim=width // HEADS, pair=2 * LAT_IMG),
        grid=(micro, groups),
        in_specs=[pl.BlockSpec(memory_space=pltpu.SMEM), one, two, two] + [kinds[kind][0] for kind, _ in more],
        out_specs=[kinds[kind][0] for kind in outs],
        out_shape=[kinds[kind][1] for kind in outs],
        compiler_params=pltpu.CompilerParams(vmem_limit_bytes=40 * MIB),
        cost_estimate=pl.CostEstimate(flops=flops, bytes_accessed=20 * MIB, transcendentals=0),
    )(counts, queries, keys, values, *[value for _, value in more])


def feed_kernel(feed, cot, up, down, *refs, row_step, width_step):
    grad_down, grad_up_w, hidden, grad_up = refs[-4:]
    rows, width = feed.shape
    for r in spans(rows, row_step):
        u = mm(feed[r, :], up[...])
        grad_hidden = mm(cot[r, :], down[...], NT)
        cdf = 0.5 * (1.0 + lax.erf(u * ROOT_HALF))
        pdf = jnp.exp(-0.5 * u * u) * DENSITY_SCALE
        hidden[r, :] = (u * cdf).astype(BF16)
        grad_up[r, :] = (grad_hidden * (cdf + u * pdf)).astype(BF16)
    for r in spans(width, width_step):
        grad_down[r, :] = mm(cot[:, r], hidden[...], TN).astype(BF16)
        grad_up_w[r, :] = mm(feed[:, r], grad_up[...], TN).astype(BF16)


def feed_part(feed, cot, up, down, start, tiles, tile, before):
    rows, width = feed.shape
    whole = pl.BlockSpec((rows, width), lambda t: (0, 0), pipeline_mode=pl.Buffered(1))
    weight_grad = pl.BlockSpec((width, tile), lambda t: (0, t))
    units = pl.BlockSpec((rows, tile), lambda t: (0, start + t))
    unit_shape = jax.ShapeDtypeStruct((rows, up.shape[1]), BF16)
    grad_shape = jax.ShapeDtypeStruct((width, tiles * tile), BF16)
    kept = [] if before is None else list(before)
    return pl.pallas_call(
        functools.partial(feed_kernel, row_step=rows // 2, width_step=width // 2),
        grid=(tiles,),
        in_specs=[
            whole,
            whole,
            pl.BlockSpec((width, tile), lambda t: (0, start + t)),
            pl.BlockSpec((tile, width), lambda t: (start + t, 0)),
        ]
        + [pl.BlockSpec(memory_space=pl.ANY)] * len(kept),
        out_specs=[weight_grad, weight_grad, units, units],
        out_shape=[grad_shape, grad_shape, unit_shape, unit_shape],
        input_output_aliases={4: 2, 5: 3} if kept else {},
        compiler_params=pltpu.CompilerParams(vmem_limit_bytes=60 * MIB),
        cost_estimate=pl.CostEstimate(flops=8 * rows * width * tile * tiles, bytes_accessed=16 * MIB, transcendentals=0),
    )(feed, cot, up, down, *kept)


def product_kernel(left, first, *refs, steps):
    out = refs[-1]
    step = pl.program_id(0)

    @pl.when(step < steps)
    def _():
        out[...] = mm(left[...], first[...], TN).astype(BF16)

    if len(refs) == 2:

        @pl.when(step >= steps)
        def _():
            rows = refs[0].shape[0]
            out[...] = mm(left[left.shape[0] - rows :, :], refs[0][...], TN).astype(BF16)


def product(left, first, second=None, part=0):
    rows, width = left.shape
    tile = width // 2
    steps = first.shape[1] // tile
    grid = steps + (second is not None)
    in_specs = [
        pl.BlockSpec((rows, width), lambda t: (0, 0), pipeline_mode=pl.Buffered(1)),
        pl.BlockSpec((rows, tile), lambda t: (0, jnp.minimum(t, steps - 1))),
    ]
    operands = [left, first]
    if second is not None:
        in_specs.append(pl.BlockSpec((second.shape[0], tile), lambda t: (0, part)))
        operands.append(second)
    return pl.pallas_call(
        functools.partial(product_kernel, steps=steps),
        grid=(grid,),
        in_specs=in_specs,
        out_specs=pl.BlockSpec((width, tile), lambda t: (0, t)),
        out_shape=jax.ShapeDtypeStruct((width, grid * tile), BF16),
        compiler_params=pltpu.CompilerParams(vmem_limit_bytes=40 * MIB),
        cost_estimate=pl.CostEstimate(flops=2 * rows * width * tile * grid, bytes_accessed=12 * MIB, transcendentals=0),
    )(*operands)


def bit_orders(count):
    bits = count.bit_length() - 1
    if bits == 4:
        return [(0, 1, 2, 3), (1, 0, 2, 3), (2, 3, 0, 1)]
    plain = tuple(range(bits))
    third = bits // 3
    return [plain[s:] + plain[:s] for s in (0, third, 2 * third)]


def sided(value, bit, bits, side):
    place = bits.index(bit)
    shape = value.shape
    outer = 1 << place
    parts = value.reshape((outer, 2, shape[0] // (2 * outer)) + shape[1:])
    return lax.dynamic_index_in_dim(parts, side, 1, keepdims=False).reshape((shape[0] // 2,) + shape[1:])


def swap_mp(value, size):
    return lax.ppermute(value, "mp", [(i, i ^ 1) for i in range(size)])


def steps_of(order, with_mp):
    if with_mp:
        return [("mp", 0)] + [("dp", bit + 1) for bit in order]
    return [("dp", bit) for bit in order]


def exchange(value, axis, bit, shifted, sizes):
    flip = 1 if axis == "mp" else 1 << (bit - shifted)
    return lax.ppermute(value, axis, [(i, i ^ flip) for i in range(sizes[axis])])


def halving(terms, bits, steps, block_index, shifted, sizes):
    for axis, bit in steps:
        mine = (block_index >> bit) & 1
        rear = [sided(t, bit, bits, 1 - mine) for t in terms]
        sent = rear[0] if len(rear) == 1 else sum(t.astype(F32) for t in rear).astype(rear[0].dtype)
        got = exchange(sent, axis, bit, shifted, sizes)
        terms = [sided(t, bit, bits, mine) for t in terms] + [got]
        bits = [b for b in bits if b != bit]
    return sum(t[0].astype(F32) for t in terms)


def scatter_partials(partials, order, block_index, with_mp, sizes):
    blocks = sizes["dp"] * (sizes["mp"] if with_mp else 1)
    width = partials.shape[0]
    all_bits = list(range(blocks.bit_length() - 1))[::-1]
    parted = partials.reshape(blocks, width // blocks, -1)
    return halving([parted], all_bits, steps_of(order, with_mp), block_index, 1 if with_mp else 0, sizes)


def small_sums(vectors, block_index, order, sizes):
    blocks = sizes["dp"] * sizes["mp"]
    count = len(vectors)
    stacked = jnp.stack(vectors).reshape(count, blocks, -1).transpose(1, 0, 2)
    all_bits = list(range(blocks.bit_length() - 1))[::-1]
    share = halving([stacked], all_bits, steps_of(order, True), block_index, 1, sizes)
    return [share[i] for i in range(count)]


def build(dp_size, mp_size):
    plain, swapped, last = bit_orders(dp_size)
    sizes = {"dp": dp_size, "mp": mp_size}

    def swap(value):
        return lax.ppermute(value, "mp", [(i, i ^ 1) for i in range(mp_size)])

    def local(
        media_feats,
        latents,
        patch_counts,
        cotangent,
        query_weight,
        key_weight,
        value_weight,
        out_weight,
        up_weight,
        down_weight,
        media_gain,
        media_shift,
        latent_gain,
        latent_shift,
        feed_gain,
        feed_shift,
    ):
        micro, patches, width = media_feats.shape
        dp_index = lax.axis_index("dp").astype(jnp.int32)
        flat_index = dp_index * mp_size + lax.axis_index("mp").astype(jnp.int32)

        grad_own = cotangent.reshape(-1, width)
        grad_all = jnp.concatenate([grad_own, swap(grad_own)])
        media_full = media_feats.reshape(-1, width).astype(F32)
        latents_full = latents.reshape(-1, width).astype(F32)
        media_n, media_hat, media_inv = normalize(media_full, media_gain, media_shift)
        latent_n, latent_hat, latent_inv = normalize(latents_full, latent_gain, latent_shift)
        latent_low = latent_n.astype(BF16)
        both_low = jnp.concatenate([media_n.astype(BF16), latent_low])
        queries = low_mm(latent_low, query_weight)
        keys = low_mm(both_low, key_weight).reshape(2, -1, width)
        values = low_mm(both_low, value_weight).reshape(2, -1, width)
        own = latent_low.shape[0]
        work = 4 * own * (patches + 2 * LAT_IMG) * width
        mixed_low, log_norm = attention_call(
            attend_kernel, patch_counts, queries, keys, values, [], ["one", "norm"], work
        )
        residual = latents_full + mm(mixed_low, out_weight)
        feed_in, feed_hat, feed_inv = normalize(residual, feed_gain, feed_shift)
        feed_own = feed_in.astype(BF16)
        feed_all = jnp.concatenate([feed_own, swap(feed_own)])

        tile = 512
        tiles = up_weight.shape[1] // tile
        second = tiles // 3
        third = tiles // 6
        shares = [(tiles - second - third, plain, swapped), (second, swapped, plain), (third, last, last)]
        before = None
        start = 0
        down_pieces, up_pieces = [], []
        for count, down_order, up_order in shares:
            grad_down, grad_up_w, *before = feed_part(
                feed_all, grad_all, up_weight, down_weight, start, count, tile, before
            )
            start += count
            if down_order is up_order:
                joined = jnp.concatenate([grad_down, grad_up_w], 1)
                piece = scatter_partials(joined, down_order, dp_index, False, sizes)
                half = piece.shape[1] // 2
                down_pieces.append(piece[:, :half])
                up_pieces.append(piece[:, half:])
            else:
                down_pieces.append(scatter_partials(grad_down, down_order, dp_index, False, sizes))
                up_pieces.append(scatter_partials(grad_up_w, up_order, dp_index, False, sizes))
        hidden, grad_up = before

        feed_back_other = mm(grad_up[own:], up_weight, NT).astype(BF16)
        grad_feed_in = mm(grad_up[:own], up_weight, NT) + swap(feed_back_other).astype(F32)
        grad_feed_part, grad_feed_gain, grad_feed_shift = normalize_back(
            grad_feed_in, feed_gain, feed_hat, feed_inv
        )
        grad_residual = grad_own.astype(F32) + grad_feed_part
        grad_residual_low = grad_residual.astype(BF16)
        grad_out_t = scatter_partials(product(grad_residual_low, mixed_low), last, flat_index, True, sizes)
        grad_mixed = mm(grad_residual_low, out_weight, NT).astype(BF16)

        grad_queries, grad_keys, grad_values = attention_call(
            attend_back_kernel,
            patch_counts,
            queries,
            keys,
            values,
            [("one", grad_mixed), ("norm", log_norm)],
            ["one", "two", "two"],
            2 * work,
        )
        grad_keys = grad_keys.reshape(-1, width)
        grad_values = grad_values.reshape(-1, width)
        key_sums = scatter_partials(product(both_low, grad_keys, grad_queries, 0), plain, flat_index, True, sizes)
        value_sums = scatter_partials(
            product(both_low, grad_values, grad_queries, 1), swapped, flat_index, True, sizes
        )
        grad_query_w = jnp.concatenate([key_sums[:, width:], value_sums[:, width:]], 1)

        grad_both = mm(grad_keys, key_weight, NT) + mm(grad_values, value_weight, NT)
        media_rows = micro * patches
        grad_latent_n = grad_both[media_rows:] + mm(grad_queries, query_weight, NT)
        grad_latent_part, grad_latent_gain, grad_latent_shift = normalize_back(
            grad_latent_n, latent_gain, latent_hat, latent_inv
        )
        grad_media, grad_media_gain, grad_media_shift = normalize_back(
            grad_both[:media_rows], media_gain, media_hat, media_inv
        )
        grad_latents = grad_residual + grad_latent_part
        branch_other = mm(hidden[own:], down_weight).astype(BF16)
        branch = mm(hidden[:own], down_weight) + swap(branch_other).astype(F32)
        result = (residual + branch).astype(BF16)
        sums = small_sums(
            [
                grad_media_gain,
                grad_media_shift,
                grad_latent_gain,
                grad_latent_shift,
                grad_feed_gain,
                grad_feed_shift,
            ],
            flat_index,
            plain,
            sizes,
        )
        return (
            result.reshape(latents.shape),
            grad_latents.reshape(latents.shape),
            grad_media.reshape(media_feats.shape),
            grad_query_w,
            key_sums[:, :width],
            value_sums[:, :width],
            grad_out_t.T,
            jnp.concatenate(up_pieces, 1),
            jnp.concatenate(down_pieces, 1).T,
            *sums,
        )

    return local


def solution(mesh):
    rows = P(None, ("dp", "mp"), None)
    in_specs = (rows, rows, P(None, ("dp", "mp")), rows, P(), P(), P(), P(), P(None, "mp"), P("mp", None)) + (P(),) * 6
    first = P(("dp", "mp"), None)
    out_specs = (rows, rows, rows, first, first, first, P(None, ("dp", "mp")), P("dp", "mp"), P("mp", "dp")) + (
        P(("dp", "mp")),
    ) * 6
    local = build(mesh.shape["dp"], mesh.shape["mp"])
    return jax.shard_map(local, mesh=mesh, in_specs=in_specs, out_specs=out_specs, check_vma=False)
```

```python
import functools

import jax
import jax.numpy as jnp
from jax import lax
from jax.experimental import pallas as pl
from jax.experimental.pallas import tpu as pltpu
from jax.sharding import PartitionSpec as P

HEADS = 16
LAT_IMG = 64
EPSILON = 1e-05
MASKED_SCORE = -1e30
ROOT_HALF = 0.7071067811865476
DENSITY_SCALE = 0.3989422804014327
F32 = jnp.float32
BF16 = jnp.bfloat16
NN = (((1,), (0,)), ((), ()))
NT = (((1,), (1,)), ((), ()))
TN = (((0,), (0,)), ((), ()))
MIB = 1024 * 1024
ROW_TILE = 16
LONG = pl.CostEstimate(flops=10**12, bytes_accessed=10**10, transcendentals=0)


def mm(left, right, dims=NN):
    return lax.dot_general(left, right, dims, preferred_element_type=F32)


def low_mm(left, right):
    return mm(left, right).astype(BF16)


def normalize(values, gain_vec, shift_vec):
    row_mean = jnp.mean(values, -1, keepdims=True)
    centred = values - row_mean
    inv_scale = lax.rsqrt(jnp.mean(centred * centred, -1, keepdims=True) + EPSILON)
    scaled = centred * inv_scale
    return (scaled * gain_vec + shift_vec, scaled, inv_scale)


def mask_biases(counts, step, keys, lats, pair):
    lane = lax.broadcasted_iota(jnp.int32, (1, lats), 1) // LAT_IMG
    first = jnp.zeros((1, lats), jnp.int32)
    past = jnp.zeros((1, lats), jnp.int32)
    total = jnp.int32(0)
    for i in range(counts.shape[1]):
        after = total + counts[step, i]
        first = jnp.where(lane == i, total, first)
        past = jnp.where(lane == i, after, past)
        total = after
    place = lax.broadcasted_iota(jnp.int32, (keys, lats), 0)
    media = jnp.where((place >= first) & (place < past), 0.0, MASKED_SCORE)
    key_image = lax.broadcasted_iota(jnp.int32, (pair, pair), 0) // LAT_IMG
    latent_image = lax.broadcasted_iota(jnp.int32, (pair, pair), 1) // LAT_IMG
    return media, jnp.where(key_image == latent_image, 0.0, MASKED_SCORE)


def spans(total, size):
    return [slice(start, start + size) for start in range(0, total, size)]


def attend_kernel(counts, q, k, v, mixed, norm, *, heads, dim, pair):
    scale = dim**-0.5
    lats = q.shape[0]
    bias_m, bias_l = mask_biases(counts, pl.program_id(0), k.shape[1], lats, pair)
    pairs = spans(lats, pair)
    for j in range(heads):
        c = slice(dim * j, dim * j + dim)
        qh = q[:, c]
        kl = k[1, :, c]
        vl = v[1, :, c]
        s_m = mm(k[0, :, c], qh, NT) * scale + bias_m
        s_l = jnp.concatenate([mm(kl[p], qh[p], NT) * scale + bias_l for p in pairs], 1)
        top = jnp.maximum(jnp.max(s_m, 0, keepdims=True), jnp.max(s_l, 0, keepdims=True))
        e_m = jnp.exp(s_m - top)
        e_l = jnp.exp(s_l - top)
        total = jnp.sum(e_m, 0, keepdims=True) + jnp.sum(e_l, 0, keepdims=True)
        inverse = 1.0 / total
        p_m = (e_m * inverse).astype(BF16)
        p_l = (e_l * inverse).astype(BF16)
        latent_part = jnp.concatenate([mm(p_l[:, p], vl[p], TN) for p in pairs], 0)
        mixed[:, c] = (mm(p_m, v[0, :, c], TN) + latent_part).astype(BF16)
        norm[0, 0, j : j + 1, :] = top + jnp.log(total)


def attend_back_kernel(counts, q, k, v, grad_mixed, norm, grad_q, grad_k, grad_v, *, heads, dim, pair):
    scale = dim**-0.5
    lats = q.shape[0]
    bias_m, bias_l = mask_biases(counts, pl.program_id(0), k.shape[1], lats, pair)
    pairs = spans(lats, pair)
    for j in range(heads):
        c = slice(dim * j, dim * j + dim)
        qh = q[:, c]
        km = k[0, :, c]
        kl = k[1, :, c]
        vl = v[1, :, c]
        gh = grad_mixed[:, c]
        log_norm = norm[0, 0, j : j + 1, :]
        p_m = jnp.exp(mm(km, qh, NT) * scale + bias_m - log_norm)
        s_l = jnp.concatenate([mm(kl[p], qh[p], NT) * scale + bias_l for p in pairs], 1)
        p_l = jnp.exp(s_l - log_norm)
        d_m = mm(v[0, :, c], gh, NT)
        d_l = jnp.concatenate([mm(vl[p], gh[p], NT) for p in pairs], 1)
        row_mean = jnp.sum(d_m * p_m, 0, keepdims=True) + jnp.sum(d_l * p_l, 0, keepdims=True)
        g_m = (p_m * (d_m - row_mean)).astype(BF16)
        g_l = (p_l * (d_l - row_mean)).astype(BF16)
        p_m = p_m.astype(BF16)
        p_l = p_l.astype(BF16)
        grad_v[0, :, c] = mm(p_m, gh).astype(BF16)
        grad_k[0, :, c] = (mm(g_m, qh) * scale).astype(BF16)
        for p in pairs:
            grad_v[1, p, c] = mm(p_l[:, p], gh[p]).astype(BF16)
            grad_k[1, p, c] = (mm(g_l[:, p], qh[p]) * scale).astype(BF16)
        latent_part = jnp.concatenate([mm(g_l[:, p], kl[p], TN) for p in pairs], 0)
        grad_q[:, c] = ((mm(g_m, km, TN) + latent_part) * scale).astype(BF16)


def call(kernel, operands, in_specs, out_specs, out_shape, grid, after=(), scalars=0, scratch=(), aliases=None):
    given = len(operands)

    def body(*refs):
        kernel(*refs[:given], *refs[given + len(after) :])

    return pl.pallas_call(
        body,
        grid_spec=pltpu.PrefetchScalarGridSpec(
            num_scalar_prefetch=scalars,
            grid=grid,
            in_specs=list(in_specs) + [pl.BlockSpec(memory_space=pl.ANY)] * len(after),
            out_specs=out_specs,
            scratch_shapes=list(scratch),
        ),
        out_shape=out_shape,
        input_output_aliases=aliases or {},
        compiler_params=pltpu.CompilerParams(vmem_limit_bytes=60 * MIB),
        cost_estimate=LONG,
    )(*operands, *after)


def gate(value, *after):
    def kernel(source, target):
        pass

    anywhere = pl.BlockSpec(memory_space=pl.ANY)
    shape = jax.ShapeDtypeStruct(value.shape, value.dtype)
    return call(kernel, [value], [anywhere], anywhere, shape, (1,), after, aliases={0: 0})


def attention_call(kernel, counts, queries, keys, values, more, outs, after=()):
    micro = counts.shape[0]
    rows = queries.shape[0] // micro
    width = queries.shape[1]
    groups = 2
    heads = HEADS // groups
    group = width // groups
    one = pl.BlockSpec((rows, group), lambda m, g: (m, g))
    two = pl.BlockSpec((2, rows, group), lambda m, g: (0, m, g))
    norm = pl.BlockSpec((1, 1, heads, rows), lambda m, g: (m, g, 0, 0))
    kinds = {
        "one": (one, jax.ShapeDtypeStruct(queries.shape, BF16)),
        "two": (two, jax.ShapeDtypeStruct(keys.shape, BF16)),
        "norm": (norm, jax.ShapeDtypeStruct((micro, groups, heads, rows), F32)),
    }
    return call(
        functools.partial(kernel, heads=heads, dim=width // HEADS, pair=2 * LAT_IMG),
        [counts, queries, keys, values] + [value for _, value in more],
        [pl.BlockSpec(memory_space=pltpu.SMEM), one, two, two] + [kinds[kind][0] for kind, _ in more],
        [kinds[kind][0] for kind in outs],
        [kinds[kind][1] for kind in outs],
        (micro, groups),
        after,
    )


def split_rows(whole, rear_ref, front_ref, block_rows, first_bit, mine):
    for i in range(rear_ref.shape[0]):
        low = i & ((1 << first_bit) - 1)
        base = ((i >> first_bit) << (first_bit + 1)) | low
        for ref, side in ((rear_ref, 1 - mine), (front_ref, mine)):
            block = base + side * (1 << first_bit)
            rows = pl.ds(pl.multiple_of(block * block_rows, block_rows), block_rows)
            ref[i, :, :] = whole[rows, :]


def feed_kernel(index, feed_own, feed_other, cot_own, cot_other, up, down, *refs, kept, bits, block_rows, joined):
    refs = refs[kept:]
    half = feed_own.shape[0]
    width = feed_own.shape[1]
    if bits is None:
        grad_down, grad_up_w, hidden, grad_up = refs
    else:
        *sides, hidden, grad_up, grad_down, grad_up_w = refs
    for n, (feed, cot) in enumerate(((feed_own, cot_own), (feed_other, cot_other))):
        r = slice(n * half, (n + 1) * half)
        u = mm(feed[...], up[...])
        grad_hidden = mm(cot[...], down[...], NT)
        cdf = 0.5 * (1.0 + lax.erf(u * ROOT_HALF))
        pdf = jnp.exp(-0.5 * u * u) * DENSITY_SCALE
        hidden[r, :] = (u * cdf).astype(BF16)
        grad_up[r, :] = (grad_hidden * (cdf + u * pdf)).astype(BF16)
    for r in spans(width, width // 2):
        down_half = mm(cot_own[:, r], hidden[:half, :], TN) + mm(cot_other[:, r], hidden[half:, :], TN)
        grad_down[r, :] = down_half.astype(BF16)
        up_half = mm(feed_own[:, r], grad_up[:half, :], TN) + mm(feed_other[:, r], grad_up[half:, :], TN)
        grad_up_w[r, :] = up_half.astype(BF16)
    if bits is not None:
        tile = up.shape[1]
        if joined:
            sides = [
                sides[0].at[:, :, :tile],
                sides[1].at[:, :, :tile],
                sides[0].at[:, :, tile:],
                sides[1].at[:, :, tile:],
            ]
        for whole, rear, front, bit in ((grad_down, *sides[:2], bits[0]), (grad_up_w, *sides[2:], bits[1])):
            split_rows(whole, rear, front, block_rows, bit, (index[0] >> bit) & 1)


def feed_part(index, rows_in, up, down, start, tiles, tile, before, bits, blocks, after=()):
    half, width = rows_in[0].shape
    block_rows = width // blocks
    whole = pl.BlockSpec((half, width), lambda t, i: (0, 0), pipeline_mode=pl.Buffered(1))
    units = pl.BlockSpec((2 * half, tile), lambda t, i: (0, start + t))
    unit_shape = jax.ShapeDtypeStruct((2 * half, up.shape[1]), BF16)
    kept = [] if before is None else list(before)
    split = block_rows % ROW_TILE == 0
    joined = split and tiles == 1 and bits[0] == bits[1]
    if split:
        columns = 2 * tile if joined else tile
        count = 2 if joined else 4
        grads = [pl.BlockSpec((blocks // 2, block_rows, columns), lambda t, i: (0, 0, t))] * count
        shapes = [jax.ShapeDtypeStruct((blocks // 2, block_rows, columns * tiles), BF16)] * count
        scratch = [pltpu.VMEM((width, tile), BF16)] * 2
    else:
        grads = [pl.BlockSpec((width, tile), lambda t, i: (0, t))] * 2
        shapes = [jax.ShapeDtypeStruct((width, tiles * tile), BF16)] * 2
        scratch = []
    first = len(shapes)
    anywhere = pl.BlockSpec(memory_space=pl.ANY)
    results = call(
        functools.partial(
            feed_kernel, kept=len(kept), bits=bits if split else None, block_rows=block_rows, joined=joined
        ),
        [index, *rows_in, up, down, *kept],
        [
            whole,
            whole,
            whole,
            whole,
            pl.BlockSpec((width, tile), lambda t, i: (0, start + t)),
            pl.BlockSpec((tile, width), lambda t, i: (start + t, 0)),
        ]
        + [anywhere] * len(kept),
        grads + [units, units],
        shapes + [unit_shape, unit_shape],
        (tiles,),
        after,
        1,
        scratch,
        {7: first, 8: first + 1} if kept else {},
    )
    return results[:-2], results[-2:]


def product_kernel(index, *refs, lefts, parts, block_rows, split):
    step = pl.program_id(0)
    target = refs[-1]
    rights = refs[lefts : lefts + len(parts)]
    for (place, first, past), right in zip(parts, rights):

        @pl.when((step >= first) & (step < past))
        def _(left=refs[place], right=right):
            skipped = left.shape[0] - right.shape[0]
            target[...] = mm(left[skipped:, :], right[...], TN).astype(BF16)

    if split:
        split_rows(target, refs[-3], refs[-2], block_rows, 0, index[0] & 1)


def product(index, lefts, parts, blocks, after):
    width = lefts[0].shape[1]
    block_rows = width // blocks
    tile = width // 2
    split = block_rows % ROW_TILE == 0
    in_specs = [pl.BlockSpec(left.shape, lambda t, i: (0, 0), pipeline_mode=pl.Buffered(1)) for left in lefts]
    steps = []
    start = 0
    for place, right, first, count in parts:

        def at(t, i, first=first, start=start, count=count):
            return (0, first + jnp.clip(t - start, 0, count - 1))

        in_specs.append(pl.BlockSpec((right.shape[0], tile), at))
        steps.append((place, start, start + count))
        start += count
    if split:
        out_specs = [pl.BlockSpec((blocks // 2, block_rows, tile), lambda t, i: (0, 0, t))] * 2
        out_shape = [jax.ShapeDtypeStruct((blocks // 2, block_rows, tile * start), BF16)] * 2
        scratch = [pltpu.VMEM((width, tile), BF16)]
    else:
        out_specs = [pl.BlockSpec((width, tile), lambda t, i: (0, t))]
        out_shape = [jax.ShapeDtypeStruct((width, tile * start), BF16)]
        scratch = []
    kernel = functools.partial(product_kernel, lefts=len(lefts), parts=steps, block_rows=block_rows, split=split)
    operands = [index, *lefts] + [right for _, right, _, _ in parts]
    return call(kernel, operands, in_specs, out_specs, out_shape, (start,), after, 1, scratch)


def feed_norm_back_kernel(own, other, source, base, gain, weight, out, out_low, mixed_low, sums):
    e = own[...] + other[...].astype(F32)
    _, hat, inverse = normalize(source[...], gain[...], 0.0)
    weighted = e * gain[...]
    first_mean = jnp.mean(weighted, -1, keepdims=True)
    second_mean = jnp.mean(weighted * hat, -1, keepdims=True)
    grad = base[...].astype(F32) + inverse * (weighted - first_mean - hat * second_mean)
    out[...] = grad
    low = grad.astype(BF16)
    out_low[...] = low
    mixed_low[...] = mm(low, weight[...], NT).astype(BF16)
    fresh = [jnp.sum(e * hat, 0, keepdims=True), jnp.sum(e, 0, keepdims=True)]

    @pl.when(pl.program_id(0) == 0)
    def _():
        sums[0:1, :], sums[1:2, :] = fresh

    @pl.when(pl.program_id(0) > 0)
    def _():
        sums[0:1, :] += fresh[0]
        sums[1:2, :] += fresh[1]


def feed_norm_back(own, other, source, base, gain, weight, after):
    rows, width = source.shape
    size = 128
    part = pl.BlockSpec((size, width), lambda t: (t, 0))
    line = pl.BlockSpec((1, width), lambda t: (0, 0))
    whole = pl.BlockSpec(weight.shape, lambda t: (0, 0), pipeline_mode=pl.Buffered(1))
    low = jax.ShapeDtypeStruct((rows, width), BF16)
    return call(
        feed_norm_back_kernel,
        [own, other, source, base, gain.reshape(1, width), weight],
        [part] * 4 + [line, whole],
        [part] * 3 + [pl.BlockSpec((2, width), lambda t: (0, 0))],
        [jax.ShapeDtypeStruct((rows, width), F32), low, low, jax.ShapeDtypeStruct((2, width), F32)],
        (rows // size,),
        after,
    )


def norm_back_kernel(*refs, pairs):
    lefts, weights, refs = refs[:pairs], refs[pairs : 2 * pairs], refs[2 * pairs :]
    source, gain, *base, out, sums, upstream = refs
    step = pl.program_id(0)
    tile = weights[0].shape[0]
    columns = pl.ds(pl.multiple_of(step * tile, tile), tile)
    total = mm(lefts[0][...], weights[0][...], NT)
    for left, weight in zip(lefts[1:], weights[1:]):
        total = total + mm(left[...], weight[...], NT)
    upstream[:, columns] = total

    @pl.when(step == pl.num_programs(0) - 1)
    def _():
        rows, width = upstream.shape
        size = 64

        def chunk(i, carry):
            gain_sum, shift_sum = carry
            r = pl.ds(pl.multiple_of(i * size, size), size)
            e = upstream[r, :]
            _, hat, inverse = normalize(source[r, :].astype(F32), gain[...], 0.0)
            weighted = e * gain[...]
            first_mean = jnp.mean(weighted, -1, keepdims=True)
            second_mean = jnp.mean(weighted * hat, -1, keepdims=True)
            grad = inverse * (weighted - first_mean - hat * second_mean)
            if base:
                grad = grad + base[0][r, :]
            out[r, :] = grad
            return gain_sum + jnp.sum(e * hat, 0, keepdims=True), shift_sum + jnp.sum(e, 0, keepdims=True)

        zero = jnp.zeros((1, width), F32)
        sums[0:1, :], sums[1:2, :] = lax.fori_loop(0, rows // size, chunk, (zero, zero))


def norm_back_product(pairs, source, base, gain, after):
    rows, width = source.shape
    tile = 512
    whole = pl.BlockSpec((rows, width), lambda t: (0, 0), pipeline_mode=pl.Buffered(1))

    def rows_of(left, place):
        return pl.BlockSpec((rows, left.shape[1]), lambda t: (place, 0), pipeline_mode=pl.Buffered(1))

    operands = [left for left, _, _ in pairs] + [weight for _, _, weight in pairs] + [source, gain.reshape(1, width)]
    in_specs = [rows_of(left, place) for left, place, _ in pairs]
    in_specs += [pl.BlockSpec((tile, weight.shape[1]), lambda t: (t, 0)) for _, _, weight in pairs]
    in_specs += [whole, pl.BlockSpec((1, width), lambda t: (0, 0))]
    if base is not None:
        operands.append(base)
        in_specs.append(whole)
    return call(
        functools.partial(norm_back_kernel, pairs=len(pairs)),
        operands,
        in_specs,
        [whole, pl.BlockSpec((2, width), lambda t: (0, 0))],
        [jax.ShapeDtypeStruct((rows, width), F32), jax.ShapeDtypeStruct((2, width), F32)],
        (width // tile,),
        after,
        scratch=[pltpu.VMEM((rows, width), F32)],
    )


def plain_kernel(left, weight, *refs, dims):
    total = mm(left[...], weight[...], dims)
    for term in refs[:-1]:
        total = total + term[...].astype(F32)
    refs[-1][...] = total.astype(refs[-1].dtype)


def plain_product(left, place, rows, weight, dims, terms, after=(), kind=BF16):
    tile = 512
    if dims is NT:
        width = weight.shape[0]
        weights = pl.BlockSpec((tile, weight.shape[1]), lambda t: (t, 0))
    else:
        width = weight.shape[1]
        weights = pl.BlockSpec((weight.shape[0], tile), lambda t: (0, t))
    columns = pl.BlockSpec((rows, tile), lambda t: (0, t))
    return call(
        functools.partial(plain_kernel, dims=dims),
        [left, weight, *terms],
        [pl.BlockSpec((rows, left.shape[1]), lambda t: (place, 0), pipeline_mode=pl.Buffered(1)), weights]
        + [columns] * len(terms),
        columns,
        jax.ShapeDtypeStruct((rows, width), kind),
        (width // tile,),
        after,
    )


def added(left, right, after):
    def kernel(a, b, out):
        out[...] = a[...] + b[...]

    whole = pl.BlockSpec(left.shape, lambda t: (0, 0))
    return call(kernel, [left, right], [whole] * 2, whole, jax.ShapeDtypeStruct(left.shape, left.dtype), (1,), after)


def sum_kernel(index, *refs, segments):
    out = refs[-1]
    column = 0
    for width, terms in segments:
        total = None
        for ref, start in terms:
            value = refs[ref][0, :, start : start + width].astype(F32)
            total = value if total is None else total + value
        out[0, :, column : column + width] = total.astype(out.dtype)
        column += width


def with_bit(position, place, bit):
    low = position & ((1 << place) - 1)
    return ((position >> place) << (place + 1)) | (bit << place) | low


class Segment:
    def __init__(self, width, arrays, taken):
        self.width = width
        self.taken = list(taken)
        self.terms = [(a, len(taken), 0) for a in arrays]


class Chain:
    def __init__(self, index, bits, sizes, first=None):
        self.index = index
        self.sizes = sizes
        self.left = sorted(bits)
        self.taken = [] if first is None else [(self.left.index(first), first)]
        if first is not None:
            self.left.remove(first)
        self.segments = []

    def add(self, width, arrays):
        self.segments.append(Segment(width, arrays, self.taken))

    def join(self, other):
        self.segments += other.segments

    def _sum(self, count, place_bit, dtype, after):
        arrays, maps, segments = [], [], []
        for segment in self.segments:
            listed = []
            for array, level, start in segment.terms:
                path = segment.taken[level:]
                known = [n for n, a in enumerate(arrays) if a is array and maps[n] == path]
                if not known:
                    arrays.append(array)
                    maps.append(path)
                    known = [len(arrays) - 1]
                listed.append((known[0], start))
            segments.append((segment.width, listed))
        rows = arrays[0].shape[1]
        size = rows
        total = sum(segment.width for segment in self.segments)

        def block(path):
            def at(i, j, index):
                position = i
                if place_bit is not None:
                    place, bit = place_bit
                    position = with_bit(position, place, 1 - ((index[0] >> bit) & 1))
                for place, bit in path[::-1]:
                    position = with_bit(position, place, (index[0] >> bit) & 1)
                return (position, j, 0)

            return at

        return call(
            functools.partial(sum_kernel, segments=segments),
            [self.index, *arrays],
            [pl.BlockSpec((1, size, a.shape[2]), block(path)) for a, path in zip(arrays, maps)],
            pl.BlockSpec((1, size, total), lambda i, j, index: (i, j, 0)),
            jax.ShapeDtypeStruct((count, rows, total), dtype),
            (count, rows // size),
            after,
            1,
        )

    def pack(self, bit, after=()):
        return self._sum(1 << (len(self.left) - 1), (self.left.index(bit), bit), BF16, after)

    def travel(self, packed, bit):
        got = lax.ppermute(packed, "dp", [(i, i ^ (1 << bit)) for i in range(self.sizes["dp"])])
        step = (self.left.index(bit), bit)
        self.left.remove(bit)
        start = 0
        for segment in self.segments:
            segment.taken.append(step)
            segment.terms.append((got, len(segment.taken), start))
            start += segment.width
        return got

    def finish(self, after=()):
        for bit in list(self.left):
            self.travel(self.pack(bit), bit)
        return self._sum(1, None, F32, after)[0]


def bit_orders(count):
    bits = count.bit_length() - 1
    if bits == 4:
        return [(0, 1, 2, 3), (1, 0, 2, 3), (2, 3, 0, 1), (0, 2, 3, 1)]
    plain = tuple(range(bits))
    third = bits // 3
    return [plain, (1, 0) + plain[2:], plain[2 * third :] + plain[: 2 * third], plain]


def sided(value, bit, bits, side):
    place = bits.index(bit)
    shape = value.shape
    outer = 1 << place
    parts = value.reshape((outer, 2, shape[0] // (2 * outer)) + shape[1:])
    return lax.dynamic_index_in_dim(parts, side, 1, keepdims=False).reshape((shape[0] // 2,) + shape[1:])


def build(dp_size, mp_size):
    plain, swapped, last, around = bit_orders(dp_size)
    sizes = {"dp": dp_size, "mp": mp_size}
    all_bits = sorted(plain)

    def swap(value):
        return lax.ppermute(value, "mp", [(i, i ^ 1) for i in range(mp_size)])

    def local(
        media_feats,
        latents,
        patch_counts,
        cotangent,
        query_weight,
        key_weight,
        value_weight,
        out_weight,
        up_weight,
        down_weight,
        media_gain,
        media_shift,
        latent_gain,
        latent_shift,
        feed_gain,
        feed_shift,
    ):
        micro, patches, width = media_feats.shape
        dp_index = lax.axis_index("dp").astype(jnp.int32)
        mp_index = lax.axis_index("mp").astype(jnp.int32)
        flat_index = dp_index * mp_size + mp_index
        dp_list = dp_index.reshape(1)
        mp_list = mp_index.reshape(1)

        def first_step(grads, bit):
            if len(grads) == 2:
                return grads
            parted = grads[0].reshape(dp_size, width // dp_size, -1)
            mine = (dp_index >> bit) & 1
            return sided(parted, bit, all_bits[::-1], 1 - mine), sided(parted, bit, all_bits[::-1], mine)

        def sent_first(grads, bit):
            rear, front = first_step(grads, bit)
            return front, lax.ppermute(rear, "dp", [(i, i ^ (1 << bit)) for i in range(dp_size)])

        def paired(grads):
            if len(grads) == 1:
                parted = grads[0].reshape(dp_size, mp_size, -1, grads[0].shape[1])
                grads = [lax.dynamic_index_in_dim(parted, side, 1, keepdims=False) for side in (1 - mp_index, mp_index)]
            rear, front = grads
            return front, swap(rear)

        grad_own = cotangent.reshape(-1, width)
        grad_other = swap(grad_own)
        media_full = media_feats.reshape(-1, width).astype(F32)
        latents_full = latents.reshape(-1, width).astype(F32)
        media_n, media_hat, media_inv = normalize(media_full, media_gain, media_shift)
        latent_n, latent_hat, latent_inv = normalize(latents_full, latent_gain, latent_shift)
        latent_low = latent_n.astype(BF16)
        both_low = jnp.concatenate([media_n.astype(BF16), latent_low])
        queries = low_mm(latent_low, query_weight)
        keys = low_mm(both_low, key_weight).reshape(2, -1, width)
        values = low_mm(both_low, value_weight).reshape(2, -1, width)
        own = latent_low.shape[0]
        mixed_low, log_norm = attention_call(
            attend_kernel, patch_counts, queries, keys, values, [], ["one", "norm"], (grad_other,)
        )
        residual = latents_full + mm(mixed_low, out_weight)
        feed_in, feed_hat, feed_inv = normalize(residual, feed_gain, feed_shift)
        feed_own = feed_in.astype(BF16)
        feed_other = swap(feed_own)

        tile = 512
        tiles = up_weight.shape[1] // tile
        first = tiles // 3
        third = tiles // 6
        second = tiles - first - third
        rows_in = [feed_own, feed_other, grad_own, grad_other]

        def part(start, count, before, down_order, up_order):
            bits = (down_order[0], up_order[0])
            grads, units = feed_part(
                dp_list, rows_in, up_weight, down_weight, start, count, tile, before, bits, dp_size
            )
            if len(grads) == 2 and width // dp_size % ROW_TILE == 0:
                return grads, None, units
            middle = len(grads) // 2
            return grads[:middle], grads[middle:], units

        along = Chain(dp_list, all_bits, sizes, plain[0])
        across = Chain(dp_list, all_bits, sizes, swapped[0])
        far = Chain(dp_list, all_bits, sizes, last[0])
        down_1, up_1, units = part(0, first, None, plain, swapped)
        along.add(first * tile, sent_first(down_1, plain[0]))
        across.add(first * tile, sent_first(up_1, swapped[0]))
        down_2, up_2, units = part(first, second, units, swapped, plain)
        across.add(second * tile, sent_first(down_2, swapped[0]))
        along.add(second * tile, sent_first(up_2, plain[0]))
        down_3, up_3, units = part(first + second, third, units, last, last)
        hidden, grad_up = units
        far_got = []
        for grads in [down_3] if up_3 is None else [down_3, up_3]:
            far.add(grads[0].shape[-1] if len(grads) == 2 else third * tile, sent_first(grads, last[0]))
            far_got.append(far.segments[-1].terms[1][0])
        part_got = [chain.segments[0].terms[1][0] for chain in (along, across)]
        feed_back_other = plain_product(grad_up, 1, own, up_weight, NT, [], part_got)
        feed_back_got = swap(feed_back_other)
        feed_back = plain_product(grad_up, 0, own, up_weight, NT, [], (feed_back_other,), F32)
        grad_residual, grad_residual_low, grad_mixed, feed_sums = feed_norm_back(
            feed_back, feed_back_got, residual, grad_own, feed_gain, out_weight, (feed_back,)
        )
        blocks = dp_size * mp_size
        grad_queries, grad_keys, grad_values = attention_call(
            attend_back_kernel,
            patch_counts,
            queries,
            keys,
            values,
            [("one", grad_mixed), ("norm", log_norm)],
            ["one", "two", "two"],
        )
        grad_keys = grad_keys.reshape(-1, width)
        grad_values = grad_values.reshape(-1, width)
        half = width // 2
        token = [grad_queries]

        def now():
            return tuple(token)

        def ran(value):
            token[:] = [value]

        def wait(*values):
            token.extend(values)

        def move(chain, bit):
            packed = chain.pack(bit, now())
            ran(packed)
            return chain.travel(packed, bit)

        def end(chain):
            total = chain.finish(now())
            ran(total)
            return total

        def join(*chains):
            joined = Chain(dp_list, chains[0].left, sizes)
            for chain in chains:
                joined.join(chain)
            return joined

        move(along, plain[1])
        move(across, swapped[1])
        wait(*far_got)
        lefts = [both_low, grad_residual_low]
        key_grads = product(
            mp_list, lefts, [(0, grad_keys, 0, 2), (0, grad_queries, 0, 1), (1, mixed_low, 0, 1)], blocks, now()
        )
        keyed = Chain(dp_list, all_bits, sizes)
        keyed.add(2 * width, paired(key_grads))
        ran(key_grads[0])
        value_grads = product(
            mp_list, lefts, [(0, grad_values, 0, 2), (0, grad_queries, 1, 1), (1, mixed_low, 1, 1)], blocks, now()
        )
        valued = Chain(dp_list, all_bits, sizes)
        valued.add(2 * width, paired(value_grads))
        ran(value_grads[0])
        move(keyed, around[0])
        grad_latents, latent_sums = norm_back_product(
            [(grad_queries, 0, query_weight), (grad_keys, 1, key_weight), (grad_values, 1, value_weight)],
            latents.reshape(-1, width),
            grad_residual,
            latent_gain,
            now(),
        )
        ran(grad_latents)
        move(valued, swapped[0])
        both = join(along, across)
        move(far, last[1])
        move(both, plain[2])
        grad_media, media_sums = norm_back_product(
            [(grad_keys, 0, key_weight), (grad_values, 0, value_weight)],
            media_feats.reshape(-1, width),
            None,
            media_gain,
            now(),
        )
        ran(grad_media)
        sums = jnp.concatenate([media_sums, latent_sums, feed_sums])
        arrived = swap(sums)

        def move_sums(bit):
            total = added(sums, arrived, now())
            ran(total)
            return total, None if bit is None else lax.ppermute(total, "dp", [(i, i ^ (1 << bit)) for i in range(dp_size)])

        move(keyed, around[1])
        sums, arrived = move_sums(plain[0])
        move(valued, swapped[1])
        move(far, last[2])
        sums, arrived = move_sums(plain[1])
        move(both, plain[3])
        sums, arrived = move_sums(plain[2])
        move(keyed, around[2])
        move(valued, swapped[2])
        sums, arrived = move_sums(plain[3])
        move(far, last[3])
        both_sum = end(both)
        for bit in plain[4:]:
            sums, arrived = move_sums(bit)
        sums, _ = move_sums(None)
        branch_other = plain_product(hidden, 1, own, down_weight, NN, [], now())
        ran(branch_other)
        branch_got = swap(branch_other)
        move(keyed, around[3])
        move(valued, swapped[3])
        result = plain_product(hidden, 0, own, down_weight, NN, [residual, branch_got], now())
        ran(result)
        far_sum = end(far)
        key_sum = end(keyed)
        value_sum = end(valued)
        split = first * tile
        edge = third * tile
        along_sum, across_sum = both_sum[:, : split + second * tile], both_sum[:, split + second * tile :]
        out_sum = jnp.concatenate([key_sum[:, width + half :], value_sum[:, width + half :]], 1)
        share = width // blocks
        sums = lax.dynamic_slice(sums, (0, flat_index * share), (sums.shape[0], share))
        grad_down_t = jnp.concatenate([along_sum[:, :split], across_sum[:, split:], far_sum[:, :edge]], 1)
        grad_up_w = jnp.concatenate([across_sum[:, :split], along_sum[:, split:], far_sum[:, edge:]], 1)
        return (
            result.reshape(latents.shape),
            grad_latents.reshape(latents.shape),
            grad_media.reshape(media_feats.shape),
            jnp.concatenate([key_sum[:, width : width + half], value_sum[:, width : width + half]], 1),
            key_sum[:, :width],
            value_sum[:, :width],
            out_sum.T,
            grad_up_w,
            grad_down_t.T,
            *[sums[i] for i in range(sums.shape[0])],
        )

    return local


def solution(mesh):
    rows = P(None, ("dp", "mp"), None)
    in_specs = (rows, rows, P(None, ("dp", "mp")), rows, P(), P(), P(), P(), P(None, "mp"), P("mp", None)) + (P(),) * 6
    first = P(("dp", "mp"), None)
    out_specs = (rows, rows, rows, first, first, first, P(None, ("dp", "mp")), P("dp", "mp"), P("mp", "dp")) + (
        P(("dp", "mp")),
    ) * 6
    local = build(mesh.shape["dp"], mesh.shape["mp"])
    return jax.shard_map(local, mesh=mesh, in_specs=in_specs, out_specs=out_specs, check_vma=False)
```

```python
import functools

import jax
import jax.numpy as jnp
from jax import lax
from jax.experimental import pallas as pl
from jax.experimental.pallas import tpu as pltpu
from jax.sharding import PartitionSpec as P

HEADS = 16
LAT_IMG = 64
EPSILON = 1e-05
MASKED_SCORE = -1e30
ROOT_HALF = 0.7071067811865476
DENSITY_SCALE = 0.3989422804014327
F32 = jnp.float32
BF16 = jnp.bfloat16
NN = (((1,), (0,)), ((), ()))
NT = (((1,), (1,)), ((), ()))
TN = (((0,), (0,)), ((), ()))
MIB = 1024 * 1024
ROW_TILE = 16
STEP_BYTES = 1200000
LONG = pl.CostEstimate(flops=10**12, bytes_accessed=10**10, transcendentals=0)


def mm(left, right, dims=NN):
    return lax.dot_general(left, right, dims, preferred_element_type=F32)


def low_mm(left, right):
    return mm(left, right).astype(BF16)


def normalize(values, gain_vec, shift_vec):
    row_mean = jnp.mean(values, -1, keepdims=True)
    centred = values - row_mean
    inv_scale = lax.rsqrt(jnp.mean(centred * centred, -1, keepdims=True) + EPSILON)
    scaled = centred * inv_scale
    return (scaled * gain_vec + shift_vec, scaled, inv_scale)


def mask_biases(counts, step, keys, lats, pair):
    lane = lax.broadcasted_iota(jnp.int32, (1, lats), 1) // LAT_IMG
    first = jnp.zeros((1, lats), jnp.int32)
    past = jnp.zeros((1, lats), jnp.int32)
    total = jnp.int32(0)
    for i in range(counts.shape[1]):
        after = total + counts[step, i]
        first = jnp.where(lane == i, total, first)
        past = jnp.where(lane == i, after, past)
        total = after
    place = lax.broadcasted_iota(jnp.int32, (keys, lats), 0)
    media = jnp.where((place >= first) & (place < past), 0.0, MASKED_SCORE)
    key_image = lax.broadcasted_iota(jnp.int32, (pair, pair), 0) // LAT_IMG
    latent_image = lax.broadcasted_iota(jnp.int32, (pair, pair), 1) // LAT_IMG
    return media, jnp.where(key_image == latent_image, 0.0, MASKED_SCORE)


def spans(total, size):
    return [slice(start, start + size) for start in range(0, total, size)]


def attend_kernel(counts, q, k, v, mixed, norm, *, start, heads, dim, pair):
    scale = dim**-0.5
    lats = q.shape[0]
    bias_m, bias_l = mask_biases(counts, start + pl.program_id(0), k.shape[1], lats, pair)
    pairs = spans(lats, pair)
    for two in spans(heads, 2):
        columns = spans(heads * dim, dim)[two]
        qs = [q[:, c] for c in columns]
        kl = [k[1, :, c] for c in columns]
        s_m = [mm(k[0, :, c], x, NT) * scale + bias_m for c, x in zip(columns, qs)]
        s_l = [jnp.concatenate([mm(y[p], x[p], NT) * scale + bias_l for p in pairs], 1) for y, x in zip(kl, qs)]
        top = [jnp.maximum(jnp.max(x, 0, keepdims=True), jnp.max(y, 0, keepdims=True)) for x, y in zip(s_m, s_l)]
        e_m = [jnp.exp(x - t) for x, t in zip(s_m, top)]
        e_l = [jnp.exp(x - t) for x, t in zip(s_l, top)]
        total = [jnp.sum(x, 0, keepdims=True) + jnp.sum(y, 0, keepdims=True) for x, y in zip(e_m, e_l)]
        inverse = [1.0 / t for t in total]
        p_m = [(x * i).astype(BF16) for x, i in zip(e_m, inverse)]
        p_l = [(x * i).astype(BF16) for x, i in zip(e_l, inverse)]
        outs = []
        for x, y, c in zip(p_m, p_l, columns):
            vl = v[1, :, c]
            latent_part = jnp.concatenate([mm(y[:, p], vl[p], TN) for p in pairs], 0)
            outs.append((mm(x, v[0, :, c], TN) + latent_part).astype(BF16))
        mixed[:, two.start * dim : two.stop * dim] = jnp.concatenate(outs, 1)
        norm[0, 0, two, :] = jnp.concatenate([t + jnp.log(x) for t, x in zip(top, total)], 0)


def attend_back_kernel(counts, q, k, v, grad_mixed, norm, *refs, start, heads, dim, pair):
    grad_q, grad_k, grad_v = refs[-3:]
    scale = dim**-0.5
    lats = q.shape[0]
    bias_m, bias_l = mask_biases(counts, start + pl.program_id(0), k.shape[1], lats, pair)
    pairs = spans(lats, pair)
    for two in spans(heads, 2):
        columns = spans(heads * dim, dim)[two]
        group = slice(two.start * dim, two.stop * dim)
        qs = [q[:, c] for c in columns]
        gs = [grad_mixed[:, c] for c in columns]
        km = [k[0, :, c] for c in columns]
        kl = [k[1, :, c] for c in columns]
        vl = [v[1, :, c] for c in columns]
        norms = [norm[0, 0, j : j + 1, :] for j in range(two.start, two.stop)]
        p_m = [jnp.exp(mm(x, y, NT) * scale + bias_m - n) for x, y, n in zip(km, qs, norms)]
        s_l = [jnp.concatenate([mm(x[p], y[p], NT) * scale + bias_l for p in pairs], 1) for x, y in zip(kl, qs)]
        p_l = [jnp.exp(x - n) for x, n in zip(s_l, norms)]
        d_m = [mm(v[0, :, c], g, NT) for c, g in zip(columns, gs)]
        d_l = [jnp.concatenate([mm(x[p], g[p], NT) for p in pairs], 1) for x, g in zip(vl, gs)]
        means = [
            jnp.sum(x * y, 0, keepdims=True) + jnp.sum(z * w, 0, keepdims=True)
            for x, y, z, w in zip(d_m, p_m, d_l, p_l)
        ]
        g_m = [(x * (y - n)).astype(BF16) for x, y, n in zip(p_m, d_m, means)]
        g_l = [(x * (y - n)).astype(BF16) for x, y, n in zip(p_l, d_l, means)]
        p_m = [x.astype(BF16) for x in p_m]
        p_l = [x.astype(BF16) for x in p_l]
        grad_v[0, :, group] = jnp.concatenate([mm(x, g).astype(BF16) for x, g in zip(p_m, gs)], 1)
        grad_k[0, :, group] = jnp.concatenate([(mm(x, y) * scale).astype(BF16) for x, y in zip(g_m, qs)], 1)
        for p in pairs:
            grad_v[1, p, group] = jnp.concatenate([mm(x[:, p], g[p]).astype(BF16) for x, g in zip(p_l, gs)], 1)
            grad_k[1, p, group] = jnp.concatenate([(mm(x[:, p], y[p]) * scale).astype(BF16) for x, y in zip(g_l, qs)], 1)
        grad_qs = []
        for x, y, z, w in zip(g_m, km, g_l, kl):
            latent_part = jnp.concatenate([mm(z[:, p], w[p], TN) for p in pairs], 0)
            grad_qs.append(((mm(x, y, TN) + latent_part) * scale).astype(BF16))
        grad_q[:, group] = jnp.concatenate(grad_qs, 1)


def call(kernel, operands, in_specs, out_specs, out_shape, grid, after=(), scalars=0, scratch=(), aliases=None):
    given = len(operands)

    def body(*refs):
        kernel(*refs[:given], *refs[given + len(after) :])

    return pl.pallas_call(
        body,
        grid_spec=pltpu.PrefetchScalarGridSpec(
            num_scalar_prefetch=scalars,
            grid=grid,
            in_specs=list(in_specs) + [pl.BlockSpec(memory_space=pl.ANY)] * len(after),
            out_specs=out_specs,
            scratch_shapes=list(scratch),
        ),
        out_shape=out_shape,
        input_output_aliases=aliases or {},
        compiler_params=pltpu.CompilerParams(vmem_limit_bytes=60 * MIB),
        cost_estimate=LONG,
    )(*operands, *after)


def gate(value, *after):
    def kernel(source, target):
        pass

    anywhere = pl.BlockSpec(memory_space=pl.ANY)
    shape = jax.ShapeDtypeStruct(value.shape, value.dtype)
    return call(kernel, [value], [anywhere], anywhere, shape, (1,), after, aliases={0: 0})


def attention_call(kernel, counts, queries, keys, values, more, outs, after=(), start=0, count=None, before=()):
    micro = counts.shape[0]
    rows = queries.shape[0] // micro
    width = queries.shape[1]
    groups = 2
    heads = HEADS // groups
    group = width // groups
    one = pl.BlockSpec((rows, group), lambda m, g: (start + m, g))
    two = pl.BlockSpec((2, rows, group), lambda m, g: (0, start + m, g))
    norm = pl.BlockSpec((1, 1, heads, rows), lambda m, g: (start + m, g, 0, 0))
    kinds = {
        "one": (one, jax.ShapeDtypeStruct(queries.shape, BF16)),
        "two": (two, jax.ShapeDtypeStruct(keys.shape, BF16)),
        "norm": (norm, jax.ShapeDtypeStruct((micro, groups, heads, rows), F32)),
    }
    operands = [counts, queries, keys, values] + [value for _, value in more]
    in_specs = [pl.BlockSpec(memory_space=pltpu.SMEM), one, two, two] + [kinds[kind][0] for kind, _ in more]
    return call(
        functools.partial(kernel, start=start, heads=heads, dim=width // HEADS, pair=2 * LAT_IMG),
        operands + list(before),
        in_specs + [pl.BlockSpec(memory_space=pl.ANY)] * len(before),
        [kinds[kind][0] for kind in outs],
        [kinds[kind][1] for kind in outs],
        (micro if count is None else count, groups),
        after,
        aliases={len(operands) + n: n for n in range(len(before))},
    )


def split_rows(whole, rear_ref, front_ref, block_rows, first_bit, mine):
    for i in range(rear_ref.shape[0]):
        low = i & ((1 << first_bit) - 1)
        base = ((i >> first_bit) << (first_bit + 1)) | low
        for ref, side in ((rear_ref, 1 - mine), (front_ref, mine)):
            block = base + side * (1 << first_bit)
            rows = pl.ds(pl.multiple_of(block * block_rows, block_rows), block_rows)
            ref[i, :, :] = whole[rows, :]


def feed_kernel(index, feed_own, feed_other, cot_own, cot_other, up, down, *refs, kept, bits, far, block_rows):
    refs = refs[kept:]
    half, width = feed_own.shape
    tile = up.shape[1]
    if bits is None:
        grad_down, grad_up_w, hidden, grad_up = refs
    else:
        *sides, hidden, grad_up, grad_down, grad_up_w = refs
    for n, (feed, cot) in enumerate(((feed_own, cot_own), (feed_other, cot_other))):
        r = slice(n * half, (n + 1) * half)
        u = mm(feed[...], up[...])
        grad_hidden = mm(cot[...], down[...], NT)
        cdf = 0.5 * (1.0 + lax.erf(u * ROOT_HALF))
        pdf = jnp.exp(-0.5 * u * u) * DENSITY_SCALE
        hidden[r, :] = (u * cdf).astype(BF16)
        grad_up[r, :] = (grad_hidden * (cdf + u * pdf)).astype(BF16)
    for r in spans(width, width // 2):
        down_half = mm(cot_own[:, r], hidden[:half, :], TN) + mm(cot_other[:, r], hidden[half:, :], TN)
        grad_down[r, :] = down_half.astype(BF16)
        up_half = mm(feed_own[:, r], grad_up[:half, :], TN) + mm(feed_other[:, r], grad_up[half:, :], TN)
        grad_up_w[r, :] = up_half.astype(BF16)
    if bits is None:
        return

    def split(whole, rear, front, bit):
        split_rows(whole, rear, front, block_rows, bit, (index[0] >> bit) & 1)

    def near():
        split(grad_down, *sides[-4:-2], bits[0])
        split(grad_up_w, *sides[-2:], bits[1])

    if far is None:
        near()
    else:
        step = pl.program_id(0)
        pl.when(step > 0)(near)

        @pl.when(step == 0)
        def _():
            rear, front = sides[:2]
            split(grad_down, rear.at[:, :, :tile], front.at[:, :, :tile], far)
            split(grad_up_w, rear.at[:, :, tile:], front.at[:, :, tile:], far)


def feed_part(index, rows_in, up, down, start, tiles, tile, before, bits, far, blocks):
    half, width = rows_in[0].shape
    block_rows = width // blocks
    whole = pl.BlockSpec((half, width), lambda t, i: (0, 0), pipeline_mode=pl.Buffered(1))
    units = pl.BlockSpec((2 * half, tile), lambda t, i: (0, start + t))
    unit_shape = jax.ShapeDtypeStruct((2 * half, up.shape[1]), BF16)
    kept = [] if before is None else list(before)
    split = block_rows % ROW_TILE == 0
    if split:
        apart = 0 if far is None else 1
        shape = (blocks // 2, block_rows)
        grads = [pl.BlockSpec((*shape, 2 * tile), lambda t, i: (0, 0, 0), pipeline_mode=pl.Buffered(1))] * (2 * apart)
        shapes = [jax.ShapeDtypeStruct((*shape, 2 * tile), BF16)] * (2 * apart)
        grads += [pl.BlockSpec((*shape, tile), lambda t, i: (0, 0, jnp.maximum(t - apart, 0)))] * 4
        shapes += [jax.ShapeDtypeStruct((*shape, (tiles - apart) * tile), BF16)] * 4
        scratch = [pltpu.VMEM((width, tile), BF16)] * 2
    else:
        grads = [pl.BlockSpec((width, tile), lambda t, i: (0, t))] * 2
        shapes = [jax.ShapeDtypeStruct((width, tiles * tile), BF16)] * 2
        scratch = []
    first = len(shapes)
    anywhere = pl.BlockSpec(memory_space=pl.ANY)
    results = call(
        functools.partial(
            feed_kernel, kept=len(kept), bits=bits if split else None, far=far if split else None, block_rows=block_rows
        ),
        [index, *rows_in, up, down, *kept],
        [
            whole,
            whole,
            whole,
            whole,
            pl.BlockSpec((width, tile), lambda t, i: (0, start + t)),
            pl.BlockSpec((tile, width), lambda t, i: (start + t, 0)),
        ]
        + [anywhere] * len(kept),
        grads + [units, units],
        shapes + [unit_shape, unit_shape],
        (tiles,),
        (),
        1,
        scratch,
        {7: first, 8: first + 1} if kept else {},
    )
    return results[:-2], results[-2:]


def product_kernel(index, *refs, lefts, parts, block_rows, split):
    step = pl.program_id(0)
    target = refs[-1]
    rights = refs[lefts : lefts + len(parts)]
    for (place, first, past), right in zip(parts, rights):

        @pl.when((step >= first) & (step < past))
        def _(left=refs[place], right=right):
            skipped = left.shape[0] - right.shape[0]
            target[...] = mm(left[skipped:, :], right[...], TN).astype(BF16)

    if split:
        split_rows(target, refs[-3], refs[-2], block_rows, 0, index[0] & 1)


def product(index, lefts, parts, blocks, after, stacked=False):
    width = lefts[0].shape[1]
    block_rows = width // blocks
    tile = width // 2
    split = block_rows % ROW_TILE == 0
    in_specs = [pl.BlockSpec(left.shape, lambda t, i: (0, 0), pipeline_mode=pl.Buffered(1)) for left in lefts]
    steps = []
    start = 0
    for place, right, first, count in parts:

        def at(t, i, first=first, start=start, count=count):
            return (0, first + jnp.clip(t - start, 0, count - 1))

        in_specs.append(pl.BlockSpec((right.shape[0], tile), at))
        steps.append((place, start, start + count))
        start += count
    if split:
        place = (lambda t, i: (0, t, 0)) if stacked else (lambda t, i: (0, 0, t))
        shape = (block_rows * start, tile) if stacked else (block_rows, tile * start)
        out_specs = [pl.BlockSpec((blocks // 2, block_rows, tile), place)] * 2
        out_shape = [jax.ShapeDtypeStruct((blocks // 2, *shape), BF16)] * 2
        scratch = [pltpu.VMEM((width, tile), BF16)]
    else:
        out_specs = [pl.BlockSpec((width, tile), lambda t, i: (0, t))]
        out_shape = [jax.ShapeDtypeStruct((width, tile * start), BF16)]
        scratch = []
    kernel = functools.partial(product_kernel, lefts=len(lefts), parts=steps, block_rows=block_rows, split=split)
    operands = [index, *lefts] + [right for _, right, _, _ in parts]
    return call(kernel, operands, in_specs, out_specs, out_shape, (start,), after, 1, scratch)


def feed_norm_back_kernel(own, other, source, base, gain, weight, out, out_low, mixed_low, sums):
    e = own[...] + other[...].astype(F32)
    _, hat, inverse = normalize(source[...], gain[...], 0.0)
    weighted = e * gain[...]
    first_mean = jnp.mean(weighted, -1, keepdims=True)
    second_mean = jnp.mean(weighted * hat, -1, keepdims=True)
    grad = base[...].astype(F32) + inverse * (weighted - first_mean - hat * second_mean)
    out[...] = grad
    low = grad.astype(BF16)
    out_low[...] = low
    mixed_low[...] = mm(low, weight[...], NT).astype(BF16)
    fresh = [jnp.sum(e * hat, 0, keepdims=True), jnp.sum(e, 0, keepdims=True)]

    @pl.when(pl.program_id(0) == 0)
    def _():
        sums[0:1, :], sums[1:2, :] = fresh

    @pl.when(pl.program_id(0) > 0)
    def _():
        sums[0:1, :] += fresh[0]
        sums[1:2, :] += fresh[1]


def feed_norm_back(own, other, source, base, gain, weight, after):
    rows, width = source.shape
    size = 256
    part = pl.BlockSpec((size, width), lambda t: (t, 0))
    line = pl.BlockSpec((1, width), lambda t: (0, 0))
    whole = pl.BlockSpec(weight.shape, lambda t: (0, 0), pipeline_mode=pl.Buffered(1))
    low = jax.ShapeDtypeStruct((rows, width), BF16)
    return call(
        feed_norm_back_kernel,
        [own, other, source, base, gain.reshape(1, width), weight],
        [part] * 4 + [line, whole],
        [part] * 3 + [pl.BlockSpec((2, width), lambda t: (0, 0))],
        [jax.ShapeDtypeStruct((rows, width), F32), low, low, jax.ShapeDtypeStruct((2, width), F32)],
        (rows // size,),
        after,
    )


def norm_back_kernel(*refs, pairs):
    lefts, weights, refs = refs[:pairs], refs[pairs : 2 * pairs], refs[2 * pairs :]
    source, gain, *base, out, sums, upstream = refs
    step = pl.program_id(0)
    tile = weights[0].shape[0]
    columns = pl.ds(pl.multiple_of(step * tile, tile), tile)
    total = mm(lefts[0][...], weights[0][...], NT)
    for left, weight in zip(lefts[1:], weights[1:]):
        total = total + mm(left[...], weight[...], NT)
    upstream[:, columns] = total

    @pl.when(step == pl.num_programs(0) - 1)
    def _():
        rows, width = upstream.shape
        size = 64

        def chunk(i, carry):
            gain_sum, shift_sum = carry
            r = pl.ds(pl.multiple_of(i * size, size), size)
            e = upstream[r, :]
            _, hat, inverse = normalize(source[r, :].astype(F32), gain[...], 0.0)
            weighted = e * gain[...]
            first_mean = jnp.mean(weighted, -1, keepdims=True)
            second_mean = jnp.mean(weighted * hat, -1, keepdims=True)
            grad = inverse * (weighted - first_mean - hat * second_mean)
            if base:
                grad = grad + base[0][r, :]
            out[r, :] = grad
            return gain_sum + jnp.sum(e * hat, 0, keepdims=True), shift_sum + jnp.sum(e, 0, keepdims=True)

        zero = jnp.zeros((1, width), F32)
        sums[0:1, :], sums[1:2, :] = lax.fori_loop(0, rows // size, chunk, (zero, zero))


def norm_back_product(pairs, source, base, gain, after):
    rows, width = source.shape
    tile = 512
    whole = pl.BlockSpec((rows, width), lambda t: (0, 0), pipeline_mode=pl.Buffered(1))

    def rows_of(left, place):
        return pl.BlockSpec((rows, left.shape[1]), lambda t: (place, 0), pipeline_mode=pl.Buffered(1))

    operands = [left for left, _, _ in pairs] + [weight for _, _, weight in pairs] + [source, gain.reshape(1, width)]
    in_specs = [rows_of(left, place) for left, place, _ in pairs]
    in_specs += [pl.BlockSpec((tile, weight.shape[1]), lambda t: (t, 0)) for _, _, weight in pairs]
    in_specs += [whole, pl.BlockSpec((1, width), lambda t: (0, 0))]
    if base is not None:
        operands.append(base)
        in_specs.append(whole)
    return call(
        functools.partial(norm_back_kernel, pairs=len(pairs)),
        operands,
        in_specs,
        [whole, pl.BlockSpec((2, width), lambda t: (0, 0))],
        [jax.ShapeDtypeStruct((rows, width), F32), jax.ShapeDtypeStruct((2, width), F32)],
        (width // tile,),
        after,
        scratch=[pltpu.VMEM((rows, width), F32)],
    )


def plain_kernel(left, weight, *refs, dims):
    total = mm(left[...], weight[...], dims)
    for term in refs[:-1]:
        total = total + term[...].astype(F32)
    refs[-1][...] = total.astype(refs[-1].dtype)


def plain_product(left, place, rows, weight, dims, terms, after=(), kind=BF16):
    tile = 512
    if dims is NT:
        width = weight.shape[0]
        weights = pl.BlockSpec((tile, weight.shape[1]), lambda t: (t, 0))
    else:
        width = weight.shape[1]
        weights = pl.BlockSpec((weight.shape[0], tile), lambda t: (0, t))
    columns = pl.BlockSpec((rows, tile), lambda t: (0, t))
    return call(
        functools.partial(plain_kernel, dims=dims),
        [left, weight, *terms],
        [pl.BlockSpec((rows, left.shape[1]), lambda t: (place, 0), pipeline_mode=pl.Buffered(1)), weights]
        + [columns] * len(terms),
        columns,
        jax.ShapeDtypeStruct((rows, width), kind),
        (width // tile,),
        after,
    )


def both_kernel(left, weight, own, other):
    half = left.shape[0] // 2
    other[...] = mm(left[half:, :], weight[...], NT).astype(other.dtype)
    own[...] = mm(left[:half, :], weight[...], NT)


def both_product(left, weight, after):
    rows, depth = left.shape
    width = weight.shape[0]
    tile = 512
    columns = pl.BlockSpec((rows // 2, tile), lambda t: (0, t))
    return call(
        both_kernel,
        [left, weight],
        [
            pl.BlockSpec((rows, depth), lambda t: (0, 0), pipeline_mode=pl.Buffered(1)),
            pl.BlockSpec((tile, depth), lambda t: (t, 0)),
        ],
        [columns, columns],
        [jax.ShapeDtypeStruct((rows // 2, width), kind) for kind in (F32, BF16)],
        (width // tile,),
        after,
    )


def added(left, right, after):
    def kernel(a, b, out):
        out[...] = a[...] + b[...]

    whole = pl.BlockSpec(left.shape, lambda t: (0, 0))
    return call(kernel, [left, right], [whole] * 2, whole, jax.ShapeDtypeStruct(left.shape, left.dtype), (1,), after)


def stacked_rows(parts, after):
    def kernel(*refs):
        start = 0
        for ref in refs[:-1]:
            refs[-1][start : start + ref.shape[0], :] = ref[...]
            start += ref.shape[0]

    rows, width = sum(part.shape[0] for part in parts), parts[0].shape[1]
    specs = [pl.BlockSpec(part.shape, lambda t: (0, 0)) for part in parts]
    out = pl.BlockSpec((rows, width), lambda t: (0, 0))
    return call(kernel, parts, specs, out, jax.ShapeDtypeStruct((rows, width), F32), (1,), after)


def last_sum_kernel(index, *refs, segments, cuts):
    outs = refs[-len(cuts) :]
    column = 0
    for width, terms in segments:
        total = None
        for ref, start in terms:
            value = refs[ref][..., start : start + width]
            value = value.reshape(value.shape[-2:]).astype(F32)
            total = value if total is None else total + value
        past = 0
        for out, cut in zip(outs, cuts):
            low, high = max(past, column), min(past + cut, column + width)
            if low < high:
                out[:, low - past : high - past] = total[:, low - column : high - column]
            past += cut
        column += width


def sum_kernel(index, *refs, segments):
    out = refs[-1]
    column = 0
    for width, terms in segments:
        values = [refs[ref][..., start : start + width] for ref, start in terms]
        values = [value.reshape(-1, *value.shape[-2:]) for value in values]
        if len(values) > 2:
            values = [value.astype(F32) for value in values]
        total = functools.reduce(jnp.add, values).astype(out.dtype)
        out[..., column : column + width] = total.reshape(*out.shape[:-1], width)
        column += width


class Segment:
    def __init__(self, width, arrays, taken):
        self.width = width
        self.taken = list(taken)
        self.terms = [(a, len(taken), 0) for a in arrays]


class Chain:
    def __init__(self, index, bits, sizes, first=None):
        self.index = index
        self.sizes = sizes
        self.left = sorted(bits)
        self.taken = [] if first is None else [(self.left.index(first), first)]
        if first is not None:
            self.left.remove(first)
        self.segments = []

    def add(self, width, arrays):
        self.segments.append(Segment(width, arrays, self.taken))

    def join(self, other):
        self.segments += other.segments

    def _sum(self, bit, after, cuts=None):
        free = [b for b in sorted(self.left)[::-1] if b != bit]
        arrays, homes, segments = [], [], []
        for segment in self.segments:
            listed = []
            for array, level, start in segment.terms:
                home = sorted(self.left + [b for _, b in segment.taken[level:]])[::-1]
                known = [n for n, a in enumerate(arrays) if a is array and homes[n] == home]
                if not known:
                    arrays.append(array)
                    homes.append(home)
                    known = [len(arrays) - 1]
                listed.append((known[0], start))
            segments.append((segment.width, listed))
        rows = arrays[0].shape[1]
        total = sum(segment.width for segment in self.segments)
        steps = 0
        while steps < len(free) and (rows * total * 2 << (len(free) - steps)) > STEP_BYTES:
            steps += 1
        grid = (2,) * steps if steps else (1,)

        def spec(home, width):
            shape = tuple(2 if b in free[steps:] else 1 for b in home)

            def at(*step_and_index):
                index = step_and_index[-1]
                place = []
                for b in home:
                    if b == bit:
                        place.append(1 - ((index[0] >> b) & 1))
                    elif b in free:
                        place.append(step_and_index[free.index(b)] if b in free[:steps] else 0)
                    else:
                        place.append((index[0] >> b) & 1)
                return (*place, 0, 0)

            return pl.BlockSpec((*shape, rows, width), at)

        operands = [self.index] + [a.reshape((2,) * len(home) + a.shape[1:]) for a, home in zip(arrays, homes)]
        in_specs = [spec(home, a.shape[2]) for a, home in zip(arrays, homes)]
        if cuts is not None:
            return call(
                functools.partial(last_sum_kernel, segments=segments, cuts=cuts),
                operands,
                in_specs,
                [pl.BlockSpec((rows, cut), lambda t, i: (0, 0)) for cut in cuts],
                [jax.ShapeDtypeStruct((rows, cut), F32) for cut in cuts],
                grid,
                after,
                1,
            )
        result = call(
            functools.partial(sum_kernel, segments=segments),
            operands,
            in_specs,
            spec(free, total),
            jax.ShapeDtypeStruct((2,) * len(free) + (rows, total), BF16),
            grid,
            after,
            1,
        )
        return result.reshape(-1, rows, total)

    def pack(self, bit, after=()):
        return self._sum(bit, after)

    def travel(self, packed, bit):
        got = lax.ppermute(packed, "dp", [(i, i ^ (1 << bit)) for i in range(self.sizes["dp"])])
        step = (self.left.index(bit), bit)
        self.left.remove(bit)
        start = 0
        for segment in self.segments:
            segment.taken.append(step)
            segment.terms.append((got, len(segment.taken), start))
            start += segment.width
        return got

    def finish(self, cuts, after=()):
        for bit in list(self.left):
            self.travel(self.pack(bit), bit)
        return self._sum(None, after, cuts)


def bit_orders(count):
    bits = count.bit_length() - 1
    if bits == 4:
        return [(0, 1, 2, 3), (1, 0, 2, 3), (2, 3, 0, 1)]
    plain = tuple(range(bits))
    third = bits // 3
    return [plain, (1, 0) + plain[2:], plain[2 * third :] + plain[: 2 * third]]


def sided(value, bit, bits, side):
    place = bits.index(bit)
    shape = value.shape
    outer = 1 << place
    parts = value.reshape((outer, 2, shape[0] // (2 * outer)) + shape[1:])
    return lax.dynamic_index_in_dim(parts, side, 1, keepdims=False).reshape((shape[0] // 2,) + shape[1:])


def build(dp_size, mp_size):
    plain, swapped, last = bit_orders(dp_size)
    sizes = {"dp": dp_size, "mp": mp_size}
    all_bits = sorted(plain)

    def swap(value):
        return lax.ppermute(value, "mp", [(i, i ^ 1) for i in range(mp_size)])

    def local(
        media_feats,
        latents,
        patch_counts,
        cotangent,
        query_weight,
        key_weight,
        value_weight,
        out_weight,
        up_weight,
        down_weight,
        media_gain,
        media_shift,
        latent_gain,
        latent_shift,
        feed_gain,
        feed_shift,
    ):
        micro, patches, width = media_feats.shape
        dp_index = lax.axis_index("dp").astype(jnp.int32)
        mp_index = lax.axis_index("mp").astype(jnp.int32)
        flat_index = dp_index * mp_size + mp_index
        dp_list = dp_index.reshape(1)
        mp_list = mp_index.reshape(1)

        def first_step(grads, bit):
            if len(grads) == 2:
                return grads
            parted = grads[0].reshape(dp_size, width // dp_size, -1)
            mine = (dp_index >> bit) & 1
            return sided(parted, bit, all_bits[::-1], 1 - mine), sided(parted, bit, all_bits[::-1], mine)

        def sent_first(grads, bit):
            rear, front = first_step(grads, bit)
            return front, lax.ppermute(rear, "dp", [(i, i ^ (1 << bit)) for i in range(dp_size)])

        def paired(grads):
            if len(grads) == 1:
                parted = grads[0].reshape(dp_size, mp_size, -1, grads[0].shape[1])
                grads = [lax.dynamic_index_in_dim(parted, side, 1, keepdims=False) for side in (1 - mp_index, mp_index)]
            rear, front = grads
            return front, swap(rear)

        grad_own = cotangent.reshape(-1, width)
        grad_other = swap(grad_own)
        media_full = media_feats.reshape(-1, width).astype(F32)
        latents_full = latents.reshape(-1, width).astype(F32)
        media_n, media_hat, media_inv = normalize(media_full, media_gain, media_shift)
        latent_n, latent_hat, latent_inv = normalize(latents_full, latent_gain, latent_shift)
        latent_low = latent_n.astype(BF16)
        both_low = jnp.concatenate([media_n.astype(BF16), latent_low])
        queries = low_mm(latent_low, query_weight)
        keys = low_mm(both_low, key_weight).reshape(2, -1, width)
        values = low_mm(both_low, value_weight).reshape(2, -1, width)
        own = latent_low.shape[0]
        mixed_low, log_norm = attention_call(
            attend_kernel, patch_counts, queries, keys, values, [], ["one", "norm"], (grad_other,)
        )
        residual = latents_full + mm(mixed_low, out_weight)
        feed_in, feed_hat, feed_inv = normalize(residual, feed_gain, feed_shift)
        feed_own = feed_in.astype(BF16)
        feed_other = swap(feed_own)

        tile = 512
        tiles = up_weight.shape[1] // tile
        third = tiles // 6
        first = tiles // 2 - third
        second = tiles - first - third
        rows_in = [feed_own, feed_other, grad_own, grad_other]
        splittable = width // dp_size % ROW_TILE == 0

        along = Chain(dp_list, all_bits, sizes, plain[0])
        across = Chain(dp_list, all_bits, sizes, swapped[0])
        far = Chain(dp_list, all_bits, sizes, last[0])
        grads, units = feed_part(
            dp_list, rows_in, up_weight, down_weight, 0, third + first, tile, None, (plain[0], swapped[0]), last[0], dp_size
        )
        if splittable:
            far_1, down_1, up_1 = grads[:2], grads[2:4], grads[4:]
        else:
            far_1 = [jnp.concatenate([g[:, : third * tile] for g in grads], 1)]
            down_1, up_1 = ([g[:, third * tile :]] for g in grads)
        along.add(first * tile, sent_first(down_1, plain[0]))
        across.add(first * tile, sent_first(up_1, swapped[0]))
        far.add(2 * third * tile, sent_first(far_1, last[0]))
        part_got = [chain.segments[0].terms[1][0] for chain in (along, across, far)]
        grads, units = feed_part(
            dp_list,
            rows_in,
            up_weight,
            down_weight,
            third + first,
            second,
            tile,
            units,
            (swapped[0], plain[0]),
            None,
            dp_size,
        )
        down_2, up_2 = (grads[:2], grads[2:]) if splittable else (grads[:1], grads[1:])
        across.add(second * tile, sent_first(down_2, swapped[0]))
        along.add(second * tile, sent_first(up_2, plain[0]))
        hidden, grad_up = units
        feed_back, feed_back_other = both_product(grad_up, up_weight, part_got)
        feed_back_got = swap(feed_back_other)
        far_packed = far.pack(last[1], (feed_back_other,))
        far_got = far.travel(far_packed, last[1])
        grad_residual, grad_residual_low, grad_mixed, feed_sums = feed_norm_back(
            feed_back, feed_back_got, residual, grad_own, feed_gain, out_weight, (far_packed,)
        )
        blocks = dp_size * mp_size
        half = width // 2
        stackable = width // blocks % ROW_TILE == 0
        token = [grad_residual]

        def now():
            return tuple(token)

        def ran(value):
            token[:] = [value]

        def wait(*values):
            token.extend(values)

        def move(chain, bit):
            packed = chain.pack(bit, now())
            ran(packed)
            return chain.travel(packed, bit)

        def end(chain, *cuts):
            totals = chain.finish(cuts, now())
            ran(totals[0])
            return totals

        def join(*chains):
            joined = Chain(dp_list, chains[0].left, sizes)
            for chain in chains:
                joined.join(chain)
            return joined

        def attend_back(start, count, before):
            made = attention_call(
                attend_back_kernel,
                patch_counts,
                queries,
                keys,
                values,
                [("one", grad_mixed), ("norm", log_norm)],
                ["one", "two", "two"],
                now(),
                start,
                count,
                before,
            )
            ran(made[0])
            return made

        out_grads = product(mp_list, [grad_residual_low], [(0, mixed_low, 0, 2)], blocks, now(), stackable)
        ran(out_grads[0])
        outs = Chain(dp_list, all_bits, sizes)
        out_pair = paired(out_grads)
        outs.add(out_pair[0].shape[-1], out_pair)
        made = attend_back(0, micro // 2, ())
        move(along, plain[1])
        move(across, swapped[1])
        wait(far_got)
        move(outs, last[0])
        grad_queries, grad_keys, grad_values = attend_back(micro // 2, micro - micro // 2, made)
        grad_keys = grad_keys.reshape(-1, width)
        grad_values = grad_values.reshape(-1, width)
        key_grads = product(
            mp_list, [both_low], [(0, grad_keys, 0, 2), (0, grad_queries, 0, 1)], blocks, now()
        )
        keyed = Chain(dp_list, all_bits, sizes)
        keyed.add(width + half, paired(key_grads))
        ran(key_grads[0])
        outs_got = move(outs, last[1])
        if stackable:
            far.join(outs)
        move(keyed, plain[0])
        value_grads = product(
            mp_list, [both_low], [(0, grad_values, 0, 2), (0, grad_queries, 1, 1)], blocks, now()
        )
        valued = Chain(dp_list, all_bits, sizes)
        valued.add(width + half, paired(value_grads))
        ran(value_grads[0])
        both = join(along, across)
        move(both, plain[2])
        move(valued, swapped[0])
        grad_latents, latent_sums = norm_back_product(
            [(grad_queries, 0, query_weight), (grad_keys, 1, key_weight), (grad_values, 1, value_weight)],
            latents.reshape(-1, width),
            grad_residual,
            latent_gain,
            now(),
        )
        ran(grad_latents)
        move(keyed, plain[1])
        grad_media, media_sums = norm_back_product(
            [(grad_keys, 0, key_weight), (grad_values, 0, value_weight)],
            media_feats.reshape(-1, width),
            None,
            media_gain,
            now(),
        )
        ran(grad_media)
        wait(outs_got)
        move(both, plain[3])
        move(valued, swapped[1])
        branch_other = plain_product(hidden, 1, own, down_weight, NN, [], now())
        ran(branch_other)
        branch_got = swap(branch_other)
        move(keyed, plain[2])
        result = plain_product(hidden, 0, own, down_weight, NN, [residual, branch_got], now())
        ran(result)
        sums = stacked_rows([media_sums, latent_sums, feed_sums], now())
        ran(sums)
        arrived = swap(sums)

        def move_sums(bit):
            total = added(sums, arrived, now())
            ran(total)
            return total, None if bit is None else lax.ppermute(total, "dp", [(i, i ^ (1 << bit)) for i in range(dp_size)])

        move(far, last[2])
        sums, arrived = move_sums(plain[0])
        move(valued, swapped[2])
        sums, arrived = move_sums(plain[1])
        move(keyed, plain[3])
        sums, arrived = move_sums(plain[2])
        move(valued, swapped[3])
        sums, arrived = move_sums(plain[3])
        edge = third * tile
        along_down, along_up, across_up, across_down = end(both, first * tile, second * tile, first * tile, second * tile)
        for bit in plain[4:]:
            sums, arrived = move_sums(bit)
            ran(sums)
        move(far, last[3])
        sums, _ = move_sums(None)
        if stackable:
            far_down, far_up, out_rows = end(far, edge, edge, half)
            out_sum = jnp.concatenate([out_rows[: out_rows.shape[0] // 2], out_rows[out_rows.shape[0] // 2 :]], 1)
        else:
            far_down, far_up = end(far, edge, edge)
            (out_sum,) = end(outs, width)
        key_sum, query_sum = end(keyed, width, half)
        value_sum, query_rest = end(valued, width, half)
        grad_down_t = jnp.concatenate([far_down, along_down, across_down], 1)
        grad_up_w = jnp.concatenate([far_up, across_up, along_up], 1)
        share = width // blocks
        sums = lax.dynamic_slice(sums, (0, flat_index * share), (sums.shape[0], share))
        return (
            result.reshape(latents.shape),
            grad_latents.reshape(latents.shape),
            grad_media.reshape(media_feats.shape),
            jnp.concatenate([query_sum, query_rest], 1),
            key_sum,
            value_sum,
            out_sum.T,
            grad_up_w,
            grad_down_t.T,
            *[sums[i] for i in range(sums.shape[0])],
        )

    return local


def solution(mesh):
    rows = P(None, ("dp", "mp"), None)
    in_specs = (rows, rows, P(None, ("dp", "mp")), rows, P(), P(), P(), P(), P(None, "mp"), P("mp", None)) + (P(),) * 6
    first = P(("dp", "mp"), None)
    out_specs = (rows, rows, rows, first, first, first, P(None, ("dp", "mp")), P("dp", "mp"), P("mp", "dp")) + (
        P(("dp", "mp")),
    ) * 6
    local = build(mesh.shape["dp"], mesh.shape["mp"])
    return jax.shard_map(local, mesh=mesh, in_specs=in_specs, out_specs=out_specs, check_vma=False)
```

```python
import functools

import jax
import jax.numpy as jnp
from jax import lax
from jax.experimental import pallas as pl
from jax.experimental.pallas import tpu as pltpu
from jax.sharding import PartitionSpec as P

HEADS = 16
LAT_IMG = 64
EPSILON = 1e-05
MASKED_SCORE = -1e30
ROOT_HALF = 0.7071067811865476
DENSITY_SCALE = 0.3989422804014327
F32 = jnp.float32
BF16 = jnp.bfloat16
NN = (((1,), (0,)), ((), ()))
NT = (((1,), (1,)), ((), ()))
TN = (((0,), (0,)), ((), ()))
MIB = 1024 * 1024
ROW_TILE = 16
STEP_BYTES = 1200000
LONG = pl.CostEstimate(flops=10**12, bytes_accessed=10**10, transcendentals=0)


def mm(left, right, dims=NN):
    return lax.dot_general(left, right, dims, preferred_element_type=F32)


def low_mm(left, right):
    return mm(left, right).astype(BF16)


def normalize(values, gain_vec, shift_vec):
    row_mean = jnp.mean(values, -1, keepdims=True)
    centred = values - row_mean
    inv_scale = lax.rsqrt(jnp.mean(centred * centred, -1, keepdims=True) + EPSILON)
    scaled = centred * inv_scale
    return (scaled * gain_vec + shift_vec, scaled, inv_scale)


def mask_biases(counts, step, keys, lats, pair):
    lane = lax.broadcasted_iota(jnp.int32, (1, lats), 1) // LAT_IMG
    first = jnp.zeros((1, lats), jnp.int32)
    past = jnp.zeros((1, lats), jnp.int32)
    total = jnp.int32(0)
    for i in range(counts.shape[1]):
        after = total + counts[step, i]
        first = jnp.where(lane == i, total, first)
        past = jnp.where(lane == i, after, past)
        total = after
    place = lax.broadcasted_iota(jnp.int32, (keys, lats), 0)
    media = jnp.where((place >= first) & (place < past), 0.0, MASKED_SCORE)
    key_image = lax.broadcasted_iota(jnp.int32, (pair, pair), 0) // LAT_IMG
    latent_image = lax.broadcasted_iota(jnp.int32, (pair, pair), 1) // LAT_IMG
    return media, jnp.where(key_image == latent_image, 0.0, MASKED_SCORE)


def spans(total, size):
    return [slice(start, start + size) for start in range(0, total, size)]


def attend_kernel(
    counts, q, k, v, latents, weight, norms, mixed, norm, residual, feed, whole, *, start, heads, dim, pair
):
    scale = dim**-0.5
    lats = q.shape[0]
    bias_m, bias_l = mask_biases(counts, start + pl.program_id(0), k.shape[1], lats, pair)
    pairs = spans(lats, pair)
    columns = spans(heads * dim, dim)
    vm = v[0].T
    vl = v[1].T
    qs = [q[:, c] for c in columns]
    kl = [k[1, :, c] for c in columns]
    s_m = [mm(k[0, :, c], x, NT) * scale + bias_m for c, x in zip(columns, qs)]
    s_l = [jnp.concatenate([mm(y[p], x[p], NT) * scale + bias_l for p in pairs], 1) for y, x in zip(kl, qs)]
    top = [jnp.maximum(jnp.max(x, 0, keepdims=True), jnp.max(y, 0, keepdims=True)) for x, y in zip(s_m, s_l)]
    e_m = [jnp.exp(x - t) for x, t in zip(s_m, top)]
    e_l = [jnp.exp(x - t) for x, t in zip(s_l, top)]
    total = [jnp.sum(x, 0, keepdims=True) + jnp.sum(y, 0, keepdims=True) for x, y in zip(e_m, e_l)]
    inverse = [1.0 / t for t in total]
    p_m = [(x * i).astype(BF16) for x, i in zip(e_m, inverse)]
    p_l = [(x * i).astype(BF16) for x, i in zip(e_l, inverse)]
    outs = []
    for x, y, c in zip(p_m, p_l, columns):
        latent_part = jnp.concatenate([mm(vl[c, p], y[:, p]) for p in pairs], 1)
        outs.append((mm(vm[c, :], x) + latent_part).astype(BF16))
    norm[0, 0, :, :] = jnp.concatenate([t + jnp.log(x) for t, x in zip(top, total)], 0)
    low = jnp.concatenate(outs, 0).T
    mixed[...] = low
    group = pl.program_id(1)
    for g in range(whole.shape[0]):

        @pl.when(group == g)
        def _(g=g):
            whole[g] = low

    @pl.when(group == whole.shape[0] - 1)
    def _():
        total = latents[...].astype(F32)
        for g in range(whole.shape[0]):
            total = total + mm(whole[g], weight[g * heads * dim : (g + 1) * heads * dim, :])
        residual[...] = total
        feed[...] = normalize(total, norms[4:5, :], norms[5:6, :])[0].astype(BF16)


def attend_back_kernel(counts, q, k, v, grad_mixed, norm, *refs, start, heads, dim, pair):
    grad_q, grad_k, grad_v = refs[-3:]
    scale = dim**-0.5
    lats = q.shape[0]
    bias_m, bias_l = mask_biases(counts, start + pl.program_id(0), k.shape[1], lats, pair)
    pairs = spans(lats, pair)
    turned_m = k[0].T
    turned_l = k[1].T
    grad_qs = []
    for some in spans(heads, 4):
        columns = spans(heads * dim, dim)[some]
        group = slice(some.start * dim, some.stop * dim)
        qs = [q[:, c] for c in columns]
        gs = [grad_mixed[:, c] for c in columns]
        kl = [k[1, :, c] for c in columns]
        vl = [v[1, :, c] for c in columns]
        norms = [norm[0, 0, j : j + 1, :] for j in range(some.start, some.stop)]
        p_m = [jnp.exp(mm(k[0, :, c], y, NT) * scale + bias_m - n) for c, y, n in zip(columns, qs, norms)]
        s_l = [jnp.concatenate([mm(x[p], y[p], NT) * scale + bias_l for p in pairs], 1) for x, y in zip(kl, qs)]
        p_l = [jnp.exp(x - n) for x, n in zip(s_l, norms)]
        d_m = [mm(v[0, :, c], g, NT) for c, g in zip(columns, gs)]
        d_l = [jnp.concatenate([mm(x[p], g[p], NT) for p in pairs], 1) for x, g in zip(vl, gs)]
        means = [
            jnp.sum(x * y, 0, keepdims=True) + jnp.sum(z * w, 0, keepdims=True)
            for x, y, z, w in zip(d_m, p_m, d_l, p_l)
        ]
        g_m = [(x * (y - n)).astype(BF16) for x, y, n in zip(p_m, d_m, means)]
        g_l = [(x * (y - n)).astype(BF16) for x, y, n in zip(p_l, d_l, means)]
        p_m = [x.astype(BF16) for x in p_m]
        p_l = [x.astype(BF16) for x in p_l]
        grad_v[0, :, group] = jnp.concatenate([mm(x, g).astype(BF16) for x, g in zip(p_m, gs)], 1)
        grad_k[0, :, group] = jnp.concatenate([(mm(x, y) * scale).astype(BF16) for x, y in zip(g_m, qs)], 1)
        for p in pairs:
            grad_v[1, p, group] = jnp.concatenate([mm(x[:, p], g[p]).astype(BF16) for x, g in zip(p_l, gs)], 1)
            grad_k[1, p, group] = jnp.concatenate([(mm(x[:, p], y[p]) * scale).astype(BF16) for x, y in zip(g_l, qs)], 1)
        for c, x, z in zip(columns, g_m, g_l):
            latent_part = jnp.concatenate([mm(turned_l[c, p], z[:, p]) for p in pairs], 1)
            grad_qs.append(((mm(turned_m[c, :], x) + latent_part) * scale).astype(BF16))
    grad_q[...] = jnp.concatenate(grad_qs, 0).T


def call(kernel, operands, in_specs, out_specs, out_shape, grid, after=(), scalars=0, scratch=(), aliases=None):
    given = len(operands)

    def body(*refs):
        kernel(*refs[:given], *refs[given + len(after) :])

    return pl.pallas_call(
        body,
        grid_spec=pltpu.PrefetchScalarGridSpec(
            num_scalar_prefetch=scalars,
            grid=grid,
            in_specs=list(in_specs) + [pl.BlockSpec(memory_space=pl.ANY)] * len(after),
            out_specs=out_specs,
            scratch_shapes=list(scratch),
        ),
        out_shape=out_shape,
        input_output_aliases=aliases or {},
        compiler_params=pltpu.CompilerParams(vmem_limit_bytes=60 * MIB),
        cost_estimate=LONG,
    )(*operands, *after)


def marker(number, source):
    def kernel(target):
        pass

    anywhere = pl.BlockSpec(memory_space=pl.ANY)
    return call(kernel, [], [], anywhere, jax.ShapeDtypeStruct((8, 128 * number), F32), (1,), (source,))


def project_kernel(media, latents, norms, query, key, value, both, queries, keys, values):
    rows = media.shape[0]

    def products(side, r, low):
        keys[side, r, :] = mm(low, key[...]).astype(BF16)
        values[side, r, :] = mm(low, value[...]).astype(BF16)
        if side:
            queries[r, :] = mm(low, query[...]).astype(BF16)

    @pl.when(pl.program_id(0) == 0)
    def _():
        for side, source in enumerate((media, latents)):
            gain, shift = norms[2 * side : 2 * side + 1, :], norms[2 * side + 1 : 2 * side + 2, :]
            for r in spans(rows, rows // 2):
                low = normalize(source[r, :].astype(F32), gain, shift)[0].astype(BF16)
                both[side * rows + r.start : side * rows + r.stop, :] = low
                products(side, r, low)

    @pl.when(pl.program_id(0) > 0)
    def _():
        for side in range(2):
            products(side, slice(0, rows), both[side * rows : (side + 1) * rows, :])


def project(media, latents, norms, query, key, value):
    rows, width = latents.shape
    tile = 512
    whole = pl.BlockSpec((rows, width), lambda t: (0, 0), pipeline_mode=pl.Buffered(1))
    weight = pl.BlockSpec((width, tile), lambda t: (0, t))
    two = jax.ShapeDtypeStruct((2, rows, width), BF16)
    return call(
        project_kernel,
        [media, latents, norms, query, key, value],
        [whole, whole, pl.BlockSpec(norms.shape, lambda t: (0, 0)), weight, weight, weight],
        [
            pl.BlockSpec((2 * rows, width), lambda t: (0, 0), pipeline_mode=pl.Buffered(1)),
            pl.BlockSpec((rows, tile), lambda t: (0, t)),
            pl.BlockSpec((2, rows, tile), lambda t: (0, 0, t)),
            pl.BlockSpec((2, rows, tile), lambda t: (0, 0, t)),
        ],
        [jax.ShapeDtypeStruct((2 * rows, width), BF16), jax.ShapeDtypeStruct((rows, width), BF16), two, two],
        (width // tile,),
    )


def attention_call(kernel, counts, queries, keys, values, more, outs, after=(), start=0, count=None, before=(), fixed=(), scratch=0):
    micro = counts.shape[0]
    rows = queries.shape[0] // micro
    width = queries.shape[1]
    groups = 2
    heads = HEADS // groups
    group = width // groups
    one = pl.BlockSpec((rows, group), lambda m, g: (start + m, g))
    two = pl.BlockSpec((2, rows, group), lambda m, g: (0, start + m, g))
    norm = pl.BlockSpec((1, 1, heads, rows), lambda m, g: (start + m, g, 0, 0))
    kinds = {
        "one": (one, jax.ShapeDtypeStruct(queries.shape, BF16)),
        "two": (two, jax.ShapeDtypeStruct(keys.shape, BF16)),
        "norm": (norm, jax.ShapeDtypeStruct((micro, groups, heads, rows), F32)),
        "row": (pl.BlockSpec((rows, width), lambda m, g: (start + m, 0)), jax.ShapeDtypeStruct(queries.shape, BF16)),
        "long": (pl.BlockSpec((rows, width), lambda m, g: (start + m, 0)), jax.ShapeDtypeStruct(queries.shape, F32)),
    }
    operands = [counts, queries, keys, values] + [value for _, value in more]
    in_specs = [pl.BlockSpec(memory_space=pltpu.SMEM), one, two, two] + [kinds[kind][0] for kind, _ in more]
    operands += fixed
    in_specs += [pl.BlockSpec(f.shape, lambda m, g: (0, 0), pipeline_mode=pl.Buffered(1)) for f in fixed]
    return call(
        functools.partial(kernel, start=start, heads=heads, dim=width // HEADS, pair=2 * LAT_IMG),
        operands + list(before),
        in_specs + [pl.BlockSpec(memory_space=pl.ANY)] * len(before),
        [kinds[kind][0] for kind in outs],
        [kinds[kind][1] for kind in outs],
        (micro if count is None else count, groups),
        after,
        scratch=[pltpu.VMEM((groups, rows, group), BF16)] * scratch,
        aliases={len(operands) + n: n for n in range(len(before))},
    )


def split_rows(whole, rear_ref, front_ref, block_rows, first_bit, mine):
    for i in range(rear_ref.shape[0]):
        low = i & ((1 << first_bit) - 1)
        base = ((i >> first_bit) << (first_bit + 1)) | low
        for ref, side in ((rear_ref, 1 - mine), (front_ref, mine)):
            block = base + side * (1 << first_bit)
            rows = pl.ds(pl.multiple_of(block * block_rows, block_rows), block_rows)
            ref[i, :, :] = whole[rows, :]


def feed_kernel(index, feed_own, feed_other, cot_own, cot_other, up, down, *refs, kept, bits, far, block_rows):
    refs = refs[kept:]
    half, width = feed_own.shape
    tile = up.shape[1]
    if bits is None:
        grad_down, grad_up_w, hidden, grad_up, feed, cot = refs
    else:
        *sides, hidden, grad_up, feed, cot, grad_down, grad_up_w = refs

    @pl.when(pl.program_id(0) == 0)
    def _():
        for whole, parts in ((feed, (feed_own, feed_other)), (cot, (cot_own, cot_other))):
            for n, part in enumerate(parts):
                whole[n * half : (n + 1) * half, :] = part[...]

    for r in spans(2 * half, half):
        u = mm(feed[r, :], up[...])
        grad_hidden = mm(cot[r, :], down[...], NT)
        cdf = 0.5 * (1.0 + lax.erf(u * ROOT_HALF))
        pdf = jnp.exp(-0.5 * u * u) * DENSITY_SCALE
        hidden[r, :] = (u * cdf).astype(BF16)
        grad_up[r, :] = (grad_hidden * (cdf + u * pdf)).astype(BF16)
    for r in spans(width, width // 2):
        grad_down[r, :] = mm(cot[:, r], hidden[...], TN).astype(BF16)
        grad_up_w[r, :] = mm(feed[:, r], grad_up[...], TN).astype(BF16)
    if bits is None:
        return

    def split(whole, rear, front, bit):
        split_rows(whole, rear, front, block_rows, bit, (index[0] >> bit) & 1)

    def near():
        split(grad_down, *sides[-4:-2], bits[0])
        split(grad_up_w, *sides[-2:], bits[1])

    if far is None:
        near()
    else:
        step = pl.program_id(0)
        pl.when(step > 0)(near)

        @pl.when(step == 0)
        def _():
            rear, front = sides[:2]
            split(grad_down, rear.at[:, :, :tile], front.at[:, :, :tile], far)
            split(grad_up_w, rear.at[:, :, tile:], front.at[:, :, tile:], far)


def feed_part(index, rows_in, up, down, start, tiles, tile, before, bits, far, blocks):
    half, width = rows_in[0].shape
    block_rows = width // blocks
    whole = pl.BlockSpec((half, width), lambda t, i: (0, 0), pipeline_mode=pl.Buffered(1))
    units = pl.BlockSpec((2 * half, tile), lambda t, i: (0, start + t))
    unit_shape = jax.ShapeDtypeStruct((2 * half, up.shape[1]), BF16)
    kept = [] if before is None else list(before)
    split = block_rows % ROW_TILE == 0
    if split:
        apart = 0 if far is None else 1
        shape = (blocks // 2, block_rows)
        grads = [pl.BlockSpec((*shape, 2 * tile), lambda t, i: (0, 0, 0), pipeline_mode=pl.Buffered(1))] * (2 * apart)
        shapes = [jax.ShapeDtypeStruct((*shape, 2 * tile), BF16)] * (2 * apart)
        grads += [pl.BlockSpec((*shape, tile), lambda t, i: (0, 0, jnp.maximum(t - apart, 0)))] * 4
        shapes += [jax.ShapeDtypeStruct((*shape, (tiles - apart) * tile), BF16)] * 4
        scratch = [pltpu.VMEM((2 * half, width), BF16)] * 2 + [pltpu.VMEM((width, tile), BF16)] * 2
    else:
        grads = [pl.BlockSpec((width, tile), lambda t, i: (0, t))] * 2
        shapes = [jax.ShapeDtypeStruct((width, tiles * tile), BF16)] * 2
        scratch = [pltpu.VMEM((2 * half, width), BF16)] * 2
    first = len(shapes)
    anywhere = pl.BlockSpec(memory_space=pl.ANY)
    results = call(
        functools.partial(
            feed_kernel, kept=len(kept), bits=bits if split else None, far=far if split else None, block_rows=block_rows
        ),
        [index, *rows_in, up, down, *kept],
        [
            whole,
            whole,
            whole,
            whole,
            pl.BlockSpec((width, tile), lambda t, i: (0, start + t)),
            pl.BlockSpec((tile, width), lambda t, i: (start + t, 0)),
        ]
        + [anywhere] * len(kept),
        grads + [units, units],
        shapes + [unit_shape, unit_shape],
        (tiles,),
        (),
        1,
        scratch,
        {7: first, 8: first + 1} if kept else {},
    )
    return results[:-2], results[-2:]


def product_kernel(index, *refs, lefts, parts, block_rows, split):
    step = pl.program_id(0)
    target = refs[-1]
    rights = refs[lefts : lefts + len(parts)]
    for (place, first, past), right in zip(parts, rights):

        @pl.when((step >= first) & (step < past))
        def _(left=refs[place], right=right):
            skipped = left.shape[0] - right.shape[0]
            target[...] = mm(left[skipped:, :], right[...], TN).astype(BF16)

    if split:
        split_rows(target, refs[-3], refs[-2], block_rows, 0, index[0] & 1)


def product(index, lefts, parts, blocks, after, stacked=False):
    width = lefts[0].shape[1]
    block_rows = width // blocks
    tile = width // 2
    split = block_rows % ROW_TILE == 0
    in_specs = [pl.BlockSpec(left.shape, lambda t, i: (0, 0), pipeline_mode=pl.Buffered(1)) for left in lefts]
    steps = []
    start = 0
    for place, right, first, count in parts:

        def at(t, i, first=first, start=start, count=count):
            return (0, first + jnp.clip(t - start, 0, count - 1))

        in_specs.append(pl.BlockSpec((right.shape[0], tile), at))
        steps.append((place, start, start + count))
        start += count
    if split:
        place = (lambda t, i: (0, t, 0)) if stacked else (lambda t, i: (0, 0, t))
        shape = (block_rows * start, tile) if stacked else (block_rows, tile * start)
        out_specs = [pl.BlockSpec((blocks // 2, block_rows, tile), place)] * 2
        out_shape = [jax.ShapeDtypeStruct((blocks // 2, *shape), BF16)] * 2
        scratch = [pltpu.VMEM((width, tile), BF16)]
    else:
        out_specs = [pl.BlockSpec((width, tile), lambda t, i: (0, t))]
        out_shape = [jax.ShapeDtypeStruct((width, tile * start), BF16)]
        scratch = []
    kernel = functools.partial(product_kernel, lefts=len(lefts), parts=steps, block_rows=block_rows, split=split)
    operands = [index, *lefts] + [right for _, right, _, _ in parts]
    return call(kernel, operands, in_specs, out_specs, out_shape, (start,), after, 1, scratch)


def feed_norm_back_kernel(own, other, source, base, norms, weight, out, out_low, mixed_low, sums):
    gain = norms[4:5, :]
    e = own[...] + other[...].astype(F32)
    _, hat, inverse = normalize(source[...], gain, 0.0)
    weighted = e * gain
    first_mean = jnp.mean(weighted, -1, keepdims=True)
    second_mean = jnp.mean(weighted * hat, -1, keepdims=True)
    grad = base[...].astype(F32) + inverse * (weighted - first_mean - hat * second_mean)
    out[...] = grad
    low = grad.astype(BF16)
    out_low[...] = low
    mixed_low[...] = mm(low, weight[...], NT).astype(BF16)
    fresh = [jnp.sum(e * hat, 0, keepdims=True), jnp.sum(e, 0, keepdims=True)]

    @pl.when(pl.program_id(0) == 0)
    def _():
        sums[0:1, :], sums[1:2, :] = fresh

    @pl.when(pl.program_id(0) > 0)
    def _():
        sums[0:1, :] += fresh[0]
        sums[1:2, :] += fresh[1]


def feed_norm_back(own, other, source, base, norms, weight, after):
    rows, width = source.shape
    size = 256
    part = pl.BlockSpec((size, width), lambda t: (t, 0))
    line = pl.BlockSpec(norms.shape, lambda t: (0, 0))
    whole = pl.BlockSpec(weight.shape, lambda t: (0, 0), pipeline_mode=pl.Buffered(1))
    low = jax.ShapeDtypeStruct((rows, width), BF16)
    return call(
        feed_norm_back_kernel,
        [own, other, source, base, norms, weight],
        [part] * 4 + [line, whole],
        [part] * 3 + [pl.BlockSpec((2, width), lambda t: (0, 0))],
        [jax.ShapeDtypeStruct((rows, width), F32), low, low, jax.ShapeDtypeStruct((2, width), F32)],
        (rows // size,),
        after,
    )


def norm_back_kernel(*refs, pairs, place):
    lefts, weights, refs = refs[:pairs], refs[pairs : 2 * pairs], refs[2 * pairs :]
    source, norms, *base, out, sums, upstream = refs
    gain = norms[place : place + 1, :]
    step = pl.program_id(0)
    tile = weights[0].shape[0]
    columns = pl.ds(pl.multiple_of(step * tile, tile), tile)
    total = mm(lefts[0][...], weights[0][...], NT)
    for left, weight in zip(lefts[1:], weights[1:]):
        total = total + mm(left[...], weight[...], NT)
    upstream[:, columns] = total

    @pl.when(step == pl.num_programs(0) - 1)
    def _():
        rows, width = upstream.shape
        size = 64

        def chunk(i, carry):
            gain_sum, shift_sum = carry
            r = pl.ds(pl.multiple_of(i * size, size), size)
            e = upstream[r, :]
            _, hat, inverse = normalize(source[r, :].astype(F32), gain, 0.0)
            weighted = e * gain
            first_mean = jnp.mean(weighted, -1, keepdims=True)
            second_mean = jnp.mean(weighted * hat, -1, keepdims=True)
            grad = inverse * (weighted - first_mean - hat * second_mean)
            if base:
                grad = grad + base[0][r, :]
            out[r, :] = grad
            return gain_sum + jnp.sum(e * hat, 0, keepdims=True), shift_sum + jnp.sum(e, 0, keepdims=True)

        zero = jnp.zeros((1, width), F32)
        sums[0:1, :], sums[1:2, :] = lax.fori_loop(0, rows // size, chunk, (zero, zero))


def norm_back_product(pairs, source, base, norms, place, after):
    rows, width = source.shape
    tile = 512
    whole = pl.BlockSpec((rows, width), lambda t: (0, 0), pipeline_mode=pl.Buffered(1))

    def rows_of(left, place):
        return pl.BlockSpec((rows, left.shape[1]), lambda t: (place, 0), pipeline_mode=pl.Buffered(1))

    operands = [left for left, _, _ in pairs] + [weight for _, _, weight in pairs] + [source, norms]
    in_specs = [rows_of(left, place) for left, place, _ in pairs]
    in_specs += [pl.BlockSpec((tile, weight.shape[1]), lambda t: (t, 0)) for _, _, weight in pairs]
    in_specs += [whole, pl.BlockSpec(norms.shape, lambda t: (0, 0))]
    if base is not None:
        operands.append(base)
        in_specs.append(whole)
    return call(
        functools.partial(norm_back_kernel, pairs=len(pairs), place=place),
        operands,
        in_specs,
        [whole, pl.BlockSpec((2, width), lambda t: (0, 0))],
        [jax.ShapeDtypeStruct((rows, width), F32), jax.ShapeDtypeStruct((2, width), F32)],
        (width // tile,),
        after,
        scratch=[pltpu.VMEM((rows, width), F32)],
    )


def plain_kernel(left, weight, *refs, dims):
    total = mm(left[...], weight[...], dims)
    for term in refs[:-1]:
        total = total + term[...].astype(F32)
    refs[-1][...] = total.astype(refs[-1].dtype)


def plain_product(left, place, rows, weight, dims, terms, after=(), kind=BF16):
    tile = 512
    if dims is NT:
        width = weight.shape[0]
        weights = pl.BlockSpec((tile, weight.shape[1]), lambda t: (t, 0))
    else:
        width = weight.shape[1]
        weights = pl.BlockSpec((weight.shape[0], tile), lambda t: (0, t))
    columns = pl.BlockSpec((rows, tile), lambda t: (0, t))
    return call(
        functools.partial(plain_kernel, dims=dims),
        [left, weight, *terms],
        [pl.BlockSpec((rows, left.shape[1]), lambda t: (place, 0), pipeline_mode=pl.Buffered(1)), weights]
        + [columns] * len(terms),
        columns,
        jax.ShapeDtypeStruct((rows, width), kind),
        (width // tile,),
        after,
    )


def both_kernel(left, weight, own, other):
    half = left.shape[0] // 2
    other[...] = mm(left[half:, :], weight[...], NT).astype(other.dtype)
    own[...] = mm(left[:half, :], weight[...], NT)


def both_product(left, weight, after):
    rows, depth = left.shape
    width = weight.shape[0]
    tile = 512
    columns = pl.BlockSpec((rows // 2, tile), lambda t: (0, t))
    return call(
        both_kernel,
        [left, weight],
        [
            pl.BlockSpec((rows, depth), lambda t: (0, 0), pipeline_mode=pl.Buffered(1)),
            pl.BlockSpec((tile, depth), lambda t: (t, 0)),
        ],
        [columns, columns],
        [jax.ShapeDtypeStruct((rows // 2, width), kind) for kind in (F32, BF16)],
        (width // tile,),
        after,
    )


def added(left, right, after):
    def kernel(a, b, out):
        out[...] = a[...] + b[...]

    whole = pl.BlockSpec(left.shape, lambda t: (0, 0))
    return call(kernel, [left, right], [whole] * 2, whole, jax.ShapeDtypeStruct(left.shape, left.dtype), (1,), after)


def stacked_rows(parts, after):
    def kernel(*refs):
        start = 0
        for ref in refs[:-1]:
            refs[-1][start : start + ref.shape[0], :] = ref[...]
            start += ref.shape[0]

    rows, width = sum(part.shape[0] for part in parts), parts[0].shape[1]
    specs = [pl.BlockSpec(part.shape, lambda t: (0, 0)) for part in parts]
    out = pl.BlockSpec((rows, width), lambda t: (0, 0))
    return call(kernel, parts, specs, out, jax.ShapeDtypeStruct((rows, width), F32), (1,), after)


def last_sum_kernel(index, *refs, segments, cuts):
    outs = refs[-len(cuts) :]
    column = 0
    for width, terms in segments:
        total = None
        for ref, start in terms:
            value = refs[ref][..., start : start + width]
            value = value.reshape(value.shape[-2:]).astype(F32)
            total = value if total is None else total + value
        past = 0
        for out, cut in zip(outs, cuts):
            low, high = max(past, column), min(past + cut, column + width)
            if low < high:
                out[:, low - past : high - past] = total[:, low - column : high - column]
            past += cut
        column += width


def sum_kernel(index, *refs, segments):
    out = refs[-1]
    column = 0
    for width, terms in segments:
        values = [refs[ref][..., start : start + width] for ref, start in terms]
        values = [value.reshape(-1, *value.shape[-2:]) for value in values]
        if len(values) > 2:
            values = [value.astype(F32) for value in values]
        total = functools.reduce(jnp.add, values).astype(out.dtype)
        out[..., column : column + width] = total.reshape(*out.shape[:-1], width)
        column += width


class Segment:
    def __init__(self, width, arrays, taken):
        self.width = width
        self.taken = list(taken)
        self.terms = [(a, len(taken), 0) for a in arrays]


class Chain:
    def __init__(self, index, bits, sizes, first=None):
        self.index = index
        self.sizes = sizes
        self.left = sorted(bits)
        self.taken = [] if first is None else [(self.left.index(first), first)]
        if first is not None:
            self.left.remove(first)
        self.segments = []

    def add(self, width, arrays):
        self.segments.append(Segment(width, arrays, self.taken))

    def join(self, other):
        self.segments += other.segments

    def _sum(self, bit, after, cuts=None):
        free = [b for b in sorted(self.left)[::-1] if b != bit]
        arrays, homes, segments = [], [], []
        for segment in self.segments:
            listed = []
            for array, level, start in segment.terms:
                home = sorted(self.left + [b for _, b in segment.taken[level:]])[::-1]
                known = [n for n, a in enumerate(arrays) if a is array and homes[n] == home]
                if not known:
                    arrays.append(array)
                    homes.append(home)
                    known = [len(arrays) - 1]
                listed.append((known[0], start))
            segments.append((segment.width, listed))
        rows = arrays[0].shape[1]
        total = sum(segment.width for segment in self.segments)
        steps = 0
        while steps < len(free) and (rows * total * 2 << (len(free) - steps)) > STEP_BYTES:
            steps += 1
        grid = (2,) * steps if steps else (1,)

        def spec(home, width):
            shape = tuple(2 if b in free[steps:] else 1 for b in home)

            def at(*step_and_index):
                index = step_and_index[-1]
                place = []
                for b in home:
                    if b == bit:
                        place.append(1 - ((index[0] >> b) & 1))
                    elif b in free:
                        place.append(step_and_index[free.index(b)] if b in free[:steps] else 0)
                    else:
                        place.append((index[0] >> b) & 1)
                return (*place, 0, 0)

            return pl.BlockSpec((*shape, rows, width), at)

        operands = [self.index] + [a.reshape((2,) * len(home) + a.shape[1:]) for a, home in zip(arrays, homes)]
        in_specs = [spec(home, a.shape[2]) for a, home in zip(arrays, homes)]
        if cuts is not None:
            return call(
                functools.partial(last_sum_kernel, segments=segments, cuts=cuts),
                operands,
                in_specs,
                [pl.BlockSpec((rows, cut), lambda t, i: (0, 0)) for cut in cuts],
                [jax.ShapeDtypeStruct((rows, cut), F32) for cut in cuts],
                grid,
                after,
                1,
            )
        result = call(
            functools.partial(sum_kernel, segments=segments),
            operands,
            in_specs,
            spec(free, total),
            jax.ShapeDtypeStruct((2,) * len(free) + (rows, total), BF16),
            grid,
            after,
            1,
        )
        return result.reshape(-1, rows, total)

    def pack(self, bit, after=()):
        return self._sum(bit, after)

    def travel(self, packed, bit):
        got = lax.ppermute(packed, "dp", [(i, i ^ (1 << bit)) for i in range(self.sizes["dp"])])
        step = (self.left.index(bit), bit)
        self.left.remove(bit)
        start = 0
        for segment in self.segments:
            segment.taken.append(step)
            segment.terms.append((got, len(segment.taken), start))
            start += segment.width
        return got

    def finish(self, cuts, after=()):
        for bit in list(self.left):
            self.travel(self.pack(bit), bit)
        return self._sum(None, after, cuts)


def bit_orders(count):
    bits = count.bit_length() - 1
    if bits == 4:
        return [(0, 1, 2, 3), (1, 0, 2, 3), (2, 3, 0, 1)]
    plain = tuple(range(bits))
    third = bits // 3
    return [plain, (1, 0) + plain[2:], plain[2 * third :] + plain[: 2 * third]]


def sided(value, bit, bits, side):
    place = bits.index(bit)
    shape = value.shape
    outer = 1 << place
    parts = value.reshape((outer, 2, shape[0] // (2 * outer)) + shape[1:])
    return lax.dynamic_index_in_dim(parts, side, 1, keepdims=False).reshape((shape[0] // 2,) + shape[1:])


def build(dp_size, mp_size):
    plain, swapped, last = bit_orders(dp_size)
    sizes = {"dp": dp_size, "mp": mp_size}
    all_bits = sorted(plain)

    def swap(value):
        return lax.ppermute(value, "mp", [(i, i ^ 1) for i in range(mp_size)])

    def local(
        media_feats,
        latents,
        patch_counts,
        cotangent,
        query_weight,
        key_weight,
        value_weight,
        out_weight,
        up_weight,
        down_weight,
        media_gain,
        media_shift,
        latent_gain,
        latent_shift,
        feed_gain,
        feed_shift,
    ):
        micro, patches, width = media_feats.shape
        dp_index = lax.axis_index("dp").astype(jnp.int32)
        mp_index = lax.axis_index("mp").astype(jnp.int32)
        flat_index = dp_index * mp_size + mp_index
        dp_list = dp_index.reshape(1)
        mp_list = mp_index.reshape(1)

        def first_step(grads, bit):
            if len(grads) == 2:
                return grads
            parted = grads[0].reshape(dp_size, width // dp_size, -1)
            mine = (dp_index >> bit) & 1
            return sided(parted, bit, all_bits[::-1], 1 - mine), sided(parted, bit, all_bits[::-1], mine)

        def sent_first(grads, bit):
            rear, front = first_step(grads, bit)
            return front, lax.ppermute(rear, "dp", [(i, i ^ (1 << bit)) for i in range(dp_size)])

        def paired(grads):
            if len(grads) == 1:
                parted = grads[0].reshape(dp_size, mp_size, -1, grads[0].shape[1])
                grads = [lax.dynamic_index_in_dim(parted, side, 1, keepdims=False) for side in (1 - mp_index, mp_index)]
            rear, front = grads
            return front, swap(rear)

        grad_own = cotangent.reshape(-1, width)
        grad_other = swap(grad_own)
        norms = jnp.stack([media_gain, media_shift, latent_gain, latent_shift, feed_gain, feed_shift])
        both_low, queries, keys, values = project(
            media_feats.reshape(-1, width), latents.reshape(-1, width), norms, query_weight, key_weight, value_weight
        )
        own = queries.shape[0]
        mixed_low, log_norm, residual, feed_own = attention_call(
            attend_kernel,
            patch_counts,
            queries,
            keys,
            values,
            [("row", latents.reshape(-1, width))],
            ["one", "norm", "long", "row"],
            (grad_other,),
            fixed=[out_weight, norms],
            scratch=1,
        )
        feed_other = swap(feed_own)

        tile = 512
        tiles = up_weight.shape[1] // tile
        third = tiles // 6
        first = tiles // 2 - third
        second = tiles - first - third
        rows_in = [feed_own, feed_other, grad_own, grad_other]
        splittable = width // dp_size % ROW_TILE == 0

        along = Chain(dp_list, all_bits, sizes, plain[0])
        across = Chain(dp_list, all_bits, sizes, swapped[0])
        far = Chain(dp_list, all_bits, sizes, last[0])
        grads, units = feed_part(
            dp_list, rows_in, up_weight, down_weight, 0, third + first, tile, None, (plain[0], swapped[0]), last[0], dp_size
        )
        if splittable:
            far_1, down_1, up_1 = grads[:2], grads[2:4], grads[4:]
        else:
            far_1 = [jnp.concatenate([g[:, : third * tile] for g in grads], 1)]
            down_1, up_1 = ([g[:, third * tile :]] for g in grads)
        along.add(first * tile, sent_first(down_1, plain[0]))
        across.add(first * tile, sent_first(up_1, swapped[0]))
        far.add(2 * third * tile, sent_first(far_1, last[0]))
        part_got = [chain.segments[0].terms[1][0] for chain in (along, across, far)]
        grads, units = feed_part(
            dp_list,
            rows_in,
            up_weight,
            down_weight,
            third + first,
            second,
            tile,
            units,
            (swapped[0], plain[0]),
            None,
            dp_size,
        )
        down_2, up_2 = (grads[:2], grads[2:]) if splittable else (grads[:1], grads[1:])
        across.add(second * tile, sent_first(down_2, swapped[0]))
        along.add(second * tile, sent_first(up_2, plain[0]))
        hidden, grad_up = units
        feed_back, feed_back_other = both_product(grad_up, up_weight, part_got)
        feed_back_got = swap(feed_back_other)
        far_packed = far.pack(last[1], (feed_back_other,))
        far_got = far.travel(far_packed, last[1])
        grad_residual, grad_residual_low, grad_mixed, feed_sums = feed_norm_back(
            feed_back, feed_back_got, residual, grad_own, norms, out_weight, (far_packed,)
        )
        blocks = dp_size * mp_size
        half = width // 2
        stackable = width // blocks % ROW_TILE == 0
        token = [grad_residual]
        markers = []

        def now():
            markers.append(marker(len(markers) + 1, patch_counts))
            return (*token, markers[-1])

        def ran(value):
            token[:] = [value]

        def wait(*values):
            token.extend(values)

        def move(chain, bit):
            packed = chain.pack(bit, now())
            ran(packed)
            return chain.travel(packed, bit)

        def end(chain, *cuts):
            totals = chain.finish(cuts, now())
            ran(totals[0])
            return totals

        def join(*chains):
            joined = Chain(dp_list, chains[0].left, sizes)
            for chain in chains:
                joined.join(chain)
            return joined

        def attend_back(start, count, before):
            made = attention_call(
                attend_back_kernel,
                patch_counts,
                queries,
                keys,
                values,
                [("one", grad_mixed), ("norm", log_norm)],
                ["one", "two", "two"],
                now(),
                start,
                count,
                before,
            )
            ran(made[0])
            return made

        out_grads = product(mp_list, [grad_residual_low], [(0, mixed_low, 0, 2)], blocks, now(), stackable)
        ran(out_grads[0])
        outs = Chain(dp_list, all_bits, sizes)
        out_pair = paired(out_grads)
        outs.add(out_pair[0].shape[-1], out_pair)
        made = attend_back(0, micro // 2, ())
        move(along, plain[1])
        move(across, swapped[1])
        wait(far_got)
        move(outs, last[0])
        grad_queries, grad_keys, grad_values = attend_back(micro // 2, micro - micro // 2, made)
        grad_keys = grad_keys.reshape(-1, width)
        grad_values = grad_values.reshape(-1, width)
        key_grads = product(
            mp_list, [both_low], [(0, grad_keys, 0, 2), (0, grad_queries, 0, 1)], blocks, now()
        )
        keyed = Chain(dp_list, all_bits, sizes)
        keyed.add(width + half, paired(key_grads))
        ran(key_grads[0])
        outs_got = move(outs, last[1])
        if stackable:
            far.join(outs)
        move(keyed, plain[0])
        value_grads = product(
            mp_list, [both_low], [(0, grad_values, 0, 2), (0, grad_queries, 1, 1)], blocks, now()
        )
        valued = Chain(dp_list, all_bits, sizes)
        valued.add(width + half, paired(value_grads))
        ran(value_grads[0])
        both = join(along, across)
        move(both, plain[2])
        move(valued, swapped[0])
        grad_latents, latent_sums = norm_back_product(
            [(grad_queries, 0, query_weight), (grad_keys, 1, key_weight), (grad_values, 1, value_weight)],
            latents.reshape(-1, width),
            grad_residual,
            norms,
            2,
            now(),
        )
        ran(grad_latents)
        move(keyed, plain[1])
        grad_media, media_sums = norm_back_product(
            [(grad_keys, 0, key_weight), (grad_values, 0, value_weight)],
            media_feats.reshape(-1, width),
            None,
            norms,
            0,
            now(),
        )
        ran(grad_media)
        sums = stacked_rows([media_sums, latent_sums, feed_sums], now())
        ran(sums)
        arrived = swap(sums)

        def move_sums(bit):
            total = added(sums, arrived, now())
            ran(total)
            return total, None if bit is None else lax.ppermute(total, "dp", [(i, i ^ (1 << bit)) for i in range(dp_size)])

        move(valued, swapped[1])
        wait(outs_got)
        move(both, plain[3])
        sums, arrived = move_sums(plain[0])
        move(keyed, plain[2])
        branch_other = plain_product(hidden, 1, own, down_weight, NN, [], now())
        ran(branch_other)
        branch_got = swap(branch_other)
        sums, arrived = move_sums(plain[1])
        move(valued, swapped[2])
        result = plain_product(hidden, 0, own, down_weight, NN, [residual, branch_got], now())
        ran(result)
        move(keyed, plain[3])
        sums, arrived = move_sums(plain[2])
        move(far, last[2])
        move(valued, swapped[3])
        sums, arrived = move_sums(plain[3])
        edge = third * tile
        along_down, along_up, across_up, across_down = end(both, first * tile, second * tile, first * tile, second * tile)
        for bit in plain[4:]:
            sums, arrived = move_sums(bit)
        move(far, last[3])
        sums, _ = move_sums(None)
        key_sum, query_sum = end(keyed, width, half)
        if stackable:
            far_down, far_up, out_rows = end(far, edge, edge, half)
            out_sum = jnp.concatenate([out_rows[: out_rows.shape[0] // 2], out_rows[out_rows.shape[0] // 2 :]], 1)
        else:
            far_down, far_up = end(far, edge, edge)
            (out_sum,) = end(outs, width)
        value_sum, query_rest = end(valued, width, half)
        grad_down_t = jnp.concatenate([far_down, along_down, across_down], 1)
        grad_up_w = jnp.concatenate([far_up, across_up, along_up], 1)
        share = width // blocks
        sums = lax.dynamic_slice(sums, (0, flat_index * share), (sums.shape[0], share))
        return (
            result.reshape(latents.shape),
            grad_latents.reshape(latents.shape),
            grad_media.reshape(media_feats.shape),
            jnp.concatenate([query_sum, query_rest], 1),
            key_sum,
            value_sum,
            out_sum.T,
            grad_up_w,
            grad_down_t.T,
            *[sums[i] for i in range(sums.shape[0])],
        )

    return local


def solution(mesh):
    rows = P(None, ("dp", "mp"), None)
    in_specs = (rows, rows, P(None, ("dp", "mp")), rows, P(), P(), P(), P(), P(None, "mp"), P("mp", None)) + (P(),) * 6
    first = P(("dp", "mp"), None)
    out_specs = (rows, rows, rows, first, first, first, P(None, ("dp", "mp")), P("dp", "mp"), P("mp", "dp")) + (
        P(("dp", "mp")),
    ) * 6
    local = build(mesh.shape["dp"], mesh.shape["mp"])
    return jax.shard_map(local, mesh=mesh, in_specs=in_specs, out_specs=out_specs, check_vma=False)
```

```python
import functools

import jax
import jax.numpy as jnp
from jax import lax
from jax.experimental import pallas as pl
from jax.experimental.pallas import tpu as pltpu
from jax.sharding import PartitionSpec as P

HEADS = 16
LAT_IMG = 64
EPSILON = 1e-05
MASKED_SCORE = -1e30
ROOT_HALF = 0.7071067811865476
DENSITY_SCALE = 0.3989422804014327
F32 = jnp.float32
BF16 = jnp.bfloat16
NN = (((1,), (0,)), ((), ()))
NT = (((1,), (1,)), ((), ()))
TN = (((0,), (0,)), ((), ()))
MIB = 1024 * 1024
ROW_TILE = 16
STEP_BYTES = 1200000
LONG = pl.CostEstimate(flops=10**12, bytes_accessed=10**10, transcendentals=0)


def mm(left, right, dims=NN):
    return lax.dot_general(left, right, dims, preferred_element_type=F32)


def low_mm(left, right):
    return mm(left, right).astype(BF16)


def normalize(values, gain_vec, shift_vec):
    row_mean = jnp.mean(values, -1, keepdims=True)
    centred = values - row_mean
    inv_scale = lax.rsqrt(jnp.mean(centred * centred, -1, keepdims=True) + EPSILON)
    scaled = centred * inv_scale
    return (scaled * gain_vec + shift_vec, scaled, inv_scale)


def mask_biases(counts, step, keys, lats, pair):
    lane = lax.broadcasted_iota(jnp.int32, (1, lats), 1) // LAT_IMG
    first = jnp.zeros((1, lats), jnp.int32)
    past = jnp.zeros((1, lats), jnp.int32)
    total = jnp.int32(0)
    for i in range(counts.shape[1]):
        after = total + counts[step, i]
        first = jnp.where(lane == i, total, first)
        past = jnp.where(lane == i, after, past)
        total = after
    place = lax.broadcasted_iota(jnp.int32, (keys, lats), 0)
    media = jnp.where((place >= first) & (place < past), 0.0, MASKED_SCORE)
    key_image = lax.broadcasted_iota(jnp.int32, (pair, pair), 0) // LAT_IMG
    latent_image = lax.broadcasted_iota(jnp.int32, (pair, pair), 1) // LAT_IMG
    return media, jnp.where(key_image == latent_image, 0.0, MASKED_SCORE)


def spans(total, size):
    return [slice(start, start + size) for start in range(0, total, size)]


def attend_kernel(
    counts, q, k, v, latents, weight, norms, mixed, norm, residual, feed, whole, *, start, heads, dim, pair
):
    scale = dim**-0.5
    lats = q.shape[0]
    bias_m, bias_l = mask_biases(counts, start + pl.program_id(0), k.shape[1], lats, pair)
    pairs = spans(lats, pair)
    columns = spans(heads * dim, dim)
    vm = v[0].T
    vl = v[1].T
    qs = [q[:, c] for c in columns]
    kl = [k[1, :, c] for c in columns]
    s_m = [mm(k[0, :, c], x, NT) * scale + bias_m for c, x in zip(columns, qs)]
    s_l = [jnp.concatenate([mm(y[p], x[p], NT) * scale + bias_l for p in pairs], 1) for y, x in zip(kl, qs)]
    top = [jnp.maximum(jnp.max(x, 0, keepdims=True), jnp.max(y, 0, keepdims=True)) for x, y in zip(s_m, s_l)]
    e_m = [jnp.exp(x - t) for x, t in zip(s_m, top)]
    e_l = [jnp.exp(x - t) for x, t in zip(s_l, top)]
    total = [jnp.sum(x, 0, keepdims=True) + jnp.sum(y, 0, keepdims=True) for x, y in zip(e_m, e_l)]
    inverse = [1.0 / t for t in total]
    p_m = [(x * i).astype(BF16) for x, i in zip(e_m, inverse)]
    p_l = [(x * i).astype(BF16) for x, i in zip(e_l, inverse)]
    outs = []
    for x, y, c in zip(p_m, p_l, columns):
        latent_part = jnp.concatenate([mm(vl[c, p], y[:, p]) for p in pairs], 1)
        outs.append((mm(vm[c, :], x) + latent_part).astype(BF16))
    norm[0, 0, :, :] = jnp.concatenate([t + jnp.log(x) for t, x in zip(top, total)], 0)
    low = jnp.concatenate(outs, 0).T
    mixed[...] = low
    group = pl.program_id(1)
    for g in range(whole.shape[0]):

        @pl.when(group == g)
        def _(g=g):
            whole[g] = low

    @pl.when(group == whole.shape[0] - 1)
    def _():
        total = latents[...].astype(F32)
        for g in range(whole.shape[0]):
            total = total + mm(whole[g], weight[g * heads * dim : (g + 1) * heads * dim, :])
        residual[...] = total
        feed[...] = normalize(total, norms[4:5, :], norms[5:6, :])[0].astype(BF16)


def attend_back_kernel(counts, q, k, v, grad_mixed, norm, *refs, start, heads, dim, pair):
    grad_q, grad_k, grad_v = refs[-3:]
    scale = dim**-0.5
    lats = q.shape[0]
    bias_m, bias_l = mask_biases(counts, start + pl.program_id(0), k.shape[1], lats, pair)
    pairs = spans(lats, pair)
    turned_m = k[0].T
    turned_l = k[1].T
    grad_qs = []
    for some in spans(heads, 4):
        columns = spans(heads * dim, dim)[some]
        group = slice(some.start * dim, some.stop * dim)
        qs = [q[:, c] for c in columns]
        gs = [grad_mixed[:, c] for c in columns]
        kl = [k[1, :, c] for c in columns]
        vl = [v[1, :, c] for c in columns]
        norms = [norm[0, 0, j : j + 1, :] for j in range(some.start, some.stop)]
        p_m = [jnp.exp(mm(k[0, :, c], y, NT) * scale + bias_m - n) for c, y, n in zip(columns, qs, norms)]
        s_l = [jnp.concatenate([mm(x[p], y[p], NT) * scale + bias_l for p in pairs], 1) for x, y in zip(kl, qs)]
        p_l = [jnp.exp(x - n) for x, n in zip(s_l, norms)]
        d_m = [mm(v[0, :, c], g, NT) for c, g in zip(columns, gs)]
        d_l = [jnp.concatenate([mm(x[p], g[p], NT) for p in pairs], 1) for x, g in zip(vl, gs)]
        means = [
            jnp.sum(x * y, 0, keepdims=True) + jnp.sum(z * w, 0, keepdims=True)
            for x, y, z, w in zip(d_m, p_m, d_l, p_l)
        ]
        g_m = [(x * (y - n)).astype(BF16) for x, y, n in zip(p_m, d_m, means)]
        g_l = [(x * (y - n)).astype(BF16) for x, y, n in zip(p_l, d_l, means)]
        p_m = [x.astype(BF16) for x in p_m]
        p_l = [x.astype(BF16) for x in p_l]
        grad_v[0, :, group] = jnp.concatenate([mm(x, g).astype(BF16) for x, g in zip(p_m, gs)], 1)
        grad_k[0, :, group] = jnp.concatenate([(mm(x, y) * scale).astype(BF16) for x, y in zip(g_m, qs)], 1)
        for p in pairs:
            grad_v[1, p, group] = jnp.concatenate([mm(x[:, p], g[p]).astype(BF16) for x, g in zip(p_l, gs)], 1)
            grad_k[1, p, group] = jnp.concatenate([(mm(x[:, p], y[p]) * scale).astype(BF16) for x, y in zip(g_l, qs)], 1)
        for c, x, z in zip(columns, g_m, g_l):
            latent_part = jnp.concatenate([mm(turned_l[c, p], z[:, p]) for p in pairs], 1)
            grad_qs.append(((mm(turned_m[c, :], x) + latent_part) * scale).astype(BF16))
    grad_q[...] = jnp.concatenate(grad_qs, 0).T


def call(kernel, operands, in_specs, out_specs, out_shape, grid, after=(), scalars=0, scratch=(), aliases=None):
    given = len(operands)

    def body(*refs):
        kernel(*refs[:given], *refs[given + len(after) :])

    return pl.pallas_call(
        body,
        grid_spec=pltpu.PrefetchScalarGridSpec(
            num_scalar_prefetch=scalars,
            grid=grid,
            in_specs=list(in_specs) + [pl.BlockSpec(memory_space=pl.ANY)] * len(after),
            out_specs=out_specs,
            scratch_shapes=list(scratch),
        ),
        out_shape=out_shape,
        input_output_aliases=aliases or {},
        compiler_params=pltpu.CompilerParams(vmem_limit_bytes=60 * MIB),
        cost_estimate=LONG,
    )(*operands, *after)


def marker(number, source):
    def kernel(target):
        pass

    anywhere = pl.BlockSpec(memory_space=pl.ANY)
    return call(kernel, [], [], anywhere, jax.ShapeDtypeStruct((8, 128 * number), F32), (1,), (source,))


def project_kernel(media, latents, norms, query, key, value, both, queries, keys, values):
    rows = media.shape[0]

    def products(side, r, low):
        keys[side, r, :] = mm(low, key[...]).astype(BF16)
        values[side, r, :] = mm(low, value[...]).astype(BF16)
        if side:
            queries[r, :] = mm(low, query[...]).astype(BF16)

    @pl.when(pl.program_id(0) == 0)
    def _():
        for side, source in enumerate((media, latents)):
            gain, shift = norms[2 * side : 2 * side + 1, :], norms[2 * side + 1 : 2 * side + 2, :]
            for r in spans(rows, rows // 2):
                low = normalize(source[r, :].astype(F32), gain, shift)[0].astype(BF16)
                both[side * rows + r.start : side * rows + r.stop, :] = low
                products(side, r, low)

    @pl.when(pl.program_id(0) > 0)
    def _():
        for side in range(2):
            products(side, slice(0, rows), both[side * rows : (side + 1) * rows, :])


def project(media, latents, norms, query, key, value):
    rows, width = latents.shape
    tile = 512
    whole = pl.BlockSpec((rows, width), lambda t: (0, 0), pipeline_mode=pl.Buffered(1))
    weight = pl.BlockSpec((width, tile), lambda t: (0, t))
    two = jax.ShapeDtypeStruct((2, rows, width), BF16)
    return call(
        project_kernel,
        [media, latents, norms, query, key, value],
        [whole, whole, pl.BlockSpec(norms.shape, lambda t: (0, 0)), weight, weight, weight],
        [
            pl.BlockSpec((2 * rows, width), lambda t: (0, 0), pipeline_mode=pl.Buffered(1)),
            pl.BlockSpec((rows, tile), lambda t: (0, t)),
            pl.BlockSpec((2, rows, tile), lambda t: (0, 0, t)),
            pl.BlockSpec((2, rows, tile), lambda t: (0, 0, t)),
        ],
        [jax.ShapeDtypeStruct((2 * rows, width), BF16), jax.ShapeDtypeStruct((rows, width), BF16), two, two],
        (width // tile,),
    )


def attention_call(kernel, counts, queries, keys, values, more, outs, after=(), start=0, count=None, before=(), fixed=(), scratch=0):
    micro = counts.shape[0]
    rows = queries.shape[0] // micro
    width = queries.shape[1]
    groups = 2
    heads = HEADS // groups
    group = width // groups
    one = pl.BlockSpec((rows, group), lambda m, g: (start + m, g))
    two = pl.BlockSpec((2, rows, group), lambda m, g: (0, start + m, g))
    norm = pl.BlockSpec((1, 1, heads, rows), lambda m, g: (start + m, g, 0, 0))
    kinds = {
        "one": (one, jax.ShapeDtypeStruct(queries.shape, BF16)),
        "two": (two, jax.ShapeDtypeStruct(keys.shape, BF16)),
        "norm": (norm, jax.ShapeDtypeStruct((micro, groups, heads, rows), F32)),
        "row": (pl.BlockSpec((rows, width), lambda m, g: (start + m, 0)), jax.ShapeDtypeStruct(queries.shape, BF16)),
        "long": (pl.BlockSpec((rows, width), lambda m, g: (start + m, 0)), jax.ShapeDtypeStruct(queries.shape, F32)),
    }
    operands = [counts, queries, keys, values] + [value for _, value in more]
    in_specs = [pl.BlockSpec(memory_space=pltpu.SMEM), one, two, two] + [kinds[kind][0] for kind, _ in more]
    operands += fixed
    in_specs += [pl.BlockSpec(f.shape, lambda m, g: (0, 0), pipeline_mode=pl.Buffered(1)) for f in fixed]
    return call(
        functools.partial(kernel, start=start, heads=heads, dim=width // HEADS, pair=2 * LAT_IMG),
        operands + list(before),
        in_specs + [pl.BlockSpec(memory_space=pl.ANY)] * len(before),
        [kinds[kind][0] for kind in outs],
        [kinds[kind][1] for kind in outs],
        (micro if count is None else count, groups),
        after,
        scratch=[pltpu.VMEM((groups, rows, group), BF16)] * scratch,
        aliases={len(operands) + n: n for n in range(len(before))},
    )


def split_rows(whole, rear_ref, front_ref, block_rows, first_bit, mine):
    for i in range(rear_ref.shape[0]):
        low = i & ((1 << first_bit) - 1)
        base = ((i >> first_bit) << (first_bit + 1)) | low
        for ref, side in ((rear_ref, 1 - mine), (front_ref, mine)):
            block = base + side * (1 << first_bit)
            rows = pl.ds(pl.multiple_of(block * block_rows, block_rows), block_rows)
            ref[i, :, :] = whole[rows, :]


def feed_kernel(index, feed_own, feed_other, cot_own, cot_other, up, down, *refs, kept, bits, far, block_rows):
    refs = refs[kept:]
    half, width = feed_own.shape
    tile = up.shape[1]
    if bits is None:
        grad_down, grad_up_w, hidden, grad_up, feed, cot = refs
    else:
        *sides, hidden, grad_up, feed, cot, grad_down, grad_up_w = refs

    @pl.when(pl.program_id(0) == 0)
    def _():
        for whole, parts in ((feed, (feed_own, feed_other)), (cot, (cot_own, cot_other))):
            for n, part in enumerate(parts):
                whole[n * half : (n + 1) * half, :] = part[...]

    for r in spans(2 * half, half):
        u = mm(feed[r, :], up[...])
        grad_hidden = mm(cot[r, :], down[...], NT)
        cdf = 0.5 * (1.0 + lax.erf(u * ROOT_HALF))
        pdf = jnp.exp(-0.5 * u * u) * DENSITY_SCALE
        hidden[r, :] = (u * cdf).astype(BF16)
        grad_up[r, :] = (grad_hidden * (cdf + u * pdf)).astype(BF16)
    for r in spans(width, width // 2):
        grad_down[r, :] = mm(cot[:, r], hidden[...], TN).astype(BF16)
        grad_up_w[r, :] = mm(feed[:, r], grad_up[...], TN).astype(BF16)
    if bits is None:
        return

    def split(whole, rear, front, bit):
        split_rows(whole, rear, front, block_rows, bit, (index[0] >> bit) & 1)

    def near():
        split(grad_down, *sides[-4:-2], bits[0])
        split(grad_up_w, *sides[-2:], bits[1])

    if far is None:
        near()
    else:
        step = pl.program_id(0)
        pl.when(step > 0)(near)

        @pl.when(step == 0)
        def _():
            rear, front = sides[:2]
            split(grad_down, rear.at[:, :, :tile], front.at[:, :, :tile], far)
            split(grad_up_w, rear.at[:, :, tile:], front.at[:, :, tile:], far)


def feed_part(index, rows_in, up, down, start, tiles, tile, before, bits, far, blocks):
    half, width = rows_in[0].shape
    block_rows = width // blocks
    whole = pl.BlockSpec((half, width), lambda t, i: (0, 0), pipeline_mode=pl.Buffered(1))
    units = pl.BlockSpec((2 * half, tile), lambda t, i: (0, start + t))
    unit_shape = jax.ShapeDtypeStruct((2 * half, up.shape[1]), BF16)
    kept = [] if before is None else list(before)
    split = block_rows % ROW_TILE == 0
    if split:
        apart = 0 if far is None else 1
        shape = (blocks // 2, block_rows)
        grads = [pl.BlockSpec((*shape, 2 * tile), lambda t, i: (0, 0, 0), pipeline_mode=pl.Buffered(1))] * (2 * apart)
        shapes = [jax.ShapeDtypeStruct((*shape, 2 * tile), BF16)] * (2 * apart)
        grads += [pl.BlockSpec((*shape, tile), lambda t, i: (0, 0, jnp.maximum(t - apart, 0)))] * 4
        shapes += [jax.ShapeDtypeStruct((*shape, (tiles - apart) * tile), BF16)] * 4
        scratch = [pltpu.VMEM((2 * half, width), BF16)] * 2 + [pltpu.VMEM((width, tile), BF16)] * 2
    else:
        grads = [pl.BlockSpec((width, tile), lambda t, i: (0, t))] * 2
        shapes = [jax.ShapeDtypeStruct((width, tiles * tile), BF16)] * 2
        scratch = [pltpu.VMEM((2 * half, width), BF16)] * 2
    first = len(shapes)
    anywhere = pl.BlockSpec(memory_space=pl.ANY)
    results = call(
        functools.partial(
            feed_kernel, kept=len(kept), bits=bits if split else None, far=far if split else None, block_rows=block_rows
        ),
        [index, *rows_in, up, down, *kept],
        [
            whole,
            whole,
            whole,
            whole,
            pl.BlockSpec((width, tile), lambda t, i: (0, start + t)),
            pl.BlockSpec((tile, width), lambda t, i: (start + t, 0)),
        ]
        + [anywhere] * len(kept),
        grads + [units, units],
        shapes + [unit_shape, unit_shape],
        (tiles,),
        (),
        1,
        scratch,
        {7: first, 8: first + 1} if kept else {},
    )
    return results[:-2], results[-2:]


def product_kernel(index, *refs, lefts, parts, block_rows, split):
    step = pl.program_id(0)
    target = refs[-1]
    rights = refs[lefts : lefts + len(parts)]
    for (place, first, past), right in zip(parts, rights):

        @pl.when((step >= first) & (step < past))
        def _(left=refs[place], right=right):
            skipped = left.shape[0] - right.shape[0]
            target[...] = mm(left[skipped:, :], right[...], TN).astype(BF16)

    if split:
        split_rows(target, refs[-3], refs[-2], block_rows, 0, index[0] & 1)


def product(index, lefts, parts, blocks, after, stacked=False):
    width = lefts[0].shape[1]
    block_rows = width // blocks
    tile = width // 2
    split = block_rows % ROW_TILE == 0
    in_specs = [pl.BlockSpec(left.shape, lambda t, i: (0, 0), pipeline_mode=pl.Buffered(1)) for left in lefts]
    steps = []
    start = 0
    for place, right, first, count in parts:

        def at(t, i, first=first, start=start, count=count):
            return (0, first + jnp.clip(t - start, 0, count - 1))

        in_specs.append(pl.BlockSpec((right.shape[0], tile), at))
        steps.append((place, start, start + count))
        start += count
    if split:
        place = (lambda t, i: (0, t, 0)) if stacked else (lambda t, i: (0, 0, t))
        shape = (block_rows * start, tile) if stacked else (block_rows, tile * start)
        out_specs = [pl.BlockSpec((blocks // 2, block_rows, tile), place)] * 2
        out_shape = [jax.ShapeDtypeStruct((blocks // 2, *shape), BF16)] * 2
        scratch = [pltpu.VMEM((width, tile), BF16)]
    else:
        out_specs = [pl.BlockSpec((width, tile), lambda t, i: (0, t))]
        out_shape = [jax.ShapeDtypeStruct((width, tile * start), BF16)]
        scratch = []
    kernel = functools.partial(product_kernel, lefts=len(lefts), parts=steps, block_rows=block_rows, split=split)
    operands = [index, *lefts] + [right for _, right, _, _ in parts]
    return call(kernel, operands, in_specs, out_specs, out_shape, (start,), after, 1, scratch)


def feed_norm_back_kernel(own, other, source, base, norms, weight, out, out_low, mixed_low, sums):
    gain = norms[4:5, :]
    e = own[...] + other[...].astype(F32)
    _, hat, inverse = normalize(source[...], gain, 0.0)
    weighted = e * gain
    first_mean = jnp.mean(weighted, -1, keepdims=True)
    second_mean = jnp.mean(weighted * hat, -1, keepdims=True)
    grad = base[...].astype(F32) + inverse * (weighted - first_mean - hat * second_mean)
    out[...] = grad
    low = grad.astype(BF16)
    out_low[...] = low
    mixed_low[...] = mm(low, weight[...], NT).astype(BF16)
    fresh = [jnp.sum(e * hat, 0, keepdims=True), jnp.sum(e, 0, keepdims=True)]

    @pl.when(pl.program_id(0) == 0)
    def _():
        sums[0:1, :], sums[1:2, :] = fresh

    @pl.when(pl.program_id(0) > 0)
    def _():
        sums[0:1, :] += fresh[0]
        sums[1:2, :] += fresh[1]


def feed_norm_back(own, other, source, base, norms, weight, after):
    rows, width = source.shape
    size = 256
    part = pl.BlockSpec((size, width), lambda t: (t, 0))
    line = pl.BlockSpec(norms.shape, lambda t: (0, 0))
    whole = pl.BlockSpec(weight.shape, lambda t: (0, 0), pipeline_mode=pl.Buffered(1))
    low = jax.ShapeDtypeStruct((rows, width), BF16)
    return call(
        feed_norm_back_kernel,
        [own, other, source, base, norms, weight],
        [part] * 4 + [line, whole],
        [part] * 3 + [pl.BlockSpec((2, width), lambda t: (0, 0))],
        [jax.ShapeDtypeStruct((rows, width), F32), low, low, jax.ShapeDtypeStruct((2, width), F32)],
        (rows // size,),
        after,
    )


def norm_back_kernel(*refs, pairs, place):
    lefts, weights, refs = refs[:pairs], refs[pairs : 2 * pairs], refs[2 * pairs :]
    source, norms, *base, out, sums, upstream = refs
    gain = norms[place : place + 1, :]
    step = pl.program_id(0)
    tile = weights[0].shape[0]
    columns = pl.ds(pl.multiple_of(step * tile, tile), tile)
    total = mm(lefts[0][...], weights[0][...], NT)
    for left, weight in zip(lefts[1:], weights[1:]):
        total = total + mm(left[...], weight[...], NT)
    upstream[:, columns] = total

    @pl.when(step == pl.num_programs(0) - 1)
    def _():
        rows, width = upstream.shape
        size = 64

        def chunk(i, carry):
            gain_sum, shift_sum = carry
            r = pl.ds(pl.multiple_of(i * size, size), size)
            e = upstream[r, :]
            _, hat, inverse = normalize(source[r, :].astype(F32), gain, 0.0)
            weighted = e * gain
            first_mean = jnp.mean(weighted, -1, keepdims=True)
            second_mean = jnp.mean(weighted * hat, -1, keepdims=True)
            grad = inverse * (weighted - first_mean - hat * second_mean)
            if base:
                grad = grad + base[0][r, :]
            out[r, :] = grad
            return gain_sum + jnp.sum(e * hat, 0, keepdims=True), shift_sum + jnp.sum(e, 0, keepdims=True)

        zero = jnp.zeros((1, width), F32)
        sums[0:1, :], sums[1:2, :] = lax.fori_loop(0, rows // size, chunk, (zero, zero))


def norm_back_product(pairs, source, base, norms, place, after):
    rows, width = source.shape
    tile = 512
    whole = pl.BlockSpec((rows, width), lambda t: (0, 0), pipeline_mode=pl.Buffered(1))

    def rows_of(left, place):
        return pl.BlockSpec((rows, left.shape[1]), lambda t: (place, 0), pipeline_mode=pl.Buffered(1))

    operands = [left for left, _, _ in pairs] + [weight for _, _, weight in pairs] + [source, norms]
    in_specs = [rows_of(left, place) for left, place, _ in pairs]
    in_specs += [pl.BlockSpec((tile, weight.shape[1]), lambda t: (t, 0)) for _, _, weight in pairs]
    in_specs += [whole, pl.BlockSpec(norms.shape, lambda t: (0, 0))]
    if base is not None:
        operands.append(base)
        in_specs.append(whole)
    return call(
        functools.partial(norm_back_kernel, pairs=len(pairs), place=place),
        operands,
        in_specs,
        [whole, pl.BlockSpec((2, width), lambda t: (0, 0))],
        [jax.ShapeDtypeStruct((rows, width), F32), jax.ShapeDtypeStruct((2, width), F32)],
        (width // tile,),
        after,
        scratch=[pltpu.VMEM((rows, width), F32)],
    )


def plain_kernel(left, weight, *refs, dims):
    total = mm(left[...], weight[...], dims)
    for term in refs[:-1]:
        total = total + term[...].astype(F32)
    refs[-1][...] = total.astype(refs[-1].dtype)


def plain_product(left, place, rows, weight, dims, terms, after=(), kind=BF16):
    tile = 512
    if dims is NT:
        width = weight.shape[0]
        weights = pl.BlockSpec((tile, weight.shape[1]), lambda t: (t, 0))
    else:
        width = weight.shape[1]
        weights = pl.BlockSpec((weight.shape[0], tile), lambda t: (0, t))
    columns = pl.BlockSpec((rows, tile), lambda t: (0, t))
    return call(
        functools.partial(plain_kernel, dims=dims),
        [left, weight, *terms],
        [pl.BlockSpec((rows, left.shape[1]), lambda t: (place, 0), pipeline_mode=pl.Buffered(1)), weights]
        + [columns] * len(terms),
        columns,
        jax.ShapeDtypeStruct((rows, width), kind),
        (width // tile,),
        after,
    )


def both_kernel(left, weight, own, other):
    half = left.shape[0] // 2
    other[...] = mm(left[half:, :], weight[...], NT).astype(other.dtype)
    own[...] = mm(left[:half, :], weight[...], NT)


def both_product(left, weight, after):
    rows, depth = left.shape
    width = weight.shape[0]
    tile = 512
    columns = pl.BlockSpec((rows // 2, tile), lambda t: (0, t))
    return call(
        both_kernel,
        [left, weight],
        [
            pl.BlockSpec((rows, depth), lambda t: (0, 0), pipeline_mode=pl.Buffered(1)),
            pl.BlockSpec((tile, depth), lambda t: (t, 0)),
        ],
        [columns, columns],
        [jax.ShapeDtypeStruct((rows // 2, width), kind) for kind in (F32, BF16)],
        (width // tile,),
        after,
    )


def added(left, right, after):
    def kernel(a, b, out):
        out[...] = a[...] + b[...]

    whole = pl.BlockSpec(left.shape, lambda t: (0, 0))
    return call(kernel, [left, right], [whole] * 2, whole, jax.ShapeDtypeStruct(left.shape, left.dtype), (1,), after)


def stacked_rows(parts, after):
    def kernel(*refs):
        start = 0
        for ref in refs[:-1]:
            refs[-1][start : start + ref.shape[0], :] = ref[...]
            start += ref.shape[0]

    rows, width = sum(part.shape[0] for part in parts), parts[0].shape[1]
    specs = [pl.BlockSpec(part.shape, lambda t: (0, 0)) for part in parts]
    out = pl.BlockSpec((rows, width), lambda t: (0, 0))
    return call(kernel, parts, specs, out, jax.ShapeDtypeStruct((rows, width), F32), (1,), after)


def last_sum_kernel(index, *refs, segments, cuts):
    outs = refs[-len(cuts) :]
    column = 0
    for width, terms in segments:
        total = None
        for ref, start in terms:
            value = refs[ref][..., start : start + width]
            value = value.reshape(value.shape[-2:]).astype(F32)
            total = value if total is None else total + value
        past = 0
        for out, cut in zip(outs, cuts):
            low, high = max(past, column), min(past + cut, column + width)
            if low < high:
                out[:, low - past : high - past] = total[:, low - column : high - column]
            past += cut
        column += width


def sum_kernel(index, *refs, segments):
    out = refs[-1]
    column = 0
    for width, terms in segments:
        values = [refs[ref][..., start : start + width] for ref, start in terms]
        values = [value.reshape(-1, *value.shape[-2:]) for value in values]
        if len(values) > 2:
            values = [value.astype(F32) for value in values]
        total = functools.reduce(jnp.add, values).astype(out.dtype)
        out[..., column : column + width] = total.reshape(*out.shape[:-1], width)
        column += width


class Segment:
    def __init__(self, width, arrays, taken):
        self.width = width
        self.taken = list(taken)
        self.terms = [(a, len(taken), 0) for a in arrays]


class Chain:
    def __init__(self, index, bits, sizes, first=None):
        self.index = index
        self.sizes = sizes
        self.left = sorted(bits)
        self.taken = [] if first is None else [(self.left.index(first), first)]
        if first is not None:
            self.left.remove(first)
        self.segments = []

    def add(self, width, arrays):
        self.segments.append(Segment(width, arrays, self.taken))

    def join(self, other):
        self.segments += other.segments

    def _sum(self, bit, after, cuts=None):
        free = [b for b in sorted(self.left)[::-1] if b != bit]
        arrays, homes, segments = [], [], []
        for segment in self.segments:
            listed = []
            for array, level, start in segment.terms:
                home = sorted(self.left + [b for _, b in segment.taken[level:]])[::-1]
                known = [n for n, a in enumerate(arrays) if a is array and homes[n] == home]
                if not known:
                    arrays.append(array)
                    homes.append(home)
                    known = [len(arrays) - 1]
                listed.append((known[0], start))
            segments.append((segment.width, listed))
        rows = arrays[0].shape[1]
        total = sum(segment.width for segment in self.segments)
        steps = 0
        while steps < len(free) and (rows * total * 2 << (len(free) - steps)) > STEP_BYTES:
            steps += 1
        grid = (2,) * steps if steps else (1,)

        def spec(home, width):
            shape = tuple(2 if b in free[steps:] else 1 for b in home)

            def at(*step_and_index):
                index = step_and_index[-1]
                place = []
                for b in home:
                    if b == bit:
                        place.append(1 - ((index[0] >> b) & 1))
                    elif b in free:
                        place.append(step_and_index[free.index(b)] if b in free[:steps] else 0)
                    else:
                        place.append((index[0] >> b) & 1)
                return (*place, 0, 0)

            return pl.BlockSpec((*shape, rows, width), at)

        operands = [self.index] + [a.reshape((2,) * len(home) + a.shape[1:]) for a, home in zip(arrays, homes)]
        in_specs = [spec(home, a.shape[2]) for a, home in zip(arrays, homes)]
        if cuts is not None:
            return call(
                functools.partial(last_sum_kernel, segments=segments, cuts=cuts),
                operands,
                in_specs,
                [pl.BlockSpec((rows, cut), lambda t, i: (0, 0)) for cut in cuts],
                [jax.ShapeDtypeStruct((rows, cut), F32) for cut in cuts],
                grid,
                after,
                1,
            )
        result = call(
            functools.partial(sum_kernel, segments=segments),
            operands,
            in_specs,
            spec(free, total),
            jax.ShapeDtypeStruct((2,) * len(free) + (rows, total), BF16),
            grid,
            after,
            1,
        )
        return result.reshape(-1, rows, total)

    def pack(self, bit, after=()):
        return self._sum(bit, after)

    def travel(self, packed, bit):
        got = lax.ppermute(packed, "dp", [(i, i ^ (1 << bit)) for i in range(self.sizes["dp"])])
        step = (self.left.index(bit), bit)
        self.left.remove(bit)
        start = 0
        for segment in self.segments:
            segment.taken.append(step)
            segment.terms.append((got, len(segment.taken), start))
            start += segment.width
        return got

    def finish(self, cuts, after=()):
        for bit in list(self.left):
            self.travel(self.pack(bit), bit)
        return self._sum(None, after, cuts)


def bit_orders(count):
    bits = count.bit_length() - 1
    if bits == 4:
        return [(0, 1, 2, 3), (1, 0, 2, 3), (2, 3, 0, 1)]
    plain = tuple(range(bits))
    third = bits // 3
    return [plain, (1, 0) + plain[2:], plain[2 * third :] + plain[: 2 * third]]


def sided(value, bit, bits, side):
    place = bits.index(bit)
    shape = value.shape
    outer = 1 << place
    parts = value.reshape((outer, 2, shape[0] // (2 * outer)) + shape[1:])
    return lax.dynamic_index_in_dim(parts, side, 1, keepdims=False).reshape((shape[0] // 2,) + shape[1:])


def build(dp_size, mp_size):
    plain, swapped, last = bit_orders(dp_size)
    sizes = {"dp": dp_size, "mp": mp_size}
    all_bits = sorted(plain)

    def swap(value):
        return lax.ppermute(value, "mp", [(i, i ^ 1) for i in range(mp_size)])

    def local(
        media_feats,
        latents,
        patch_counts,
        cotangent,
        query_weight,
        key_weight,
        value_weight,
        out_weight,
        up_weight,
        down_weight,
        media_gain,
        media_shift,
        latent_gain,
        latent_shift,
        feed_gain,
        feed_shift,
    ):
        micro, patches, width = media_feats.shape
        dp_index = lax.axis_index("dp").astype(jnp.int32)
        mp_index = lax.axis_index("mp").astype(jnp.int32)
        flat_index = dp_index * mp_size + mp_index
        dp_list = dp_index.reshape(1)
        mp_list = mp_index.reshape(1)

        def first_step(grads, bit):
            if len(grads) == 2:
                return grads
            parted = grads[0].reshape(dp_size, width // dp_size, -1)
            mine = (dp_index >> bit) & 1
            return sided(parted, bit, all_bits[::-1], 1 - mine), sided(parted, bit, all_bits[::-1], mine)

        def sent_first(grads, bit):
            rear, front = first_step(grads, bit)
            return front, lax.ppermute(rear, "dp", [(i, i ^ (1 << bit)) for i in range(dp_size)])

        def paired(grads):
            if len(grads) == 1:
                parted = grads[0].reshape(dp_size, mp_size, -1, grads[0].shape[1])
                grads = [lax.dynamic_index_in_dim(parted, side, 1, keepdims=False) for side in (1 - mp_index, mp_index)]
            rear, front = grads
            return front, swap(rear)

        grad_own = cotangent.reshape(-1, width)
        grad_other = swap(grad_own)
        norms = jnp.stack([media_gain, media_shift, latent_gain, latent_shift, feed_gain, feed_shift])
        both_low, queries, keys, values = project(
            media_feats.reshape(-1, width), latents.reshape(-1, width), norms, query_weight, key_weight, value_weight
        )
        own = queries.shape[0]
        mixed_low, log_norm, residual, feed_own = attention_call(
            attend_kernel,
            patch_counts,
            queries,
            keys,
            values,
            [("row", latents.reshape(-1, width))],
            ["one", "norm", "long", "row"],
            (grad_other,),
            fixed=[out_weight, norms],
            scratch=1,
        )
        feed_other = swap(feed_own)

        tile = 512
        tiles = up_weight.shape[1] // tile
        third = tiles // 6
        first = tiles // 2 - third
        second = tiles - first - third
        rows_in = [feed_own, feed_other, grad_own, grad_other]
        splittable = width // dp_size % ROW_TILE == 0

        along, along_2 = (Chain(dp_list, all_bits, sizes, plain[0]) for _ in range(2))
        across, across_2 = (Chain(dp_list, all_bits, sizes, swapped[0]) for _ in range(2))
        far = Chain(dp_list, all_bits, sizes, last[0])
        grads, units = feed_part(
            dp_list, rows_in, up_weight, down_weight, 0, third + first, tile, None, (plain[0], swapped[0]), last[0], dp_size
        )
        if splittable:
            far_1, down_1, up_1 = grads[:2], grads[2:4], grads[4:]
        else:
            far_1 = [jnp.concatenate([g[:, : third * tile] for g in grads], 1)]
            down_1, up_1 = ([g[:, third * tile :]] for g in grads)
        along.add(first * tile, sent_first(down_1, plain[0]))
        across.add(first * tile, sent_first(up_1, swapped[0]))
        far.add(2 * third * tile, sent_first(far_1, last[0]))
        part_got = [chain.segments[0].terms[1][0] for chain in (along, across, far)]
        grads, units = feed_part(
            dp_list,
            rows_in,
            up_weight,
            down_weight,
            third + first,
            second,
            tile,
            units,
            (swapped[0], plain[0]),
            None,
            dp_size,
        )
        down_2, up_2 = (grads[:2], grads[2:]) if splittable else (grads[:1], grads[1:])
        across_2.add(second * tile, sent_first(down_2, swapped[0]))
        along_2.add(second * tile, sent_first(up_2, plain[0]))
        hidden, grad_up = units
        feed_back, feed_back_other = both_product(grad_up, up_weight, part_got)
        feed_back_got = swap(feed_back_other)
        far_packed = far.pack(last[1], (feed_back_other,))
        far_got = far.travel(far_packed, last[1])
        grad_residual, grad_residual_low, grad_mixed, feed_sums = feed_norm_back(
            feed_back, feed_back_got, residual, grad_own, norms, out_weight, (far_packed,)
        )
        blocks = dp_size * mp_size
        token = [grad_residual]
        markers = []

        def now():
            markers.append(marker(len(markers) + 1, patch_counts))
            return (*token, markers[-1])

        def ran(value):
            token[:] = [value]

        def wait(*values):
            token.extend(values)

        def move(chain, bit):
            packed = chain.pack(bit, now())
            ran(packed)
            return chain.travel(packed, bit)

        def end(chain, *cuts):
            totals = chain.finish(cuts, now())
            ran(totals[0])
            return totals

        def join(*chains):
            joined = Chain(dp_list, chains[0].left, sizes)
            for chain in chains:
                joined.join(chain)
            return joined

        def attend_back(start, count, before):
            made = attention_call(
                attend_back_kernel,
                patch_counts,
                queries,
                keys,
                values,
                [("one", grad_mixed), ("norm", log_norm)],
                ["one", "two", "two"],
                now(),
                start,
                count,
                before,
            )
            ran(made[0])
            return made

        grad_queries, grad_keys, grad_values = attend_back(0, micro, ())
        move(along, plain[1])
        move(across, swapped[1])
        move(along_2, plain[1])
        move(across_2, swapped[1])
        wait(far_got)
        grad_keys = grad_keys.reshape(-1, width)
        grad_values = grad_values.reshape(-1, width)
        key_grads = product(
            mp_list, [both_low], [(0, grad_keys, 0, 2), (0, grad_queries, 0, 2)], blocks, now()
        )
        keyed = Chain(dp_list, all_bits, sizes)
        keyed.add(2 * width, paired(key_grads))
        ran(key_grads[0])
        both = join(along, across)
        move(both, plain[2])
        branch_other = plain_product(hidden, 1, own, down_weight, NN, [], now())
        ran(branch_other)
        branch_got = swap(branch_other)
        move(keyed, plain[0])
        wait(branch_got)
        value_grads = product(
            mp_list, [both_low, grad_residual_low], [(0, grad_values, 0, 2), (1, mixed_low, 0, 2)], blocks, now()
        )
        valued = Chain(dp_list, all_bits, sizes)
        valued.add(2 * width, paired(value_grads))
        ran(value_grads[0])
        both_got = move(both, plain[3])
        both_2 = join(along_2, across_2)
        move(both_2, plain[2])
        move(valued, swapped[0])
        grad_latents, latent_sums = norm_back_product(
            [(grad_queries, 0, query_weight), (grad_keys, 1, key_weight), (grad_values, 1, value_weight)],
            latents.reshape(-1, width),
            grad_residual,
            norms,
            2,
            now(),
        )
        ran(grad_latents)
        grad_media, media_sums = norm_back_product(
            [(grad_keys, 0, key_weight), (grad_values, 0, value_weight)],
            media_feats.reshape(-1, width),
            None,
            norms,
            0,
            now(),
        )
        ran(grad_media)
        wait(both_got)
        move(both_2, plain[3])
        move(keyed, plain[1])
        sums = stacked_rows([media_sums, latent_sums, feed_sums], now())
        ran(sums)
        arrived = swap(sums)

        def move_sums(bit):
            total = added(sums, arrived, now())
            ran(total)
            return total, None if bit is None else lax.ppermute(total, "dp", [(i, i ^ (1 << bit)) for i in range(dp_size)])

        result = plain_product(hidden, 0, own, down_weight, NN, [residual, branch_got], now())
        ran(result)
        sums, arrived = move_sums(plain[0])
        move(valued, swapped[1])
        sums, arrived = move_sums(plain[1])
        move(far, last[2])
        move(keyed, plain[2])
        sums, arrived = move_sums(plain[2])
        move(valued, swapped[2])
        move(keyed, plain[3])
        sums, arrived = move_sums(plain[3])
        edge = third * tile
        along_down, across_up = end(both, first * tile, first * tile)
        along_up, across_down = end(both_2, second * tile, second * tile)
        move(far, last[3])
        move(valued, swapped[3])
        for bit in plain[4:]:
            sums, arrived = move_sums(bit)
        sums, _ = move_sums(None)
        far_down, far_up = end(far, edge, edge)
        key_sum, query_sum = end(keyed, width, width)
        value_sum, out_sum = end(valued, width, width)
        grad_down_t = jnp.concatenate([far_down, along_down, across_down], 1)
        grad_up_w = jnp.concatenate([far_up, across_up, along_up], 1)
        share = width // blocks
        sums = lax.dynamic_slice(sums, (0, flat_index * share), (sums.shape[0], share))
        return (
            result.reshape(latents.shape),
            grad_latents.reshape(latents.shape),
            grad_media.reshape(media_feats.shape),
            query_sum,
            key_sum,
            value_sum,
            out_sum.T,
            grad_up_w,
            grad_down_t.T,
            *[sums[i] for i in range(sums.shape[0])],
        )

    return local


def solution(mesh):
    rows = P(None, ("dp", "mp"), None)
    in_specs = (rows, rows, P(None, ("dp", "mp")), rows, P(), P(), P(), P(), P(None, "mp"), P("mp", None)) + (P(),) * 6
    first = P(("dp", "mp"), None)
    out_specs = (rows, rows, rows, first, first, first, P(None, ("dp", "mp")), P("dp", "mp"), P("mp", "dp")) + (
        P(("dp", "mp")),
    ) * 6
    local = build(mesh.shape["dp"], mesh.shape["mp"])
    return jax.shard_map(local, mesh=mesh, in_specs=in_specs, out_specs=out_specs, check_vma=False)
```

```python
import functools

import jax
import jax.numpy as jnp
from jax import lax
from jax.experimental import pallas as pl
from jax.experimental.pallas import tpu as pltpu
from jax.sharding import PartitionSpec as P

HEADS = 16
LAT_IMG = 64
EPSILON = 1e-05
MASKED_SCORE = -1e30
ROOT_HALF = 0.7071067811865476
DENSITY_SCALE = 0.3989422804014327
F32 = jnp.float32
BF16 = jnp.bfloat16
NN = (((1,), (0,)), ((), ()))
NT = (((1,), (1,)), ((), ()))
TN = (((0,), (0,)), ((), ()))
MIB = 1024 * 1024
ROW_TILE = 16
STEP_BYTES = 1200000
LONG = pl.CostEstimate(flops=10**12, bytes_accessed=10**10, transcendentals=0)


def mm(left, right, dims=NN):
    return lax.dot_general(left, right, dims, preferred_element_type=F32)


def low_mm(left, right):
    return mm(left, right).astype(BF16)


def normalize(values, gain_vec, shift_vec):
    row_mean = jnp.mean(values, -1, keepdims=True)
    centred = values - row_mean
    inv_scale = lax.rsqrt(jnp.mean(centred * centred, -1, keepdims=True) + EPSILON)
    scaled = centred * inv_scale
    return (scaled * gain_vec + shift_vec, scaled, inv_scale)


def mask_biases(counts, step, keys, lats, pair):
    lane = lax.broadcasted_iota(jnp.int32, (1, lats), 1) // LAT_IMG
    first = jnp.zeros((1, lats), jnp.int32)
    past = jnp.zeros((1, lats), jnp.int32)
    total = jnp.int32(0)
    for i in range(counts.shape[1]):
        after = total + counts[step, i]
        first = jnp.where(lane == i, total, first)
        past = jnp.where(lane == i, after, past)
        total = after
    place = lax.broadcasted_iota(jnp.int32, (keys, lats), 0)
    media = jnp.where((place >= first) & (place < past), 0.0, MASKED_SCORE)
    key_image = lax.broadcasted_iota(jnp.int32, (pair, pair), 0) // LAT_IMG
    latent_image = lax.broadcasted_iota(jnp.int32, (pair, pair), 1) // LAT_IMG
    return media, jnp.where(key_image == latent_image, 0.0, MASKED_SCORE)


def spans(total, size):
    return [slice(start, start + size) for start in range(0, total, size)]


def attend_kernel(
    counts, q, k, v, latents, weight, norms, mixed, norm, residual, feed, whole, *, start, heads, dim, pair
):
    scale = dim**-0.5
    lats = q.shape[0]
    bias_m, bias_l = mask_biases(counts, start + pl.program_id(0), k.shape[1], lats, pair)
    pairs = spans(lats, pair)
    columns = spans(heads * dim, dim)
    vm = v[0].T
    vl = v[1].T
    qs = [q[:, c] for c in columns]
    kl = [k[1, :, c] for c in columns]
    s_m = [mm(k[0, :, c], x, NT) * scale + bias_m for c, x in zip(columns, qs)]
    s_l = [jnp.concatenate([mm(y[p], x[p], NT) * scale + bias_l for p in pairs], 1) for y, x in zip(kl, qs)]
    top = [jnp.maximum(jnp.max(x, 0, keepdims=True), jnp.max(y, 0, keepdims=True)) for x, y in zip(s_m, s_l)]
    e_m = [jnp.exp(x - t) for x, t in zip(s_m, top)]
    e_l = [jnp.exp(x - t) for x, t in zip(s_l, top)]
    total = [jnp.sum(x, 0, keepdims=True) + jnp.sum(y, 0, keepdims=True) for x, y in zip(e_m, e_l)]
    inverse = [1.0 / t for t in total]
    p_m = [(x * i).astype(BF16) for x, i in zip(e_m, inverse)]
    p_l = [(x * i).astype(BF16) for x, i in zip(e_l, inverse)]
    outs = []
    for x, y, c in zip(p_m, p_l, columns):
        latent_part = jnp.concatenate([mm(vl[c, p], y[:, p]) for p in pairs], 1)
        outs.append((mm(vm[c, :], x) + latent_part).astype(BF16))
    norm[0, 0, :, :] = jnp.concatenate([t + jnp.log(x) for t, x in zip(top, total)], 0)
    low = jnp.concatenate(outs, 0).T
    mixed[...] = low
    group = pl.program_id(1)
    for g in range(whole.shape[0]):

        @pl.when(group == g)
        def _(g=g):
            whole[g] = low

    @pl.when(group == whole.shape[0] - 1)
    def _():
        total = latents[...].astype(F32)
        for g in range(whole.shape[0]):
            total = total + mm(whole[g], weight[g * heads * dim : (g + 1) * heads * dim, :])
        residual[...] = total
        feed[...] = normalize(total, norms[4:5, :], norms[5:6, :])[0].astype(BF16)


def attend_back_kernel(counts, q, k, v, grad_mixed, norm, *refs, start, heads, dim, pair):
    grad_q, grad_k, grad_v = refs[-3:]
    scale = dim**-0.5
    lats = q.shape[0]
    bias_m, bias_l = mask_biases(counts, start + pl.program_id(0), k.shape[1], lats, pair)
    pairs = spans(lats, pair)
    turned_m = k[0].T
    turned_l = k[1].T
    grad_qs = []
    for some in spans(heads, 4):
        columns = spans(heads * dim, dim)[some]
        group = slice(some.start * dim, some.stop * dim)
        qs = [q[:, c] for c in columns]
        gs = [grad_mixed[:, c] for c in columns]
        kl = [k[1, :, c] for c in columns]
        vl = [v[1, :, c] for c in columns]
        norms = [norm[0, 0, j : j + 1, :] for j in range(some.start, some.stop)]
        p_m = [jnp.exp(mm(k[0, :, c], y, NT) * scale + bias_m - n) for c, y, n in zip(columns, qs, norms)]
        s_l = [jnp.concatenate([mm(x[p], y[p], NT) * scale + bias_l for p in pairs], 1) for x, y in zip(kl, qs)]
        p_l = [jnp.exp(x - n) for x, n in zip(s_l, norms)]
        d_m = [mm(v[0, :, c], g, NT) for c, g in zip(columns, gs)]
        d_l = [jnp.concatenate([mm(x[p], g[p], NT) for p in pairs], 1) for x, g in zip(vl, gs)]
        means = [
            jnp.sum(x * y, 0, keepdims=True) + jnp.sum(z * w, 0, keepdims=True)
            for x, y, z, w in zip(d_m, p_m, d_l, p_l)
        ]
        g_m = [(x * (y - n)).astype(BF16) for x, y, n in zip(p_m, d_m, means)]
        g_l = [(x * (y - n)).astype(BF16) for x, y, n in zip(p_l, d_l, means)]
        p_m = [x.astype(BF16) for x in p_m]
        p_l = [x.astype(BF16) for x in p_l]
        grad_v[0, :, group] = jnp.concatenate([mm(x, g).astype(BF16) for x, g in zip(p_m, gs)], 1)
        grad_k[0, :, group] = jnp.concatenate([(mm(x, y) * scale).astype(BF16) for x, y in zip(g_m, qs)], 1)
        for p in pairs:
            grad_v[1, p, group] = jnp.concatenate([mm(x[:, p], g[p]).astype(BF16) for x, g in zip(p_l, gs)], 1)
            grad_k[1, p, group] = jnp.concatenate([(mm(x[:, p], y[p]) * scale).astype(BF16) for x, y in zip(g_l, qs)], 1)
        for c, x, z in zip(columns, g_m, g_l):
            latent_part = jnp.concatenate([mm(turned_l[c, p], z[:, p]) for p in pairs], 1)
            grad_qs.append(((mm(turned_m[c, :], x) + latent_part) * scale).astype(BF16))
    grad_q[...] = jnp.concatenate(grad_qs, 0).T


def call(kernel, operands, in_specs, out_specs, out_shape, grid, after=(), scalars=0, scratch=(), aliases=None):
    given = len(operands)

    def body(*refs):
        kernel(*refs[:given], *refs[given + len(after) :])

    return pl.pallas_call(
        body,
        grid_spec=pltpu.PrefetchScalarGridSpec(
            num_scalar_prefetch=scalars,
            grid=grid,
            in_specs=list(in_specs) + [pl.BlockSpec(memory_space=pl.ANY)] * len(after),
            out_specs=out_specs,
            scratch_shapes=list(scratch),
        ),
        out_shape=out_shape,
        input_output_aliases=aliases or {},
        compiler_params=pltpu.CompilerParams(vmem_limit_bytes=60 * MIB),
        cost_estimate=LONG,
    )(*operands, *after)


def marker(number, source):
    def kernel(target):
        pass

    anywhere = pl.BlockSpec(memory_space=pl.ANY)
    return call(kernel, [], [], anywhere, jax.ShapeDtypeStruct((8, 128 * number), F32), (1,), (source,))


def project_kernel(media, latents, norms, query, key, value, both, queries, keys, values):
    rows = media.shape[0]

    def products(side, r, low):
        keys[side, r, :] = mm(low, key[...]).astype(BF16)
        values[side, r, :] = mm(low, value[...]).astype(BF16)
        if side:
            queries[r, :] = mm(low, query[...]).astype(BF16)

    @pl.when(pl.program_id(0) == 0)
    def _():
        for side, source in enumerate((media, latents)):
            gain, shift = norms[2 * side : 2 * side + 1, :], norms[2 * side + 1 : 2 * side + 2, :]
            for r in spans(rows, rows // 2):
                low = normalize(source[r, :].astype(F32), gain, shift)[0].astype(BF16)
                both[side * rows + r.start : side * rows + r.stop, :] = low
                products(side, r, low)

    @pl.when(pl.program_id(0) > 0)
    def _():
        for side in range(2):
            products(side, slice(0, rows), both[side * rows : (side + 1) * rows, :])


def project(media, latents, norms, query, key, value):
    rows, width = latents.shape
    tile = 512
    whole = pl.BlockSpec((rows, width), lambda t: (0, 0), pipeline_mode=pl.Buffered(1))
    weight = pl.BlockSpec((width, tile), lambda t: (0, t))
    two = jax.ShapeDtypeStruct((2, rows, width), BF16)
    return call(
        project_kernel,
        [media, latents, norms, query, key, value],
        [whole, whole, pl.BlockSpec(norms.shape, lambda t: (0, 0)), weight, weight, weight],
        [
            pl.BlockSpec((2 * rows, width), lambda t: (0, 0), pipeline_mode=pl.Buffered(1)),
            pl.BlockSpec((rows, tile), lambda t: (0, t)),
            pl.BlockSpec((2, rows, tile), lambda t: (0, 0, t)),
            pl.BlockSpec((2, rows, tile), lambda t: (0, 0, t)),
        ],
        [jax.ShapeDtypeStruct((2 * rows, width), BF16), jax.ShapeDtypeStruct((rows, width), BF16), two, two],
        (width // tile,),
    )


def attention_call(kernel, counts, queries, keys, values, more, outs, after=(), start=0, count=None, before=(), fixed=(), scratch=0):
    micro = counts.shape[0]
    rows = queries.shape[0] // micro
    width = queries.shape[1]
    groups = 2
    heads = HEADS // groups
    group = width // groups
    one = pl.BlockSpec((rows, group), lambda m, g: (start + m, g))
    two = pl.BlockSpec((2, rows, group), lambda m, g: (0, start + m, g))
    norm = pl.BlockSpec((1, 1, heads, rows), lambda m, g: (start + m, g, 0, 0))
    kinds = {
        "one": (one, jax.ShapeDtypeStruct(queries.shape, BF16)),
        "two": (two, jax.ShapeDtypeStruct(keys.shape, BF16)),
        "norm": (norm, jax.ShapeDtypeStruct((micro, groups, heads, rows), F32)),
        "row": (pl.BlockSpec((rows, width), lambda m, g: (start + m, 0)), jax.ShapeDtypeStruct(queries.shape, BF16)),
        "long": (pl.BlockSpec((rows, width), lambda m, g: (start + m, 0)), jax.ShapeDtypeStruct(queries.shape, F32)),
    }
    operands = [counts, queries, keys, values] + [value for _, value in more]
    in_specs = [pl.BlockSpec(memory_space=pltpu.SMEM), one, two, two] + [kinds[kind][0] for kind, _ in more]
    operands += fixed
    in_specs += [pl.BlockSpec(f.shape, lambda m, g: (0, 0), pipeline_mode=pl.Buffered(1)) for f in fixed]
    return call(
        functools.partial(kernel, start=start, heads=heads, dim=width // HEADS, pair=2 * LAT_IMG),
        operands + list(before),
        in_specs + [pl.BlockSpec(memory_space=pl.ANY)] * len(before),
        [kinds[kind][0] for kind in outs],
        [kinds[kind][1] for kind in outs],
        (micro if count is None else count, groups),
        after,
        scratch=[pltpu.VMEM((groups, rows, group), BF16)] * scratch,
        aliases={len(operands) + n: n for n in range(len(before))},
    )


def split_rows(whole, rear_ref, front_ref, block_rows, first_bit, mine):
    for i in range(rear_ref.shape[0]):
        low = i & ((1 << first_bit) - 1)
        base = ((i >> first_bit) << (first_bit + 1)) | low
        for ref, side in ((rear_ref, 1 - mine), (front_ref, mine)):
            block = base + side * (1 << first_bit)
            rows = pl.ds(pl.multiple_of(block * block_rows, block_rows), block_rows)
            ref[i, :, :] = whole[rows, :]


def feed_kernel(index, feed_own, feed_other, cot_own, cot_other, up, down, *refs, kept, bits, far, block_rows):
    refs = refs[kept:]
    half, width = feed_own.shape
    tile = up.shape[1]
    if bits is None:
        grad_down, grad_up_w, hidden, grad_up, feed, cot = refs
    else:
        *sides, hidden, grad_up, feed, cot, grad_down, grad_up_w = refs

    @pl.when(pl.program_id(0) == 0)
    def _():
        for whole, parts in ((feed, (feed_own, feed_other)), (cot, (cot_own, cot_other))):
            for n, part in enumerate(parts):
                whole[n * half : (n + 1) * half, :] = part[...]

    for r in spans(2 * half, half):
        u = mm(feed[r, :], up[...])
        grad_hidden = mm(cot[r, :], down[...], NT)
        cdf = 0.5 * (1.0 + lax.erf(u * ROOT_HALF))
        pdf = jnp.exp(-0.5 * u * u) * DENSITY_SCALE
        hidden[r, :] = (u * cdf).astype(BF16)
        grad_up[r, :] = (grad_hidden * (cdf + u * pdf)).astype(BF16)
    for r in spans(width, width // 2):
        grad_down[r, :] = mm(cot[:, r], hidden[...], TN).astype(BF16)
        grad_up_w[r, :] = mm(feed[:, r], grad_up[...], TN).astype(BF16)
    if bits is None:
        return

    def split(whole, rear, front, bit):
        split_rows(whole, rear, front, block_rows, bit, (index[0] >> bit) & 1)

    def near():
        split(grad_down, *sides[-4:-2], bits[0])
        split(grad_up_w, *sides[-2:], bits[1])

    if far is None:
        near()
    else:
        step = pl.program_id(0)
        pl.when(step > 0)(near)

        @pl.when(step == 0)
        def _():
            rear, front = sides[:2]
            split(grad_down, rear.at[:, :, :tile], front.at[:, :, :tile], far)
            split(grad_up_w, rear.at[:, :, tile:], front.at[:, :, tile:], far)


def feed_part(index, rows_in, up, down, start, tiles, tile, before, bits, far, blocks):
    half, width = rows_in[0].shape
    block_rows = width // blocks
    whole = pl.BlockSpec((half, width), lambda t, i: (0, 0), pipeline_mode=pl.Buffered(1))
    units = pl.BlockSpec((2 * half, tile), lambda t, i: (0, start + t))
    unit_shape = jax.ShapeDtypeStruct((2 * half, up.shape[1]), BF16)
    kept = [] if before is None else list(before)
    split = block_rows % ROW_TILE == 0
    if split:
        apart = 0 if far is None else 1
        shape = (blocks // 2, block_rows)
        grads = [pl.BlockSpec((*shape, 2 * tile), lambda t, i: (0, 0, 0), pipeline_mode=pl.Buffered(1))] * (2 * apart)
        shapes = [jax.ShapeDtypeStruct((*shape, 2 * tile), BF16)] * (2 * apart)
        grads += [pl.BlockSpec((*shape, tile), lambda t, i: (0, 0, jnp.maximum(t - apart, 0)))] * 4
        shapes += [jax.ShapeDtypeStruct((*shape, (tiles - apart) * tile), BF16)] * 4
        scratch = [pltpu.VMEM((2 * half, width), BF16)] * 2 + [pltpu.VMEM((width, tile), BF16)] * 2
    else:
        grads = [pl.BlockSpec((width, tile), lambda t, i: (0, t))] * 2
        shapes = [jax.ShapeDtypeStruct((width, tiles * tile), BF16)] * 2
        scratch = [pltpu.VMEM((2 * half, width), BF16)] * 2
    first = len(shapes)
    anywhere = pl.BlockSpec(memory_space=pl.ANY)
    results = call(
        functools.partial(
            feed_kernel, kept=len(kept), bits=bits if split else None, far=far if split else None, block_rows=block_rows
        ),
        [index, *rows_in, up, down, *kept],
        [
            whole,
            whole,
            whole,
            whole,
            pl.BlockSpec((width, tile), lambda t, i: (0, start + t)),
            pl.BlockSpec((tile, width), lambda t, i: (start + t, 0)),
        ]
        + [anywhere] * len(kept),
        grads + [units, units],
        shapes + [unit_shape, unit_shape],
        (tiles,),
        (),
        1,
        scratch,
        {7: first, 8: first + 1} if kept else {},
    )
    return results[:-2], results[-2:]


def product_kernel(index, *refs, lefts, parts, block_rows, split):
    step = pl.program_id(0)
    target = refs[-1]
    rights = refs[lefts : lefts + len(parts)]
    for (place, first, past), right in zip(parts, rights):

        @pl.when((step >= first) & (step < past))
        def _(left=refs[place], right=right):
            skipped = left.shape[0] - right.shape[0]
            target[...] = mm(left[skipped:, :], right[...], TN).astype(BF16)

    if split:
        split_rows(target, refs[-3], refs[-2], block_rows, 0, index[0] & 1)


def product(index, lefts, parts, blocks, after, stacked=False):
    width = lefts[0].shape[1]
    block_rows = width // blocks
    tile = width // 2
    split = block_rows % ROW_TILE == 0
    in_specs = [pl.BlockSpec(left.shape, lambda t, i: (0, 0), pipeline_mode=pl.Buffered(1)) for left in lefts]
    steps = []
    start = 0
    for place, right, first, count in parts:

        def at(t, i, first=first, start=start, count=count):
            return (0, first + jnp.clip(t - start, 0, count - 1))

        in_specs.append(pl.BlockSpec((right.shape[0], tile), at))
        steps.append((place, start, start + count))
        start += count
    if split:
        place = (lambda t, i: (0, t, 0)) if stacked else (lambda t, i: (0, 0, t))
        shape = (block_rows * start, tile) if stacked else (block_rows, tile * start)
        out_specs = [pl.BlockSpec((blocks // 2, block_rows, tile), place)] * 2
        out_shape = [jax.ShapeDtypeStruct((blocks // 2, *shape), BF16)] * 2
        scratch = [pltpu.VMEM((width, tile), BF16)]
    else:
        out_specs = [pl.BlockSpec((width, tile), lambda t, i: (0, t))]
        out_shape = [jax.ShapeDtypeStruct((width, tile * start), BF16)]
        scratch = []
    kernel = functools.partial(product_kernel, lefts=len(lefts), parts=steps, block_rows=block_rows, split=split)
    operands = [index, *lefts] + [right for _, right, _, _ in parts]
    return call(kernel, operands, in_specs, out_specs, out_shape, (start,), after, 1, scratch)


def feed_norm_back_kernel(own, other, source, base, norms, weight, out, out_low, mixed_low, sums):
    gain = norms[4:5, :]
    e = own[...] + other[...].astype(F32)
    _, hat, inverse = normalize(source[...], gain, 0.0)
    weighted = e * gain
    first_mean = jnp.mean(weighted, -1, keepdims=True)
    second_mean = jnp.mean(weighted * hat, -1, keepdims=True)
    grad = base[...].astype(F32) + inverse * (weighted - first_mean - hat * second_mean)
    out[...] = grad
    low = grad.astype(BF16)
    out_low[...] = low
    mixed_low[...] = mm(low, weight[...], NT).astype(BF16)
    fresh = [jnp.sum(e * hat, 0, keepdims=True), jnp.sum(e, 0, keepdims=True)]

    @pl.when(pl.program_id(0) == 0)
    def _():
        sums[0:1, :], sums[1:2, :] = fresh

    @pl.when(pl.program_id(0) > 0)
    def _():
        sums[0:1, :] += fresh[0]
        sums[1:2, :] += fresh[1]


def feed_norm_back(own, other, source, base, norms, weight, after):
    rows, width = source.shape
    size = 256
    part = pl.BlockSpec((size, width), lambda t: (t, 0))
    line = pl.BlockSpec(norms.shape, lambda t: (0, 0))
    whole = pl.BlockSpec(weight.shape, lambda t: (0, 0), pipeline_mode=pl.Buffered(1))
    low = jax.ShapeDtypeStruct((rows, width), BF16)
    return call(
        feed_norm_back_kernel,
        [own, other, source, base, norms, weight],
        [part] * 4 + [line, whole],
        [part] * 3 + [pl.BlockSpec((2, width), lambda t: (0, 0))],
        [jax.ShapeDtypeStruct((rows, width), F32), low, low, jax.ShapeDtypeStruct((2, width), F32)],
        (rows // size,),
        after,
    )


def norm_back_kernel(*refs, pairs, place):
    lefts, weights, refs = refs[:pairs], refs[pairs : 2 * pairs], refs[2 * pairs :]
    source, norms, *base, out, sums, upstream = refs
    gain = norms[place : place + 1, :]
    step = pl.program_id(0)
    tile = weights[0].shape[0]
    columns = pl.ds(pl.multiple_of(step * tile, tile), tile)
    total = mm(lefts[0][...], weights[0][...], NT)
    for left, weight in zip(lefts[1:], weights[1:]):
        total = total + mm(left[...], weight[...], NT)
    upstream[:, columns] = total

    @pl.when(step == pl.num_programs(0) - 1)
    def _():
        rows, width = upstream.shape
        size = 64

        def chunk(i, carry):
            gain_sum, shift_sum = carry
            r = pl.ds(pl.multiple_of(i * size, size), size)
            e = upstream[r, :]
            _, hat, inverse = normalize(source[r, :].astype(F32), gain, 0.0)
            weighted = e * gain
            first_mean = jnp.mean(weighted, -1, keepdims=True)
            second_mean = jnp.mean(weighted * hat, -1, keepdims=True)
            grad = inverse * (weighted - first_mean - hat * second_mean)
            if base:
                grad = grad + base[0][r, :]
            out[r, :] = grad
            return gain_sum + jnp.sum(e * hat, 0, keepdims=True), shift_sum + jnp.sum(e, 0, keepdims=True)

        zero = jnp.zeros((1, width), F32)
        sums[0:1, :], sums[1:2, :] = lax.fori_loop(0, rows // size, chunk, (zero, zero))


def norm_back_product(pairs, source, base, norms, place, after):
    rows, width = source.shape
    tile = 512
    whole = pl.BlockSpec((rows, width), lambda t: (0, 0), pipeline_mode=pl.Buffered(1))

    def rows_of(left, place):
        return pl.BlockSpec((rows, left.shape[1]), lambda t: (place, 0), pipeline_mode=pl.Buffered(1))

    operands = [left for left, _, _ in pairs] + [weight for _, _, weight in pairs] + [source, norms]
    in_specs = [rows_of(left, place) for left, place, _ in pairs]
    in_specs += [pl.BlockSpec((tile, weight.shape[1]), lambda t: (t, 0)) for _, _, weight in pairs]
    in_specs += [whole, pl.BlockSpec(norms.shape, lambda t: (0, 0))]
    if base is not None:
        operands.append(base)
        in_specs.append(whole)
    return call(
        functools.partial(norm_back_kernel, pairs=len(pairs), place=place),
        operands,
        in_specs,
        [whole, pl.BlockSpec((2, width), lambda t: (0, 0))],
        [jax.ShapeDtypeStruct((rows, width), F32), jax.ShapeDtypeStruct((2, width), F32)],
        (width // tile,),
        after,
        scratch=[pltpu.VMEM((rows, width), F32)],
    )


def plain_kernel(left, weight, *refs, dims):
    total = mm(left[...], weight[...], dims)
    for term in refs[:-1]:
        total = total + term[...].astype(F32)
    refs[-1][...] = total.astype(refs[-1].dtype)


def plain_product(left, place, rows, weight, dims, terms, after=(), kind=BF16):
    tile = 512
    if dims is NT:
        width = weight.shape[0]
        weights = pl.BlockSpec((tile, weight.shape[1]), lambda t: (t, 0))
    else:
        width = weight.shape[1]
        weights = pl.BlockSpec((weight.shape[0], tile), lambda t: (0, t))
    columns = pl.BlockSpec((rows, tile), lambda t: (0, t))
    return call(
        functools.partial(plain_kernel, dims=dims),
        [left, weight, *terms],
        [pl.BlockSpec((rows, left.shape[1]), lambda t: (place, 0), pipeline_mode=pl.Buffered(1)), weights]
        + [columns] * len(terms),
        columns,
        jax.ShapeDtypeStruct((rows, width), kind),
        (width // tile,),
        after,
    )


def added(left, right, after):
    def kernel(a, b, out):
        out[...] = a[...] + b[...]

    whole = pl.BlockSpec(left.shape, lambda t: (0, 0))
    return call(kernel, [left, right], [whole] * 2, whole, jax.ShapeDtypeStruct(left.shape, left.dtype), (1,), after)


def stacked_rows(parts, after):
    def kernel(*refs):
        start = 0
        for ref in refs[:-1]:
            refs[-1][start : start + ref.shape[0], :] = ref[...]
            start += ref.shape[0]

    rows, width = sum(part.shape[0] for part in parts), parts[0].shape[1]
    specs = [pl.BlockSpec(part.shape, lambda t: (0, 0)) for part in parts]
    out = pl.BlockSpec((rows, width), lambda t: (0, 0))
    return call(kernel, parts, specs, out, jax.ShapeDtypeStruct((rows, width), F32), (1,), after)


def last_sum_kernel(index, *refs, segments, cuts):
    outs = refs[-len(cuts) :]
    column = 0
    for width, terms in segments:
        total = None
        for ref, start in terms:
            value = refs[ref][..., start : start + width]
            value = value.reshape(value.shape[-2:]).astype(F32)
            total = value if total is None else total + value
        past = 0
        for out, cut in zip(outs, cuts):
            low, high = max(past, column), min(past + cut, column + width)
            if low < high:
                out[:, low - past : high - past] = total[:, low - column : high - column]
            past += cut
        column += width


def sum_kernel(index, *refs, segments):
    out = refs[-1]
    column = 0
    for width, terms in segments:
        values = [refs[ref][..., start : start + width] for ref, start in terms]
        values = [value.reshape(-1, *value.shape[-2:]) for value in values]
        if len(values) > 2:
            values = [value.astype(F32) for value in values]
        total = functools.reduce(jnp.add, values).astype(out.dtype)
        out[..., column : column + width] = total.reshape(*out.shape[:-1], width)
        column += width


class Segment:
    def __init__(self, width, arrays, taken):
        self.width = width
        self.taken = list(taken)
        self.terms = [(a, len(taken), 0) for a in arrays]


class Chain:
    def __init__(self, index, bits, sizes, first=None):
        self.index = index
        self.sizes = sizes
        self.left = sorted(bits)
        self.taken = [] if first is None else [(self.left.index(first), first)]
        if first is not None:
            self.left.remove(first)
        self.segments = []

    def add(self, width, arrays):
        self.segments.append(Segment(width, arrays, self.taken))

    def join(self, other):
        self.segments += other.segments

    def _sum(self, bit, after, cuts=None):
        free = [b for b in sorted(self.left)[::-1] if b != bit]
        arrays, homes, segments = [], [], []
        for segment in self.segments:
            listed = []
            for array, level, start in segment.terms:
                home = sorted(self.left + [b for _, b in segment.taken[level:]])[::-1]
                known = [n for n, a in enumerate(arrays) if a is array and homes[n] == home]
                if not known:
                    arrays.append(array)
                    homes.append(home)
                    known = [len(arrays) - 1]
                listed.append((known[0], start))
            segments.append((segment.width, listed))
        rows = arrays[0].shape[1]
        total = sum(segment.width for segment in self.segments)
        steps = 0
        while steps < len(free) and (rows * total * 2 << (len(free) - steps)) > STEP_BYTES:
            steps += 1
        grid = (2,) * steps if steps else (1,)

        def spec(home, width):
            shape = tuple(2 if b in free[steps:] else 1 for b in home)

            def at(*step_and_index):
                index = step_and_index[-1]
                place = []
                for b in home:
                    if b == bit:
                        place.append(1 - ((index[0] >> b) & 1))
                    elif b in free:
                        place.append(step_and_index[free.index(b)] if b in free[:steps] else 0)
                    else:
                        place.append((index[0] >> b) & 1)
                return (*place, 0, 0)

            return pl.BlockSpec((*shape, rows, width), at)

        operands = [self.index] + [a.reshape((2,) * len(home) + a.shape[1:]) for a, home in zip(arrays, homes)]
        in_specs = [spec(home, a.shape[2]) for a, home in zip(arrays, homes)]
        if cuts is not None:
            return call(
                functools.partial(last_sum_kernel, segments=segments, cuts=cuts),
                operands,
                in_specs,
                [pl.BlockSpec((rows, cut), lambda t, i: (0, 0)) for cut in cuts],
                [jax.ShapeDtypeStruct((rows, cut), F32) for cut in cuts],
                grid,
                after,
                1,
            )
        result = call(
            functools.partial(sum_kernel, segments=segments),
            operands,
            in_specs,
            spec(free, total),
            jax.ShapeDtypeStruct((2,) * len(free) + (rows, total), BF16),
            grid,
            after,
            1,
        )
        return result.reshape(-1, rows, total)

    def pack(self, bit, after=()):
        return self._sum(bit, after)

    def travel(self, packed, bit):
        got = lax.ppermute(packed, "dp", [(i, i ^ (1 << bit)) for i in range(self.sizes["dp"])])
        step = (self.left.index(bit), bit)
        self.left.remove(bit)
        start = 0
        for segment in self.segments:
            segment.taken.append(step)
            segment.terms.append((got, len(segment.taken), start))
            start += segment.width
        return got

    def finish(self, cuts, after=()):
        for bit in list(self.left):
            self.travel(self.pack(bit), bit)
        return self._sum(None, after, cuts)


def bit_orders(count):
    bits = count.bit_length() - 1
    if bits == 4:
        return [(0, 1, 2, 3), (1, 0, 2, 3), (2, 3, 0, 1)]
    plain = tuple(range(bits))
    third = bits // 3
    return [plain, (1, 0) + plain[2:], plain[2 * third :] + plain[: 2 * third]]


def sided(value, bit, bits, side):
    place = bits.index(bit)
    shape = value.shape
    outer = 1 << place
    parts = value.reshape((outer, 2, shape[0] // (2 * outer)) + shape[1:])
    return lax.dynamic_index_in_dim(parts, side, 1, keepdims=False).reshape((shape[0] // 2,) + shape[1:])


def build(dp_size, mp_size):
    plain, swapped, last = bit_orders(dp_size)
    sizes = {"dp": dp_size, "mp": mp_size}
    all_bits = sorted(plain)

    def swap(value):
        return lax.ppermute(value, "mp", [(i, i ^ 1) for i in range(mp_size)])

    def local(
        media_feats,
        latents,
        patch_counts,
        cotangent,
        query_weight,
        key_weight,
        value_weight,
        out_weight,
        up_weight,
        down_weight,
        media_gain,
        media_shift,
        latent_gain,
        latent_shift,
        feed_gain,
        feed_shift,
    ):
        micro, patches, width = media_feats.shape
        dp_index = lax.axis_index("dp").astype(jnp.int32)
        mp_index = lax.axis_index("mp").astype(jnp.int32)
        flat_index = dp_index * mp_size + mp_index
        dp_list = dp_index.reshape(1)
        mp_list = mp_index.reshape(1)

        def first_step(grads, bit):
            if len(grads) == 2:
                return grads
            parted = grads[0].reshape(dp_size, width // dp_size, -1)
            mine = (dp_index >> bit) & 1
            return sided(parted, bit, all_bits[::-1], 1 - mine), sided(parted, bit, all_bits[::-1], mine)

        def sent_first(grads, bit):
            rear, front = first_step(grads, bit)
            return front, lax.ppermute(rear, "dp", [(i, i ^ (1 << bit)) for i in range(dp_size)])

        def paired(grads):
            if len(grads) == 1:
                parted = grads[0].reshape(dp_size, mp_size, -1, grads[0].shape[1])
                grads = [lax.dynamic_index_in_dim(parted, side, 1, keepdims=False) for side in (1 - mp_index, mp_index)]
            rear, front = grads
            return front, swap(rear)

        grad_own = cotangent.reshape(-1, width)
        grad_other = swap(grad_own)
        norms = jnp.stack([media_gain, media_shift, latent_gain, latent_shift, feed_gain, feed_shift])
        both_low, queries, keys, values = project(
            media_feats.reshape(-1, width), latents.reshape(-1, width), norms, query_weight, key_weight, value_weight
        )
        own = queries.shape[0]
        mixed_low, log_norm, residual, feed_own = attention_call(
            attend_kernel,
            patch_counts,
            queries,
            keys,
            values,
            [("row", latents.reshape(-1, width))],
            ["one", "norm", "long", "row"],
            (grad_other,),
            fixed=[out_weight, norms],
            scratch=1,
        )
        feed_other = swap(feed_own)

        tile = 512
        tiles = up_weight.shape[1] // tile
        third = tiles // 6
        first = tiles // 2 - third
        second = tiles - first - third
        rows_in = [feed_own, feed_other, grad_own, grad_other]
        splittable = width // dp_size % ROW_TILE == 0

        along, along_2 = (Chain(dp_list, all_bits, sizes, plain[0]) for _ in range(2))
        across, across_2 = (Chain(dp_list, all_bits, sizes, swapped[0]) for _ in range(2))
        far = Chain(dp_list, all_bits, sizes, last[0])
        grads, units = feed_part(
            dp_list, rows_in, up_weight, down_weight, 0, third + first, tile, None, (plain[0], swapped[0]), last[0], dp_size
        )
        if splittable:
            far_1, down_1, up_1 = grads[:2], grads[2:4], grads[4:]
        else:
            far_1 = [jnp.concatenate([g[:, : third * tile] for g in grads], 1)]
            down_1, up_1 = ([g[:, third * tile :]] for g in grads)
        along.add(first * tile, sent_first(down_1, plain[0]))
        across.add(first * tile, sent_first(up_1, swapped[0]))
        far.add(2 * third * tile, sent_first(far_1, last[0]))
        part_got = [chain.segments[0].terms[1][0] for chain in (along, across, far)]
        grads, units = feed_part(
            dp_list,
            rows_in,
            up_weight,
            down_weight,
            third + first,
            second,
            tile,
            units,
            (swapped[0], plain[0]),
            None,
            dp_size,
        )
        down_2, up_2 = (grads[:2], grads[2:]) if splittable else (grads[:1], grads[1:])
        across_2.add(second * tile, sent_first(down_2, swapped[0]))
        along_2.add(second * tile, sent_first(up_2, plain[0]))
        hidden, grad_up = units
        markers = []

        def fresh():
            markers.append(marker(len(markers) + 1, patch_counts))
            return markers[-1]

        feed_back = plain_product(grad_up, 0, own, up_weight, NT, [], (fresh(),), F32)
        feed_back_other = plain_product(grad_up, 1, own, up_weight, NT, [], (feed_back, *part_got, fresh()))
        feed_back_got = swap(feed_back_other)
        far_packed = far.pack(last[1], (feed_back_other,))
        far_got = far.travel(far_packed, last[1])
        grad_residual, grad_residual_low, grad_mixed, feed_sums = feed_norm_back(
            feed_back, feed_back_got, residual, grad_own, norms, out_weight, (far_packed,)
        )
        blocks = dp_size * mp_size
        token = [grad_residual]

        def now():
            return (*token, fresh())

        def ran(value):
            token[:] = [value]

        def wait(*values):
            token.extend(values)

        def move(chain, bit):
            packed = chain.pack(bit, now())
            ran(packed)
            return chain.travel(packed, bit)

        def end(chain, *cuts):
            totals = chain.finish(cuts, now())
            ran(totals[0])
            return totals

        def join(*chains):
            joined = Chain(dp_list, chains[0].left, sizes)
            for chain in chains:
                joined.join(chain)
            return joined

        def attend_back(start, count, before):
            made = attention_call(
                attend_back_kernel,
                patch_counts,
                queries,
                keys,
                values,
                [("one", grad_mixed), ("norm", log_norm)],
                ["one", "two", "two"],
                now(),
                start,
                count,
                before,
            )
            ran(made[0])
            return made

        grad_queries, grad_keys, grad_values = attend_back(0, micro, ())
        move(along, plain[1])
        move(across, swapped[1])
        move(along_2, plain[1])
        move(across_2, swapped[1])
        wait(far_got)
        grad_keys = grad_keys.reshape(-1, width)
        grad_values = grad_values.reshape(-1, width)
        key_grads = product(
            mp_list, [both_low], [(0, grad_keys, 0, 2), (0, grad_queries, 0, 2)], blocks, now()
        )
        keyed = Chain(dp_list, all_bits, sizes)
        keyed.add(2 * width, paired(key_grads))
        ran(key_grads[0])
        both = join(along, across)
        move(both, plain[2])
        branch_other = plain_product(hidden, 1, own, down_weight, NN, [], now())
        ran(branch_other)
        branch_got = swap(branch_other)
        move(keyed, plain[0])
        wait(branch_got)
        value_grads = product(
            mp_list, [both_low, grad_residual_low], [(0, grad_values, 0, 2), (1, mixed_low, 0, 2)], blocks, now()
        )
        valued = Chain(dp_list, all_bits, sizes)
        valued.add(2 * width, paired(value_grads))
        ran(value_grads[0])
        both_got = move(both, plain[3])
        both_2 = join(along_2, across_2)
        move(both_2, plain[2])
        move(valued, swapped[0])
        grad_latents, latent_sums = norm_back_product(
            [(grad_queries, 0, query_weight), (grad_keys, 1, key_weight), (grad_values, 1, value_weight)],
            latents.reshape(-1, width),
            grad_residual,
            norms,
            2,
            now(),
        )
        ran(grad_latents)
        grad_media, media_sums = norm_back_product(
            [(grad_keys, 0, key_weight), (grad_values, 0, value_weight)],
            media_feats.reshape(-1, width),
            None,
            norms,
            0,
            now(),
        )
        ran(grad_media)
        wait(both_got)
        move(both_2, plain[3])
        move(keyed, plain[1])
        sums = stacked_rows([media_sums, latent_sums, feed_sums], now())
        ran(sums)
        arrived = swap(sums)

        def move_sums(bit):
            total = added(sums, arrived, now())
            ran(total)
            return total, None if bit is None else lax.ppermute(total, "dp", [(i, i ^ (1 << bit)) for i in range(dp_size)])

        result = plain_product(hidden, 0, own, down_weight, NN, [residual, branch_got], now())
        ran(result)
        sums, arrived = move_sums(plain[0])
        move(valued, swapped[1])
        sums, arrived = move_sums(plain[1])
        move(far, last[2])
        move(keyed, plain[2])
        sums, arrived = move_sums(plain[2])
        move(valued, swapped[2])
        move(keyed, plain[3])
        sums, arrived = move_sums(plain[3])
        edge = third * tile
        along_down, across_up = end(both, first * tile, first * tile)
        along_up, across_down = end(both_2, second * tile, second * tile)
        move(far, last[3])
        move(valued, swapped[3])
        for bit in plain[4:]:
            sums, arrived = move_sums(bit)
        sums, _ = move_sums(None)
        far_down, far_up = end(far, edge, edge)
        key_sum, query_sum = end(keyed, width, width)
        value_sum, out_sum = end(valued, width, width)
        grad_down_t = jnp.concatenate([far_down, along_down, across_down], 1)
        grad_up_w = jnp.concatenate([far_up, across_up, along_up], 1)
        share = width // blocks
        sums = lax.dynamic_slice(sums, (0, flat_index * share), (sums.shape[0], share))
        return (
            result.reshape(latents.shape),
            grad_latents.reshape(latents.shape),
            grad_media.reshape(media_feats.shape),
            query_sum,
            key_sum,
            value_sum,
            out_sum.T,
            grad_up_w,
            grad_down_t.T,
            *[sums[i] for i in range(sums.shape[0])],
        )

    return local


def solution(mesh):
    rows = P(None, ("dp", "mp"), None)
    in_specs = (rows, rows, P(None, ("dp", "mp")), rows, P(), P(), P(), P(), P(None, "mp"), P("mp", None)) + (P(),) * 6
    first = P(("dp", "mp"), None)
    out_specs = (rows, rows, rows, first, first, first, P(None, ("dp", "mp")), P("dp", "mp"), P("mp", "dp")) + (
        P(("dp", "mp")),
    ) * 6
    local = build(mesh.shape["dp"], mesh.shape["mp"])
    return jax.shard_map(local, mesh=mesh, in_specs=in_specs, out_specs=out_specs, check_vma=False)
```
